128 devices in a mesh: req: 16 (over y, x), mlp: 8 (over z, core).
Axes of the slice: x: 4, y: 4, z: 4, core: 2. Of those that a mesh axis runs over, the one named last changes fastest.
Arguments:
- decode_query: bfloat16 [768, 1600], P(('req', 'mlp')), may hold values from -12 to 12
- decode_key_value: bfloat16 [768, 640], P(('req', 'mlp')), may hold values from -4 to 4
- dec_xz: bfloat16 [768, 6400], P(('req', 'mlp')), may hold values from -6 to 6
- dec_resid: bfloat16 [768, 1600], P(('req', 'mlp')), may hold values from -6 to 6
- dec_conv: bfloat16 [768, 3, 3200], P(('req', 'mlp')), may hold values from -6 to 6
- dec_state: float32 [768, 3200, 16], P(('req', 'mlp')), may hold values from -4 to 4
- dec_len: int32 [16, 8, 6], P(None, 'mlp'), may hold values from 1 to 4096, as said below
- page_owner: int32 [16, 8, 6, 9], P(None, 'mlp'), may hold values from 0 to 15, as said below
- page_slot: int32 [16, 8, 6, 9], P(None, 'mlp'), may hold values from 0 to 63, as said below
- kv_pool: bfloat16 [8192, 128, 640], P(('req', 'mlp')), may hold values from -12 to 12
- pre_q: bfloat16 [8, 2048, 1600], P('mlp', 'req'), may hold values from -12 to 12
- pre_kv: bfloat16 [8, 2048, 640], P('mlp', 'req'), may hold values from -12 to 12
- pre_xz: bfloat16 [8, 2048, 6400], P('mlp', 'req'), may hold values from -6 to 6
- pre_resid: bfloat16 [8, 2048, 1600], P('mlp', 'req'), may hold values from -6 to 6
- w_xproj: bfloat16 [3200, 132], replicated, may hold values from -0.109375 to 0.109375
- w_dt: bfloat16 [100, 3200], replicated, may hold values from -0.625 to 0.625
- dt_bias: float32 [3200], replicated, may hold values from -8 to -3
- a_rate: float32 [3200, 16], replicated, may hold values from 0.01 to 4
- conv_w: float32 [4, 3200], replicated, may hold values from -3 to 3
- conv_b: float32 [3200], replicated, may hold values from -3 to 3
- d_skip: float32 [3200], replicated, may hold values from 0.5 to 1.5
- g_attn: float32 [1600], replicated, may hold values from 0.1 to 1.9
- g_ssm: float32 [3200], replicated, may hold values from 0.1 to 1.9
- w_out: bfloat16 [4800, 1600], P('mlp'), may hold values from -0.09375 to 0.09375
- g_mlp: float32 [1600], replicated, may hold values from 0.1 to 1.9
- w_gate: bfloat16 [1600, 5504], P(None, 'mlp'), may hold values from -0.15625 to 0.15625
- w_up: bfloat16 [1600, 5504], P(None, 'mlp'), may hold values from -0.15625 to 0.15625
- w_down: bfloat16 [5504, 1600], P('mlp'), may hold values from -0.078125 to 0.078125
Outputs:
- dec_out: bfloat16 [768, 1600], P(('req', 'mlp'))
- pre_out: bfloat16 [8, 2048, 1600], P('mlp', 'req')
The draws below stay inside these ranges and needn't reach their ends.
Inputs may be any that keep to these rules, and one draw needn't show every extreme that they name: `dec_len`: Heavy-tailed; one request has exactly 4096. `page_owner`: of the 54 entries of one device's requests, at most 4 name the same owner, and some owner is named exactly 4 times for every device. `page_slot`: no two entries with the same owner and the same index along mlp share a slot.
All inputs are finite; a program needn't handle non-finite values.
Results may differ from the reference program's by a relative error of at most 0.02.
Values may be sent and summed in bfloat16 or wider, within the bound.
No kernel may reach another device: no remote copies, remote signals or barrier semaphores. Data moves between devices by JAX's collectives and lax.ppermute only.
A program may use at most 192 MiB of HBM per device.

```python
import math
import jax
import jax.numpy as jnp
from jax import lax

D = 1600
QUERY_HEADS = 25
KEY_VALUE_HEADS = 5
HEAD_SIZE = 64
DI = 3200
DS = 16
DTR = 100
CONV = 4
FF = 5504
WINDOW = 1024
PAGE = 128
CTX = 4096
R_DEV = 6
PREFILL_PER_CHIP = 128
WP = 9
MOST = 4
SLOTS = 64
REQS = 768
SPANS = 8
SPAN_POSITIONS = 2048
POOL = 8192
MIXW = 4800
KVW = 640
XPW = 132
N_REQ = 16
N_MLP = 8


def base_floats(key, shape):
    return jnp.clip(jax.random.normal(key, shape, jnp.float32), -4.0, 4.0)


def draw_decode_query(key, part):
    value_rows = base_floats(jax.random.fold_in(key, 1), (REQS, QUERY_HEADS * HEAD_SIZE))
    return value_rows.astype(jnp.bfloat16)


def draw_pre_q(key, part):
    value_rows = base_floats(jax.random.fold_in(key, 2), (SPANS, SPAN_POSITIONS, QUERY_HEADS * HEAD_SIZE))
    return value_rows.astype(jnp.bfloat16)


def draw_pre_kv(key, part):
    value_rows = base_floats(jax.random.fold_in(key, 3), (SPANS, SPAN_POSITIONS, KVW))
    return value_rows.astype(jnp.bfloat16)


def draw_kv_pool(key, part):
    value_rows = base_floats(jax.random.fold_in(key, 4), (POOL, PAGE, KVW))
    return value_rows.astype(jnp.bfloat16)


def draw_dec_len(key, part):
    shape = (N_REQ, N_MLP, R_DEV)
    top = CTX.bit_length() - 1
    power = jax.random.randint(jax.random.fold_in(key, 5), shape, 0, top + 1)
    upper = jnp.left_shift(jnp.ones(shape, jnp.int32), power.astype(jnp.int32))
    lengths = jax.random.randint(jax.random.fold_in(key, 6), shape, 1, upper + 1)
    forced = jax.random.randint(jax.random.fold_in(key, 7), (), 0, N_REQ * N_MLP * R_DEV)
    flat = lengths.reshape(-1).at[forced].set(CTX)
    return flat.reshape(shape).astype(jnp.int32)


def page_tables(key):
    base_key = jax.random.fold_in(key, 11)
    entries = R_DEV * WP
    groups = N_REQ * N_MLP
    choices_pool = jnp.repeat(jnp.arange(N_REQ, dtype=jnp.int32), MOST)
    owners = jax.vmap(lambda subkey: jax.random.permutation(subkey, choices_pool)[:entries])(jax.random.split(jax.random.fold_in(base_key, 1), groups))
    owners = owners.reshape(N_REQ, N_MLP, entries)
    earlier = jnp.arange(entries)[None, :] < jnp.arange(entries)[:, None]
    same = owners[:, :, :, None] == owners[:, :, None, :]
    rank_of = jnp.sum(same & earlier[None, None], axis=3).astype(jnp.int32)
    position = jnp.arange(N_REQ, dtype=jnp.int32)[:, None, None] * MOST + rank_of
    orders = jax.vmap(lambda subkey: jax.random.permutation(subkey, SLOTS))(jax.random.split(jax.random.fold_in(base_key, 2), groups))
    orders = orders.reshape(N_REQ, N_MLP, SLOTS)
    column = jnp.arange(N_MLP, dtype=jnp.int32)[None, :, None]
    slot_ids = orders[owners, column, position]
    return (owners.reshape(N_REQ, N_MLP, R_DEV, WP).astype(jnp.int32), slot_ids.reshape(N_REQ, N_MLP, R_DEV, WP).astype(jnp.int32))


def draw_page_owner(key, part):
    return page_tables(key)[0]


def draw_page_slot(key, part):
    return page_tables(key)[1]


def levels(key, shape, cuts, least, high):
    level, own = 1.0, jax.random.fold_in(key, 6)
    for dim, shards_of in cuts:
        heights = jnp.exp(jax.random.uniform(jax.random.fold_in(own, dim), (shards_of,), jnp.float32, least / len(cuts), high / len(cuts)))
        level = level * jnp.repeat(heights, shape[dim] // shards_of).reshape([-1 if axis == dim else 1 for axis in range(len(shape))])
    return level


def centred(own_key, dims, spread, bound, cuts=(), kind=jnp.bfloat16):
    values = jax.random.normal(own_key, dims, jnp.float32) * spread
    if len(cuts) > 0:
        values = levels(own_key, dims, cuts, -0.22, 0.18) * values
    return jnp.clip(values, min=-bound, max=bound).astype(kind)


def setup_inputs(seed: int = 0) -> dict:
    keys = jax.random.split(jax.random.key(seed), 29)
    return {
        "decode_query": draw_decode_query(jax.random.fold_in(keys[28], 71), 0),
        "decode_key_value": centred(keys[1], (REQS, KVW), 1.0, 4.0, ((0, 128),)),
        "dec_xz": centred(keys[2], (REQS, 2 * DI), 1.0, 6.0, ((0, 128),)),
        "dec_resid": centred(keys[3], (REQS, D), 1.0, 6.0, ((0, 128),)),
        "dec_conv": centred(keys[4], (REQS, CONV - 1, DI), 1.0, 6.0, ((0, 128),)),
        "dec_state": centred(keys[5], (REQS, DI, DS), 0.5, 4.0, ((0, 128),), jnp.float32),
        "dec_len": draw_dec_len(jax.random.fold_in(keys[28], 71), 0),
        "page_owner": draw_page_owner(jax.random.fold_in(keys[28], 71), 0),
        "page_slot": draw_page_slot(jax.random.fold_in(keys[28], 71), 0),
        "kv_pool": draw_kv_pool(jax.random.fold_in(keys[28], 71), 0),
        "pre_q": draw_pre_q(jax.random.fold_in(keys[28], 71), 0),
        "pre_kv": draw_pre_kv(jax.random.fold_in(keys[28], 71), 0),
        "pre_xz": centred(keys[12], (SPANS, SPAN_POSITIONS, 2 * DI), 1.0, 6.0, ((0, 8), (1, 16))),
        "pre_resid": centred(keys[13], (SPANS, SPAN_POSITIONS, D), 1.0, 6.0, ((0, 8), (1, 16))),
        "w_xproj": centred(keys[14], (DI, XPW), DI ** -0.5, 0.109375),
        "w_dt": centred(keys[15], (DTR, DI), DTR ** -0.5, 0.625),
        "dt_bias": jnp.clip(jax.random.uniform(keys[16], (DI,), jnp.float32, -8.0, -3.0), -8.0, -3.0),
        "a_rate": jnp.clip(jnp.exp(jax.random.uniform(keys[17], (DI, DS), jnp.float32, math.log(0.01), math.log(4.0))), 0.01, 4.0),
        "conv_w": centred(keys[18], (CONV, DI), 0.5, 3.0, (), jnp.float32),
        "conv_b": centred(keys[19], (DI,), 0.5, 3.0, (), jnp.float32),
        "d_skip": jnp.clip(jax.random.uniform(keys[20], (DI,), jnp.float32, 0.5, 1.5), 0.5, 1.5),
        "g_attn": jnp.clip(1.0 + 0.18 * jax.random.normal(keys[21], (QUERY_HEADS * HEAD_SIZE,), jnp.float32), 0.1, 1.9),
        "g_ssm": jnp.clip(1.0 + 0.18 * jax.random.normal(keys[22], (DI,), jnp.float32), 0.1, 1.9),
        "w_out": centred(keys[23], (MIXW, D), MIXW ** -0.5, 0.09375, ((0, 8),)),
        "g_mlp": jnp.clip(1.0 + 0.18 * jax.random.normal(keys[24], (D,), jnp.float32), 0.1, 1.9),
        "w_gate": centred(keys[25], (D, FF), D ** -0.5, 0.15625, ((1, 8),)),
        "w_up": centred(keys[26], (D, FF), D ** -0.5, 0.15625, ((1, 8),)),
        "w_down": centred(keys[27], (FF, D), FF ** -0.5, 0.078125, ((0, 8),)),
    }


EPSILON = 1e-06
MASKED_SCORE = -1e+30

def rms_gain(value_rows, gain):
    return value_rows * lax.rsqrt(lax.optimization_barrier(jnp.mean(value_rows * value_rows, axis=-1, keepdims=True)) + EPSILON) * gain

def ssm_inputs(conv_total, conv_b, w_xproj, w_dt, dt_bias):
    conv_act = jax.nn.silu(conv_total + conv_b)
    projected = jnp.dot(conv_act.astype(jnp.bfloat16), w_xproj, preferred_element_type=jnp.float32)
    dt_low = projected[:, :DTR].astype(jnp.bfloat16)
    step_size = jax.nn.softplus(jnp.dot(dt_low, w_dt, preferred_element_type=jnp.float32) + dt_bias)
    return (conv_act, step_size, projected[:, DTR:DTR + DS], projected[:, DTR + DS:])

def attend(query_rows, key_row_list, allowed):
    row_number = query_rows.shape[0]
    key_count = key_row_list.shape[1]
    queries_per_key = QUERY_HEADS // KEY_VALUE_HEADS
    key_row_width = KEY_VALUE_HEADS * HEAD_SIZE
    score_scale = 1.0 / math.sqrt(HEAD_SIZE)
    query_four_axes = query_rows.astype(jnp.float32).reshape(row_number, KEY_VALUE_HEADS, queries_per_key, HEAD_SIZE)
    key_four_axes = key_row_list[:, :, :key_row_width].astype(jnp.float32).reshape(row_number, key_count, KEY_VALUE_HEADS, HEAD_SIZE)
    value_four_axes = key_row_list[:, :, key_row_width:].astype(jnp.float32).reshape(row_number, key_count, KEY_VALUE_HEADS, HEAD_SIZE)
    scores = jnp.einsum('rhgd,rkhd->rhgk', query_four_axes, key_four_axes) * score_scale
    mask4 = allowed[:, None, None, :]
    scores = jnp.where(mask4, scores, MASKED_SCORE)
    weights = jnp.where(mask4, jnp.exp(scores - lax.optimization_barrier(jnp.max(scores, axis=3, keepdims=True))), 0.0)
    weights = weights / lax.optimization_barrier(jnp.sum(weights, axis=3, keepdims=True))
    return jnp.einsum('rhgk,rkhd->rhgd', weights, value_four_axes).reshape(row_number, QUERY_HEADS * HEAD_SIZE)

def reference(decode_query, decode_key_value, dec_xz, dec_resid, dec_conv, dec_state, dec_len, page_owner, page_slot, kv_pool, pre_q, pre_kv, pre_xz, pre_resid, w_xproj, w_dt, dt_bias, a_rate, conv_w, conv_b, d_skip, g_attn, g_ssm, w_out, g_mlp, w_gate, w_up, w_down):
    groups = N_REQ * N_MLP
    queries_per_key = QUERY_HEADS // KEY_VALUE_HEADS
    key_row_width = KEY_VALUE_HEADS * HEAD_SIZE
    score_scale = 1.0 / math.sqrt(HEAD_SIZE)
    dec_x = dec_xz[:, :DI].astype(jnp.float32)
    dec_z = dec_xz[:, DI:].astype(jnp.float32)
    history = jnp.concatenate([dec_conv.astype(jnp.float32), dec_x[:, None, :]], axis=1)
    conv_total = lax.optimization_barrier(jnp.sum(history * conv_w[None], axis=1))
    conv_act, step_size, ssm_b, ssm_c = ssm_inputs(conv_total, conv_b, w_xproj, w_dt, dt_bias)
    new_state = jnp.exp(-a_rate[None] * step_size[:, :, None]) * dec_state + (step_size * conv_act)[:, :, None] * ssm_b[:, None, :]
    dec_y = (lax.optimization_barrier(jnp.sum(new_state * ssm_c[:, None, :], axis=2)) + d_skip * conv_act) * jax.nn.silu(dec_z)

    def one_group(inputs):
        query_rows, own_kv, owners, slot_ids, lengths, group = inputs
        column = group % N_MLP
        row_ids = (owners * N_MLP + column) * SLOTS + slot_ids
        page_row_list = kv_pool[row_ids.reshape(-1)].reshape(R_DEV, WP * PAGE, KVW)
        first_page = jnp.maximum(lengths - WINDOW + 1, 0) // PAGE
        position = (first_page[:, None, None] + jnp.arange(WP, dtype=jnp.int32)[None, :, None]) * PAGE + jnp.arange(PAGE, dtype=jnp.int32)[None, None, :]
        position = position.reshape(R_DEV, WP * PAGE)
        allowed = (position > (lengths - WINDOW)[:, None]) & (position < lengths[:, None])
        key_row_list = jnp.concatenate([page_row_list, own_kv[:, None, :]], axis=1)
        allowed = jnp.concatenate([allowed, jnp.ones((R_DEV, 1), jnp.bool_)], axis=1)
        return attend(query_rows, key_row_list, allowed)
    dec_attn = lax.map(one_group, (decode_query.reshape(groups, R_DEV, QUERY_HEADS * HEAD_SIZE), decode_key_value.reshape(groups, R_DEV, KVW), page_owner.reshape(groups, R_DEV, WP), page_slot.reshape(groups, R_DEV, WP), dec_len.reshape(groups, R_DEV), jnp.arange(groups, dtype=jnp.int32))).reshape(REQS, QUERY_HEADS * HEAD_SIZE)
    pre_x = pre_xz[:, :, :DI].astype(jnp.float32)
    pre_z = pre_xz[:, :, DI:].astype(jnp.float32).reshape(SPANS * SPAN_POSITIONS, DI)
    padded = jnp.pad(pre_x, ((0, 0), (CONV - 1, 0), (0, 0)))
    conv_total = conv_w[0] * padded[:, 0:SPAN_POSITIONS]
    for offset in range(1, CONV):
        conv_total = conv_total + conv_w[offset] * padded[:, offset:offset + SPAN_POSITIONS]
    conv_act, step_size, ssm_b, ssm_c = ssm_inputs(conv_total.reshape(SPANS * SPAN_POSITIONS, DI), conv_b, w_xproj, w_dt, dt_bias)

    def major(value_rows):
        return jnp.swapaxes(value_rows.reshape(SPANS, SPAN_POSITIONS, -1), 0, 1)

    def advance(ssm_state, inputs):
        step_t, act_t, b_t, c_t = inputs
        ssm_state = jnp.exp(-a_rate[None] * step_t[:, :, None]) * ssm_state + (step_t * act_t)[:, :, None] * b_t[:, None, :]
        return (ssm_state, lax.optimization_barrier(jnp.sum(ssm_state * c_t[:, None, :], axis=2)))
    final_state, pre_y = lax.scan(advance, jnp.zeros((SPANS, DI, DS), jnp.float32), (major(step_size), major(conv_act), major(ssm_b), major(ssm_c)))
    pre_y = jnp.swapaxes(pre_y, 0, 1).reshape(SPANS * SPAN_POSITIONS, DI)
    pre_y = (pre_y + d_skip * conv_act) * jax.nn.silu(pre_z)

    def one_span(inputs):
        query_rows, key_row_list = inputs
        key_four_axes = key_row_list[:, :key_row_width].astype(jnp.float32).reshape(SPAN_POSITIONS, KEY_VALUE_HEADS, HEAD_SIZE)
        value_four_axes = key_row_list[:, key_row_width:].astype(jnp.float32).reshape(SPAN_POSITIONS, KEY_VALUE_HEADS, HEAD_SIZE)
        positions = jnp.arange(SPAN_POSITIONS, dtype=jnp.int32)

        def one_block(block_inputs):
            query_block, first_row = block_inputs
            q_pos = first_row + jnp.arange(PREFILL_PER_CHIP, dtype=jnp.int32)
            allowed = (positions[None, :] <= q_pos[:, None]) & (q_pos[:, None] - positions[None, :] < WINDOW)
            query_four_axes = query_block.astype(jnp.float32).reshape(PREFILL_PER_CHIP, KEY_VALUE_HEADS, queries_per_key, HEAD_SIZE)
            scores = jnp.einsum('qhgd,khd->qhgk', query_four_axes, key_four_axes) * score_scale
            mask4 = allowed[:, None, None, :]
            scores = jnp.where(mask4, scores, MASKED_SCORE)
            weights = jnp.where(mask4, jnp.exp(scores - lax.optimization_barrier(jnp.max(scores, axis=3, keepdims=True))), 0.0)
            weights = weights / lax.optimization_barrier(jnp.sum(weights, axis=3, keepdims=True))
            return jnp.einsum('qhgk,khd->qhgd', weights, value_four_axes).reshape(PREFILL_PER_CHIP, QUERY_HEADS * HEAD_SIZE)
        blocks = SPAN_POSITIONS // PREFILL_PER_CHIP
        return lax.map(one_block, (query_rows.reshape(blocks, PREFILL_PER_CHIP, QUERY_HEADS * HEAD_SIZE), jnp.arange(blocks, dtype=jnp.int32) * PREFILL_PER_CHIP)).reshape(SPAN_POSITIONS, QUERY_HEADS * HEAD_SIZE)
    pre_attn = lax.map(one_span, (pre_q, pre_kv)).reshape(SPANS * SPAN_POSITIONS, QUERY_HEADS * HEAD_SIZE)

    def finish(attn_rows, y_rows, resid_rows):
        mix_rows = jnp.concatenate([rms_gain(attn_rows, g_attn).astype(jnp.bfloat16), rms_gain(y_rows, g_ssm).astype(jnp.bfloat16)], axis=1)
        after_mix = resid_rows.astype(jnp.float32) + jnp.dot(mix_rows, w_out, preferred_element_type=jnp.float32)
        normed = rms_gain(after_mix, g_mlp).astype(jnp.bfloat16)
        gate = jnp.dot(normed, w_gate, preferred_element_type=jnp.float32)
        upward = jnp.dot(normed, w_up, preferred_element_type=jnp.float32)
        hidden = (jax.nn.silu(gate) * upward).astype(jnp.bfloat16)
        return (after_mix + jnp.dot(hidden, w_down, preferred_element_type=jnp.float32)).astype(jnp.bfloat16)
    dec_out = finish(dec_attn, dec_y, dec_resid)
    pre_out = finish(pre_attn, pre_y, pre_resid.reshape(SPANS * SPAN_POSITIONS, D)).reshape(SPANS, SPAN_POSITIONS, D)
    return (dec_out, pre_out)
```

```python
import functools
import math

import jax
import jax.numpy as jnp
from jax import lax
from jax.experimental import pallas as pl
from jax.experimental.pallas import tpu as pltpu
from jax.sharding import PartitionSpec as P

QUERY_HEADS = 25
KEY_VALUE_HEADS = 5
GROUP = QUERY_HEADS // KEY_VALUE_HEADS
HEAD_SIZE = 64
D = QUERY_HEADS * HEAD_SIZE
KEYW = KEY_VALUE_HEADS * HEAD_SIZE
DI = 3200
DS = 16
DTR = 100
CONV = 4
WINDOW = 1024
PAGE = 128

T = 128
ROWS = 144
TAIL = ROWS - T
LANES = 640
BLOCKS = DI // LANES
HEADS = 32
SIDE = 4
DEPTH = 8

EPSILON = 1e-06
MASKED = -1e30
LOG2E = math.log2(math.e)
F32 = jnp.float32
BF16 = jnp.bfloat16
NT = (((1,), (1,)), ((), ()))
NN = (((1,), (0,)), ((), ()))
TN = (((0,), (0,)), ((), ()))

VMEM = pl.BlockSpec(memory_space=pltpu.VMEM)
SMEM = pl.BlockSpec(memory_space=pltpu.SMEM)
ANY = pl.BlockSpec(memory_space=pl.ANY)


def dot(a, b, dims):
    return lax.dot_general(a, b, dims, preferred_element_type=F32)


def params(mib):
    return pltpu.CompilerParams(vmem_limit_bytes=mib * 2**20)


def cost(flops, bytes_accessed):
    return pl.CostEstimate(flops=flops, bytes_accessed=bytes_accessed, transcendentals=0)


def lanes_of(block, start=0):
    return pl.ds(pl.multiple_of(start + block * LANES, 128), LANES)


def silu(v):
    return v * lax.logistic(v)


def softplus(v):
    return jnp.maximum(v, 0.0) + jnp.log1p(jnp.exp(-jnp.abs(v)))


def wide(tile):
    return jnp.concatenate([tile] * (LANES // 128), axis=1)


def spread(columns, out_ref):
    for t in range(T):
        out_ref[t] = jnp.broadcast_to(columns[:, t : t + 1], (DS, 128))


def front_kernel(
    x_ref, rim_ref, tail_ref, taps_ref, conv_b_ref, w_ref, w_bc_ref, w_dt_ref, bias_ref, rate_ref,
    act_ref, step_ref, bc_ref, end_ref,
    padded, drive, b_wide,
):
    def fill(k, _):
        cols = lanes_of(k)
        padded[0:8, cols] = rim_ref[:, cols].astype(F32)[8:16]
        padded[8 : 8 + T, cols] = x_ref[:, cols].astype(F32)
        return 0

    lax.fori_loop(0, BLOCKS, fill, 0)

    def conv(k, carry):
        proj, bc = carry
        cols = lanes_of(k)
        total = taps_ref[0:1, cols] * padded[5 : 5 + T, cols]
        for tap in range(1, CONV):
            total = total + taps_ref[tap : tap + 1, cols] * padded[5 + tap : 5 + tap + T, cols]
        total = jnp.concatenate([total, tail_ref[:, cols]], axis=0)
        act = silu(total + conv_b_ref[:, cols])
        act_ref[:, cols] = act
        low = act.astype(BF16)
        return (
            proj + dot(low, w_ref[:, cols], NT),
            bc + dot(w_bc_ref[:, cols], low, NT),
        )

    proj, bc = lax.fori_loop(
        0, BLOCKS, conv, (jnp.zeros((ROWS, DTR + 2 * DS), F32), jnp.zeros((2 * DS, ROWS), F32))
    )
    bc_ref[...] = bc
    dt_low = proj[:, :DTR].astype(BF16)
    spread(bc[:DS], b_wide)

    def step(k, _):
        cols = lanes_of(k)
        size = softplus(dot(dt_low, w_dt_ref[:, cols], NN) + bias_ref[:, cols])
        step_ref[:, cols] = size
        drive[:, cols] = size[:T] * act_ref[0:T, cols]
        return 0

    lax.fori_loop(0, BLOCKS, step, 0)

    def scan(k, _):
        cols = lanes_of(k)
        rate = rate_ref[:, cols] * -LOG2E

        def one(t, state):
            size = step_ref[pl.ds(t, 1), cols]
            push = drive[pl.ds(t, 1), cols]
            return jnp.exp2(rate * size) * state + wide(b_wide[t]) * push

        state = lax.fori_loop(0, T, one, jnp.zeros((DS, LANES), F32), unroll=8)
        total = jnp.sum(step_ref[0:T, cols], axis=0, keepdims=True)
        high = total.astype(BF16).astype(F32)
        row = lax.broadcasted_iota(jnp.int32, (DS, LANES), 0)
        sums = jnp.where(row == 0, high, jnp.where(row == 1, total - high, 0.0))
        end_ref[:, cols] = jnp.concatenate([state, sums], axis=0).astype(BF16)
        return 0

    lax.fori_loop(0, BLOCKS, scan, 0)


def front(x, rim, tail, taps, conv_b, w, w_bc, w_dt, bias, rate):
    rest = (rim, tail, taps, conv_b, w, w_bc, w_dt, bias, rate)
    return pl.pallas_call(
        front_kernel,
        out_shape=(
            jax.ShapeDtypeStruct((ROWS, DI), F32),
            jax.ShapeDtypeStruct((ROWS, DI), F32),
            jax.ShapeDtypeStruct((2 * DS, ROWS), F32),
            jax.ShapeDtypeStruct((2 * DS, DI), BF16),
        ),
        in_specs=[VMEM] * 10,
        out_specs=(VMEM,) * 4,
        scratch_shapes=[
            pltpu.VMEM((8 + T, DI), F32),
            pltpu.VMEM((T, DI), F32),
            pltpu.VMEM((T, DS, 128), F32),
        ],
        compiler_params=params(40),
        cost_estimate=cost(10**9, 40 * 10**6),
        name="front",
    )(x, *rest)


def scan_kernel(
    z_ref, act_ref, step_ref, bc_ref, rate_ref, enter_ref, skip_ref, gain_ref,
    out_ref,
    drive, b_wide, c_wide, parts, y_ref,
):
    bc = bc_ref[...]
    spread(bc[:DS], b_wide)
    spread(bc[DS:], c_wide)
    row = lax.broadcasted_iota(jnp.int32, (T, 8 * T), 0)
    col = lax.broadcasted_iota(jnp.int32, (T, 8 * T), 1)
    pick = jnp.where(col // 8 == row, 1.0, 0.0).astype(BF16)

    def block(k, squares):
        cols = lanes_of(k)
        rate = rate_ref[:, cols] * -LOG2E
        drive[...] = step_ref[0:T, cols] * act_ref[0:T, cols]

        def one(pair, state):
            halves = []
            for t in (2 * pair, 2 * pair + 1):
                size = step_ref[pl.ds(t, 1), cols]
                push = drive[pl.ds(t, 1), :]
                state = jnp.exp2(rate * size) * state + wide(b_wide[t]) * push
                seen = state * wide(c_wide[t])
                halves.append(seen[0:8] + seen[8:16])
            at = pl.multiple_of(16 * pair, 16)
            parts[pl.ds(at, 16), :] = jnp.concatenate(halves, axis=0).astype(BF16)
            return state

        lax.fori_loop(0, T // 2, one, enter_ref[:, cols], unroll=4)
        y = dot(pick, parts[...], NN) + skip_ref[:, cols] * act_ref[0:T, cols]
        y = y * silu(z_ref[:, lanes_of(k, DI)].astype(F32))
        y_ref[:, cols] = y
        return squares + jnp.sum(y * y, axis=1, keepdims=True)

    squares = lax.fori_loop(0, BLOCKS, block, jnp.zeros((T, 1), F32))
    scale = lax.rsqrt(squares * (1.0 / DI) + EPSILON)

    def norm(k, _):
        cols = lanes_of(k)
        out_ref[:, cols] = (y_ref[:, cols] * scale * gain_ref[:, cols]).astype(BF16)
        return 0

    lax.fori_loop(0, BLOCKS, norm, 0)


def scan(xz, act, step, bc, rate, enter, skip, gain):
    rest = (act, step, bc, rate, enter, skip, gain)
    return pl.pallas_call(
        scan_kernel,
        out_shape=jax.ShapeDtypeStruct((T, DI), BF16),
        in_specs=[VMEM] * 8,
        out_specs=VMEM,
        scratch_shapes=[
            pltpu.VMEM((T, LANES), F32),
            pltpu.VMEM((T, DS, 128), F32),
            pltpu.VMEM((T, DS, 128), F32),
            pltpu.VMEM((8 * T, LANES), BF16),
            pltpu.VMEM((T, DI), F32),
        ],
        compiler_params=params(40),
        cost_estimate=cost(10**9, 40 * 10**6),
        name="scan",
    )(xz, *rest)


def attend_kernel(r_ref, q_ref, kv_ref, gain_ref, out_ref, scores, mixed):
    r = r_ref[0]
    wide_rows = GROUP * T
    back = WINDOW // T
    key = lax.broadcasted_iota(jnp.int32, (T, wide_rows), 0)
    query = lax.broadcasted_iota(jnp.int32, (T, wide_rows), 1) % T
    for h in range(KEY_VALUE_HEADS):
        first = h * GROUP * HEAD_SIZE
        q = jnp.concatenate(
            [q_ref[first + g * HEAD_SIZE : first + (g + 1) * HEAD_SIZE, :] for g in range(GROUP)],
            axis=1,
        )
        q = (q.astype(F32) * (1.0 / math.sqrt(HEAD_SIZE))).astype(BF16)
        none = jnp.zeros_like(q)
        q = jnp.concatenate([q, none] if h % 2 == 0 else [none, q], axis=0)
        key_cols = slice(128 * (h // 2), 128 * (h // 2) + 128)
        at = KEYW + h * HEAD_SIZE
        value_cols = slice(at // 128 * 128, at // 128 * 128 + 128)
        value_row = at % 128
        top = jnp.full((1, wide_rows), MASKED, F32)
        for j in range(back + 1):
            rows = pl.ds(pl.multiple_of(jnp.maximum(r - back + j, 0) * T, T), T)
            s = dot(kv_ref[rows, key_cols], q, NN)
            if j == back:
                s = jnp.where(key <= query, s, MASKED)
            elif j == 0:
                s = jnp.where(jnp.logical_and(key > query, r >= back), s, MASKED)
            else:
                s = jnp.where(r - back + j >= 0, s, MASKED)
            scores[j] = s
            top = jnp.maximum(top, jnp.max(s, axis=0, keepdims=True))
        total = jnp.zeros((1, wide_rows), F32)
        sums = jnp.zeros((128, wide_rows), F32)
        for j in range(back + 1):
            rows = pl.ds(pl.multiple_of(jnp.maximum(r - back + j, 0) * T, T), T)
            weight = jnp.exp(scores[j] - top)
            total = total + jnp.sum(weight, axis=0, keepdims=True)
            sums = sums + dot(kv_ref[rows, value_cols], weight.astype(BF16), TN)
        part = sums[value_row : value_row + HEAD_SIZE] / total
        for g in range(GROUP):
            mixed[first + g * HEAD_SIZE : first + (g + 1) * HEAD_SIZE, :] = part[
                :, g * T : (g + 1) * T
            ]
    values = mixed[...]
    scale = lax.rsqrt(jnp.mean(values * values, axis=0, keepdims=True) + EPSILON)
    out_ref[...] = (jnp.transpose(values * scale) * gain_ref[...]).astype(BF16)


def attend(r, q, kv, gain):
    return pl.pallas_call(
        attend_kernel,
        out_shape=jax.ShapeDtypeStruct((T, D), BF16),
        in_specs=[SMEM, VMEM, VMEM, VMEM],
        out_specs=VMEM,
        scratch_shapes=[
            pltpu.VMEM((WINDOW // T + 1, T, GROUP * T), F32),
            pltpu.VMEM((D, T), F32),
        ],
        compiler_params=params(40),
        cost_estimate=cost(10**9, 30 * 10**6),
        name="attend",
    )(r, q, kv, gain)


def pages_kernel(count_ref, code_ref, len_ref, q_ref, pool_ref, out_ref, pages, sems):
    count = count_ref[0]

    def fetch(n):
        slot = code_ref[n] & 63
        place = lax.rem(n, DEPTH)
        return pltpu.make_async_copy(pool_ref.at[slot], pages.at[place], sems.at[place])

    for n in range(DEPTH):

        @pl.when(n < count)
        def _():
            fetch(n).start()

    head = lax.broadcasted_iota(jnp.int32, (HEADS, 128), 0)
    lane = lax.broadcasted_iota(jnp.int32, (HEADS, 128), 1)
    block_of = head // (2 * GROUP)
    kv_head = head // GROUP

    def one(n, _):
        code = code_ref[n]
        place = lax.rem(n, DEPTH)
        request = (code >> 6) & 127
        page_index = (code >> 13) & 15
        row = (code >> 17) & 63
        length = len_ref[request]
        first = jnp.maximum(length - (WINDOW - 1), 0) // PAGE
        base = (first + page_index) * PAGE
        q = q_ref[pl.ds(pl.multiple_of(request * HEADS, HEADS), HEADS), :].astype(F32)
        q = jnp.concatenate([jnp.where(block_of == b, q, 0.0) for b in range(3)], axis=1)
        q = (q * (1.0 / math.sqrt(HEAD_SIZE))).astype(BF16)
        fetch(n).wait()
        s = dot(q, pages[place, :, 0:384], NT)
        position = base + lane
        seen = jnp.logical_and(position > length - WINDOW, position < length)
        s = jnp.where(seen, s, MASKED)
        top = jnp.max(s, axis=1, keepdims=True)
        weight = jnp.where(seen, jnp.exp(s - top), 0.0)
        total = jnp.sum(weight, axis=1, keepdims=True)
        sums = dot(weight.astype(BF16), pages[place, :, 256:640], NN)
        picked = jnp.where(
            kv_head == 0,
            sums[:, 0:128],
            jnp.where(kv_head <= 2, sums[:, 128:256], sums[:, 256:384]),
        )
        picked = jnp.where(kv_head % 2 == 0, pltpu.roll(picked, 64, 1), picked)
        level = top + jnp.log(total)
        high = level.astype(BF16).astype(F32)
        middle = (level - high).astype(BF16).astype(F32)
        low = level - high - middle
        tile = jnp.where(
            lane < HEAD_SIZE,
            picked / total,
            jnp.where(
                lane == HEAD_SIZE,
                high,
                jnp.where(lane == HEAD_SIZE + 1, middle, jnp.where(lane == HEAD_SIZE + 2, low, 0.0)),
            ),
        )
        out_ref[pl.ds(pl.multiple_of(row * HEADS, HEADS), HEADS), :] = tile.astype(BF16)

        @pl.when(n + DEPTH < count)
        def _():
            fetch(n + DEPTH).start()

        return 0

    lax.fori_loop(0, count, one, 0)


def page_shares(count, codes, lengths, queries, pool, rows):
    return pl.pallas_call(
        pages_kernel,
        out_shape=jax.ShapeDtypeStruct((rows * HEADS, 128), BF16),
        in_specs=[SMEM, SMEM, SMEM, VMEM, ANY],
        out_specs=VMEM,
        scratch_shapes=[
            pltpu.VMEM((DEPTH, PAGE, 2 * KEYW), BF16),
            pltpu.SemaphoreType.DMA((DEPTH,)),
        ],
        compiler_params=params(32),
        cost_estimate=cost(10**8, 20 * 10**6),
        name="page_shares",
    )(count, codes, lengths, queries, pool)


def decode_kernel(
    count_ref, code_ref, shares_ref, score_ref, value_ref, gain_a_ref,
    act_ref, step_ref, bc_ref, state_ref, rate_ref, skip_ref, z_ref, gain_s_ref,
    attn_ref, y_out_ref,
    tops, totals, sums, y_ref,
):
    requests = score_ref.shape[0]
    count = count_ref[0]
    tops[...] = score_ref[...]

    def level_of(share):
        return jnp.broadcast_to(share[:, 64:65] + share[:, 65:66] + share[:, 66:67], (HEADS, 128))

    def share_of(row):
        return shares_ref[pl.ds(pl.multiple_of(row * HEADS, HEADS), HEADS), :].astype(F32)

    def highest(n, _):
        request = code_ref[n] >> 6
        tops[request] = jnp.maximum(tops[request], level_of(share_of(code_ref[n] & 63)))
        return 0

    lax.fori_loop(0, count, highest, 0)
    own = jnp.exp(score_ref[...] - tops[...])
    totals[...] = own
    sums[...] = own * value_ref[...]

    def add(n, _):
        request = code_ref[n] >> 6
        share = share_of(code_ref[n] & 63)
        weight = jnp.exp(level_of(share) - tops[request])
        totals[request] = totals[request] + weight
        sums[request] = sums[request] + weight * share
        return 0

    lax.fori_loop(0, count, add, 0)
    head = lax.broadcasted_iota(jnp.int32, (HEADS, 128), 0)
    lane = lax.broadcasted_iota(jnp.int32, (HEADS, 128), 1)
    real = jnp.logical_and(head < QUERY_HEADS, lane < HEAD_SIZE)
    for i in range(requests):
        value = jnp.where(real, sums[i] / totals[i], 0.0)
        square = jnp.sum(jnp.sum(value * value, axis=1, keepdims=True), axis=0, keepdims=True)
        scale = lax.rsqrt(square * (1.0 / D) + EPSILON)
        attn_ref[i] = (value * scale * gain_a_ref[...]).astype(BF16)

    bc = bc_ref[...]
    y_ref[...] = jnp.zeros_like(y_ref)

    def block(k, squares):
        cols = lanes_of(k)
        rate = rate_ref[:, cols] * -LOG2E
        for i in range(requests):
            size = step_ref[T + i : T + i + 1, cols]
            act = act_ref[T + i : T + i + 1, cols]
            b = bc[:DS, T + i : T + i + 1]
            c = bc[DS:, T + i : T + i + 1]
            state = jnp.exp2(rate * size) * state_ref[i, :, cols] + b * (size * act)
            y_ref[i : i + 1, cols] = jnp.sum(state * c, axis=0, keepdims=True)
        y = y_ref[:, cols] + skip_ref[:, cols] * act_ref[T:ROWS, cols]
        y = y * silu(z_ref[:, cols])
        y_ref[:, cols] = y
        return squares + jnp.sum(y * y, axis=1, keepdims=True)

    squares = lax.fori_loop(0, BLOCKS, block, jnp.zeros((TAIL, 1), F32))
    scale = lax.rsqrt(squares * (1.0 / DI) + EPSILON)

    def norm(k, _):
        cols = lanes_of(k)
        y_out_ref[:, cols] = (y_ref[:, cols] * scale * gain_s_ref[:, cols]).astype(BF16)
        return 0

    lax.fori_loop(0, BLOCKS, norm, 0)


def decode(count, codes, *rest):
    requests = rest[1].shape[0]
    return pl.pallas_call(
        decode_kernel,
        out_shape=(
            jax.ShapeDtypeStruct((requests, HEADS, 128), BF16),
            jax.ShapeDtypeStruct((TAIL, DI), BF16),
        ),
        in_specs=[SMEM, SMEM] + [VMEM] * len(rest),
        out_specs=(VMEM, VMEM),
        scratch_shapes=[
            pltpu.VMEM((requests, HEADS, 128), F32),
            pltpu.VMEM((requests, HEADS, 128), F32),
            pltpu.VMEM((requests, HEADS, 128), F32),
            pltpu.VMEM((TAIL, DI), F32),
        ],
        compiler_params=params(32),
        cost_estimate=cost(10**8, 20 * 10**6),
        name="decode",
    )(count, codes, *rest)


def project_kernel(
    place_ref, attn_ref, attn_tail_ref, y_ref, y_tail_ref, resid_ref, gain_ref, *rest
):
    shards = place_ref.shape[0]
    weights = rest[:shards]
    after_ref, normed_ref, mix = rest[shards:]
    width = mix.shape[2]
    for m in range(shards):
        low, high = m * width, (m + 1) * width
        for rows, attn, y in (
            (slice(0, T), attn_ref, y_ref),
            (slice(T, ROWS), attn_tail_ref, y_tail_ref),
        ):
            pieces = []
            if low < D:
                pieces.append(attn[:, low : min(high, D)].astype(F32))
            if high > D:
                pieces.append(y[:, max(low, D) - D : high - D].astype(F32))
            piece = pieces[0] if len(pieces) == 1 else jnp.concatenate(pieces, axis=1)
            mix[m, rows, :] = piece.astype(BF16)
    after_ref[...] = resid_ref[...].astype(F32)
    for s in range(shards):
        after_ref[...] += dot(mix[place_ref[s]], weights[s][...], NN)
    after = after_ref[...]
    scale = lax.rsqrt(jnp.mean(after * after, axis=1, keepdims=True) + EPSILON)
    normed_ref[...] = (after * scale * gain_ref[...]).astype(BF16)


def project(places, attn, attn_tail, y, y_tail, resid, gain, weights):
    width = weights[0].shape[0]
    return pl.pallas_call(
        project_kernel,
        out_shape=(
            jax.ShapeDtypeStruct((ROWS, D), F32),
            jax.ShapeDtypeStruct((ROWS, D), BF16),
        ),
        in_specs=[SMEM] + [VMEM] * (6 + len(weights)),
        out_specs=(VMEM, VMEM),
        scratch_shapes=[pltpu.VMEM((len(weights), ROWS, width), BF16)],
        compiler_params=params(48),
        cost_estimate=cost(2 * 10**9, 30 * 10**6),
        name="project",
    )(places, attn, attn_tail, y, y_tail, resid, gain, *weights)


def mlp_kernel(count, *refs):
    rows = refs[:count]
    sources = refs[count : count + 6]
    outs = refs[count + 6 : 2 * count + 6]
    buffers = refs[2 * count + 6 : 2 * count + 12]
    sems = refs[2 * count + 12]
    copies = [
        pltpu.make_async_copy(sources[i], buffers[i], sems.at[i]) for i in range(6)
    ]
    for copy in copies:
        copy.start()
    totals = [None] * count
    for s in range(2):
        for i in range(3):
            copies[3 * s + i].wait()
        gate_w, up_w, down_w = buffers[3 * s : 3 * s + 3]
        for n in range(count):
            value = rows[n][...]
            hidden = silu(dot(value, gate_w[...], NT)) * dot(value, up_w[...], NT)
            part = dot(hidden.astype(BF16), down_w[...], NN)
            if s == 0:
                refs[2 * count + 13 + n][...] = part
            else:
                outs[n][...] = (refs[2 * count + 13 + n][...] + part).astype(outs[n].dtype)


def mlp(rows, weights, kind):
    count = len(rows)
    return pl.pallas_call(
        functools.partial(mlp_kernel, count),
        out_shape=tuple(jax.ShapeDtypeStruct((ROWS, D), kind) for _ in rows),
        in_specs=[VMEM] * count + [ANY] * 6,
        out_specs=(VMEM,) * count,
        scratch_shapes=[pltpu.VMEM(w.shape, BF16) for w in weights]
        + [pltpu.SemaphoreType.DMA((6,))]
        + [pltpu.VMEM((ROWS, D), F32) for _ in rows],
        compiler_params=params(48),
        cost_estimate=cost(2 * 10**9 * count, 15 * 10**6),
        name="mlp",
    )(*rows, *weights)


def padded_to(a, axis, size):
    pads = [(0, 0)] * a.ndim
    pads[axis] = (0, size - a.shape[axis])
    return jnp.pad(a, pads)


def shards(
    decode_query,
    decode_key_value,
    dec_xz,
    dec_resid,
    dec_conv,
    dec_state,
    dec_len,
    page_owner,
    page_slot,
    kv_pool,
    pre_q,
    pre_kv,
    pre_xz,
    pre_resid,
    w_xproj,
    w_dt,
    dt_bias,
    a_rate,
    conv_w,
    conv_b,
    d_skip,
    g_attn,
    g_ssm,
    w_out,
    g_mlp,
    w_gate,
    w_up,
    w_down,
):
    req_count = lax.axis_size("req")
    mlp_count = lax.axis_size("mlp")
    my_req = lax.axis_index("req")
    my_mlp = lax.axis_index("mlp")
    my_x = my_req % SIDE
    my_y = my_req // SIDE
    my_z, my_core = my_mlp // 2, my_mlp % 2
    requests = decode_query.shape[0]
    row = lambda a: a[None, :]

    def along_x(a, by):
        pairs = [(r, r // SIDE * SIDE + (r + by) % SIDE) for r in range(req_count)]
        return lax.ppermute(a, "req", pairs)

    def along_y(a, by):
        pairs = [(r, (r // SIDE + by) % SIDE * SIDE + r % SIDE) for r in range(req_count)]
        return lax.ppermute(a, "req", pairs)

    def along_z(a, by):
        pairs = [
            (m, (m // 2 + (by if m % 2 == 0 else -by)) % SIDE * 2 + m % 2) for m in range(mlp_count)
        ]
        return lax.ppermute(a, "mlp", pairs)

    def across(a):
        return lax.ppermute(a, "mlp", [(m, m ^ 1) for m in range(mlp_count)])

    xz = pre_xz[0]
    rim = lax.ppermute(
        xz[T - 16 :, :DI], "req", [(r, r + 1) for r in range(req_count - 1)]
    )

    window_pages = page_owner.shape[3]
    entries = requests * window_pages
    owners = page_owner[:, 0].reshape(req_count, entries)
    slot_ids = page_slot[:, 0].reshape(req_count, entries)
    lengths = dec_len[:, 0]
    first_page = jnp.maximum(lengths - (WINDOW - 1), 0) // PAGE
    page_index = jnp.arange(window_pages, dtype=jnp.int32)
    used = ((first_page[:, :, None] + page_index) * PAGE < lengths[:, :, None]).reshape(
        req_count, entries
    )
    entry = jnp.arange(entries, dtype=jnp.int32)
    earlier = entry[None, :] < entry[:, None]
    same = (owners[:, :, None] == owners[:, None, :]) & used[:, None, :]
    rank = jnp.sum(jnp.where(same & earlier[None], 1, 0), axis=2)
    most = 64 // req_count
    device = jnp.arange(req_count, dtype=jnp.int32)[:, None]
    code = (
        slot_ids
        | (device * requests + entry[None, :] // window_pages) << 6
        | (entry[None, :] % window_pages) << 13
        | (device * most + rank) << 17
    )

    def compact(mask, values):
        mask, values = mask.reshape(-1), values.reshape(-1)
        number = jnp.arange(mask.shape[0], dtype=jnp.int32)
        ahead = mask[None, :] & (number[None, :] < number[:, None])
        order = jnp.sum(jnp.where(ahead, 1, 0), axis=1)
        hit = mask[None, :] & (order[None, :] == jnp.arange(64, dtype=jnp.int32)[:, None])
        count = jnp.sum(jnp.where(mask, 1, 0)).reshape(1)
        return count, jnp.sum(jnp.where(hit, values[None, :], 0), axis=1)

    sent_count, sent_codes = compact((owners == my_req) & used, code)
    own = lambda a: lax.dynamic_index_in_dim(a, my_req, 0, keepdims=False)
    got_count, got_codes = compact(
        own(used), (own(owners) * most + own(rank)) | (entry // window_pages) << 6
    )

    heads = decode_query.reshape(requests, QUERY_HEADS, HEAD_SIZE)
    upper = (jnp.arange(QUERY_HEADS) // GROUP % 2 == 1)[None, :, None]
    none = jnp.zeros_like(heads)
    halves = jnp.concatenate([jnp.where(upper, none, heads), jnp.where(upper, heads, none)], axis=2)
    halves = padded_to(halves, 1, HEADS).reshape(requests * HEADS, 128)
    queries = lax.all_gather(halves, "req", axis=0, tiled=True)
    span_kv = lax.all_gather(pre_kv[0], "req", axis=0, tiled=True)

    up_one = along_z(w_out, 1)
    down_one = along_z(w_out, -1)
    up_two = along_z(up_one, 1)
    held = [w_out, up_one, down_one, up_two]
    out_weights = held + [across(a) for a in held]
    sign = 1 - 2 * my_core
    offsets = jnp.array([0, -1, 1, -2], jnp.int32)
    mine = (my_z + sign * offsets) % SIDE * 2 + my_core
    other = (my_z - sign * offsets) % SIDE * 2 + 1 - my_core
    places = jnp.concatenate([mine, other]).astype(jnp.int32)
    gate_t, up_t = jnp.swapaxes(w_gate, 0, 1), jnp.swapaxes(w_up, 0, 1)
    mlp_weights = [gate_t, up_t, w_down]
    mlp_weights = mlp_weights + [across(a) for a in mlp_weights]

    rate = jnp.swapaxes(a_rate, 0, 1)
    w_x = jnp.swapaxes(w_xproj, 0, 1)
    tail = jnp.sum(dec_conv.astype(F32) * conv_w[None, : CONV - 1], axis=1) + dec_xz[:, :DI].astype(
        F32
    ) * row(conv_w[CONV - 1])
    act, step, bc, ends = front(
        xz, rim, padded_to(tail, 0, TAIL), conv_w, row(conv_b), w_x, w_x[DTR:], w_dt, row(dt_bias), rate
    )

    def parts_of(block):
        block = block.astype(F32)
        return block[:DS], block[DS] + block[DS + 1]

    def chain(state, block, valid):
        end, total = block
        decay = jnp.exp2(rate * -LOG2E * total[None, :])
        return jnp.where(valid, decay * state + end, state)

    blocks = [parts_of(along_x(ends, by)) for by in range(1, SIDE)]
    state = jnp.zeros((DS, DI), F32)
    before = jnp.zeros((DI,), F32)
    for by in range(SIDE - 1, 0, -1):
        state = chain(state, blocks[by - 1], my_x >= by)
        before = before + jnp.where(my_x >= by, blocks[by - 1][1], 0.0)
    row_start = state
    own_block = parts_of(ends)
    state = chain(state, own_block, True)
    for by in range(SIDE - 1, 0, -1):
        state = chain(state, blocks[by - 1], my_x < by)
    row_total = own_block[1] + blocks[0][1] + blocks[1][1] + blocks[2][1]
    high = row_total.astype(BF16)
    low = (row_total - high.astype(F32)).astype(BF16)
    row_block = jnp.concatenate(
        [state.astype(BF16), row(high), row(low), jnp.zeros((DS - 2, DI), BF16)], axis=0
    )
    state = jnp.zeros((DS, DI), F32)
    row_blocks = [parts_of(along_y(row_block, by)) for by in range(1, SIDE)]
    for by in range(SIDE - 1, 0, -1):
        state = chain(state, row_blocks[by - 1], my_y >= by)
    enter = chain(state, (row_start, before), True)

    shares = page_shares(
        sent_count, sent_codes, lengths.reshape(-1), queries, kv_pool, req_count * most
    )
    shares = lax.all_to_all(shares, "req", split_axis=0, concat_axis=0, tiled=True)
    by_head = lambda a: jnp.repeat(a.reshape(requests, KEY_VALUE_HEADS, HEAD_SIZE), GROUP, axis=1)
    own_key = by_head(decode_key_value[:, :KEYW]).astype(F32)
    own_value = by_head(decode_key_value[:, KEYW:]).astype(F32)
    own_score = jnp.sum(heads.astype(F32) * own_key, axis=2, keepdims=True) / math.sqrt(HEAD_SIZE)
    tile = lambda a: padded_to(padded_to(a, 1, HEADS), 2, 128)
    own_score = padded_to(jnp.broadcast_to(own_score, (requests, QUERY_HEADS, 128)), 1, HEADS)
    gain_a = tile(g_attn.reshape(1, QUERY_HEADS, HEAD_SIZE))[0]
    dec_attn, dec_y = decode(
        got_count, got_codes, shares, own_score, tile(own_value), gain_a,
        act, step, bc, jnp.swapaxes(dec_state, 1, 2), rate, row(d_skip),
        padded_to(dec_xz[:, DI:].astype(F32), 0, TAIL), row(g_ssm),
    )
    dec_attn = padded_to(dec_attn[:, :QUERY_HEADS, :HEAD_SIZE].reshape(requests, D), 0, TAIL)

    pre_attn = attend(
        my_req.reshape(1).astype(jnp.int32), jnp.swapaxes(pre_q[0], 0, 1), span_kv, row(g_attn)
    )
    pre_y = scan(xz, act, step, bc, rate, enter, row(d_skip), row(g_ssm))

    resid = jnp.concatenate([pre_resid[0], padded_to(dec_resid, 0, TAIL)], axis=0)
    after_mix, normed = project(
        places, pre_attn, dec_attn, pre_y, dec_y, resid, row(g_mlp), out_weights
    )

    one_up = along_z(normed, 1)
    one_down = along_z(normed, -1)
    two_up = along_z(one_up, 1)
    (sum_own,) = mlp([normed], mlp_weights, F32)
    sum_up, sum_down = mlp([one_up, one_down], mlp_weights, BF16)
    (sum_two,) = mlp([two_up], mlp_weights, BF16)
    back_two = along_z(sum_two, -1)
    back_down = along_z(sum_down, 1)
    back_up = along_z((sum_up.astype(F32) + back_two.astype(F32)).astype(BF16), -1)
    final_rows = (
        after_mix + sum_own + back_down.astype(F32) + back_up.astype(F32)
    ).astype(BF16)
    return (final_rows[T : T + requests], final_rows[:T][None])


def solution(mesh):
    both = ("req", "mlp")
    in_specs = (
        P(both, None),
        P(both, None),
        P(both, None),
        P(both, None),
        P(both, None, None),
        P(both, None, None),
        P(None, "mlp", None),
        P(None, "mlp", None, None),
        P(None, "mlp", None, None),
        P(both, None, None),
        P("mlp", "req", None),
        P("mlp", "req", None),
        P("mlp", "req", None),
        P("mlp", "req", None),
        P(),
        P(),
        P(),
        P(),
        P(),
        P(),
        P(),
        P(),
        P(),
        P("mlp", None),
        P(),
        P(None, "mlp"),
        P(None, "mlp"),
        P("mlp", None),
    )
    out_specs = (P(both, None), P("mlp", "req", None))
    return jax.shard_map(shards, mesh=mesh, in_specs=in_specs, out_specs=out_specs, check_vma=False)
```

```python
import functools
import math

import jax
import jax.numpy as jnp
from jax import lax
from jax.experimental import pallas as pl
from jax.experimental.pallas import tpu as pltpu
from jax.sharding import PartitionSpec as P

QUERY_HEADS = 25
KEY_VALUE_HEADS = 5
GROUP = QUERY_HEADS // KEY_VALUE_HEADS
HEAD_SIZE = 64
D = QUERY_HEADS * HEAD_SIZE
KEYW = KEY_VALUE_HEADS * HEAD_SIZE
DI = 3200
DS = 16
DTR = 100
CONV = 4
WINDOW = 1024
PAGE = 128

T = 128
ROWS = 144
TAIL = ROWS - T
LANES = 640
BLOCKS = DI // LANES
HEADS = 32
SIDE = 4

EPSILON = 1e-06
MASKED = -1e30
LOG2E = math.log2(math.e)
F32 = jnp.float32
BF16 = jnp.bfloat16
NT = (((1,), (1,)), ((), ()))
NN = (((1,), (0,)), ((), ()))
TN = (((0,), (0,)), ((), ()))

VMEM = pl.BlockSpec(memory_space=pltpu.VMEM)
SMEM = pl.BlockSpec(memory_space=pltpu.SMEM)
ANY = pl.BlockSpec(memory_space=pl.ANY)


def dot(a, b, dims):
    return lax.dot_general(a, b, dims, preferred_element_type=F32)


def params(mib):
    return pltpu.CompilerParams(vmem_limit_bytes=mib * 2**20)


def cost(flops, bytes_accessed):
    return pl.CostEstimate(flops=flops, bytes_accessed=bytes_accessed, transcendentals=0)


def lanes_of(block, start=0):
    return pl.ds(pl.multiple_of(start + block * LANES, 128), LANES)


def silu(v):
    return v * lax.logistic(v)


def softplus(v):
    return jnp.maximum(v, 0.0) + jnp.log1p(jnp.exp(-jnp.abs(v)))


def wide(tile):
    return jnp.concatenate([tile] * (LANES // 128), axis=1)


def spread(columns, out_ref):
    for t in range(T):
        out_ref[t] = jnp.broadcast_to(columns[:, t : t + 1], (DS, 128))


def front_kernel(
    x_ref, rim_ref, last_ref, past_ref, taps_ref, vectors_ref, w_ref, w_dt_ref, rate_ref,
    *rest
):
    act_ref, step_ref, bc_ref, end_ref, padded, drive, b_wide, tail_ref = rest[-8:]
    requests = last_ref.shape[0]
    tail_ref[...] = jnp.zeros_like(tail_ref)
    def fill(k, _):
        cols = lanes_of(k)
        padded[0:8, cols] = rim_ref[:, cols].astype(F32)[8:16]
        padded[8 : 8 + T, cols] = x_ref[:, cols].astype(F32)
        recent = taps_ref[CONV - 1 : CONV, cols] * last_ref[:, cols].astype(F32)
        for i in range(requests):
            past = taps_ref[0 : CONV - 1, cols] * past_ref[i, :, cols].astype(F32)
            tail_ref[i : i + 1, cols] = jnp.sum(past, axis=0, keepdims=True) + recent[i : i + 1]
        return 0

    lax.fori_loop(0, BLOCKS, fill, 0)

    def conv(k, carry):
        proj, bc = carry
        cols = lanes_of(k)
        total = taps_ref[0:1, cols] * padded[5 : 5 + T, cols]
        for tap in range(1, CONV):
            total = total + taps_ref[tap : tap + 1, cols] * padded[5 + tap : 5 + tap + T, cols]
        total = jnp.concatenate([total, tail_ref[:, cols]], axis=0)
        act = silu(total + vectors_ref[0:1, cols])
        act_ref[:, cols] = act
        low = act.astype(BF16)
        return (
            proj + dot(low, w_ref[:, cols], NT),
            bc + dot(w_ref[DTR - DTR % 16 :, cols], low, NT),
        )

    proj, bc = lax.fori_loop(
        0, BLOCKS, conv, (jnp.zeros((ROWS, DTR + 2 * DS), F32), jnp.zeros((DTR % 16 + 2 * DS, ROWS), F32))
    )
    bc = bc[DTR % 16 :]
    bc_ref[...] = bc
    dt_low = proj[:, :DTR].astype(BF16)
    spread(bc[:DS], b_wide)

    def step(k, _):
        cols = lanes_of(k)
        size = softplus(dot(dt_low, w_dt_ref[:, cols], NN) + vectors_ref[1:2, cols])
        step_ref[:, cols] = size
        drive[:, cols] = size[:T] * act_ref[0:T, cols]
        return 0

    lax.fori_loop(0, BLOCKS, step, 0)

    def scan(k, _):
        cols = lanes_of(k)
        rate = rate_ref[:, cols] * -LOG2E

        def one(t, state):
            size = step_ref[pl.ds(t, 1), cols]
            push = drive[pl.ds(t, 1), cols]
            return jnp.exp2(rate * size) * state + wide(b_wide[t]) * push

        state = lax.fori_loop(0, T, one, jnp.zeros((DS, LANES), F32), unroll=8)
        total = jnp.sum(step_ref[0:T, cols], axis=0, keepdims=True)
        high = total.astype(BF16).astype(F32)
        row = lax.broadcasted_iota(jnp.int32, (DS, LANES), 0)
        sums = jnp.where(row == 0, high, jnp.where(row == 1, total - high, 0.0))
        end_ref[:, cols] = jnp.concatenate([state, sums], axis=0).astype(BF16)
        return 0

    lax.fori_loop(0, BLOCKS, scan, 0)


def front(operands, later):
    return pl.pallas_call(
        front_kernel,
        out_shape=(
            jax.ShapeDtypeStruct((ROWS, DI), F32),
            jax.ShapeDtypeStruct((ROWS, DI), F32),
            jax.ShapeDtypeStruct((2 * DS, ROWS), F32),
            jax.ShapeDtypeStruct((2 * DS, DI), BF16),
        ),
        in_specs=[VMEM] * len(operands) + [ANY] * len(later),
        out_specs=(VMEM,) * 4,
        scratch_shapes=[
            pltpu.VMEM((8 + T, DI), F32),
            pltpu.VMEM((T, DI), F32),
            pltpu.VMEM((T, DS, 128), F32),
            pltpu.VMEM((TAIL, DI), F32),
        ],
        compiler_params=params(40),
        cost_estimate=cost(10**9, 40 * 10**6),
        name="front",
    )(*operands, *later)


def chained(state, block, rate, valid):
    block = block.astype(F32)
    decay = jnp.exp2(rate * (block[DS : DS + 1] + block[DS + 1 : DS + 2]))
    return jnp.where(valid, decay * state + block[:DS], state)


def join_kernel(own_ref, one_ref, two_ref, three_ref, rate_ref, *rest):
    enter_ref, row_ref = rest[-2:]
    x = lax.axis_index("req") & 3
    line = lax.broadcasted_iota(jnp.int32, (DS, LANES), 0)

    def block(k, _):
        cols = lanes_of(k)
        rate = rate_ref[:, cols] * -LOG2E
        near = ((3, three_ref[:, cols]), (2, two_ref[:, cols]), (1, one_ref[:, cols]))
        state = jnp.zeros((DS, LANES), F32)
        before = jnp.zeros((DS, LANES), F32)
        for by, ends in near:
            state = chained(state, ends, rate, x >= by)
            before = jnp.where(x >= by, before + ends[DS:].astype(F32), before)
        enter_ref[:, cols] = jnp.concatenate([state, before], axis=0)
        own = own_ref[:, cols]
        state = chained(state, own, rate, True)
        sums = own[DS:].astype(F32)
        for by, ends in near:
            state = chained(state, ends, rate, x < by)
            sums = sums + ends[DS:].astype(F32)
        total = sums[0:1] + sums[1:2]
        high = total.astype(BF16).astype(F32)
        sums = jnp.where(line == 0, high, jnp.where(line == 1, total - high, 0.0))
        row_ref[:, cols] = jnp.concatenate([state, sums], axis=0).astype(BF16)
        return 0

    lax.fori_loop(0, BLOCKS, block, 0)


def join(own, others, rate, later):
    return pl.pallas_call(
        join_kernel,
        out_shape=(
            jax.ShapeDtypeStruct((2 * DS, DI), F32),
            jax.ShapeDtypeStruct((2 * DS, DI), BF16),
        ),
        in_specs=[VMEM] * 5 + [ANY] * len(later),
        out_specs=(VMEM, VMEM),
        compiler_params=params(16),
        cost_estimate=cost(10**7, 4 * 10**6),
        name="join",
    )(own, *others, rate, *later)


def scan_kernel(
    z_ref, act_ref, step_ref, bc_ref, rate_ref, enter_ref, one_ref, two_ref, three_ref,
    vectors_ref, *rest
):
    out_ref, drive, b_wide, c_wide, parts, y_ref = rest[-6:]
    place = lax.axis_index("req") >> 2
    bc = bc_ref[...]
    spread(bc[:DS], b_wide)
    spread(bc[DS:], c_wide)
    row = lax.broadcasted_iota(jnp.int32, (T, 8 * T), 0)
    col = lax.broadcasted_iota(jnp.int32, (T, 8 * T), 1)
    pick = jnp.where(col // 8 == row, 1.0, 0.0).astype(BF16)

    def block(k, squares):
        cols = lanes_of(k)
        rate = rate_ref[:, cols] * -LOG2E
        drive[...] = step_ref[0:T, cols] * act_ref[0:T, cols]

        def one(pair, state):
            halves = []
            for t in (2 * pair, 2 * pair + 1):
                size = step_ref[pl.ds(t, 1), cols]
                push = drive[pl.ds(t, 1), :]
                state = jnp.exp2(rate * size) * state + wide(b_wide[t]) * push
                seen = state * wide(c_wide[t])
                halves.append(seen[0:8] + seen[8:16])
            at = pl.multiple_of(16 * pair, 16)
            parts[pl.ds(at, 16), :] = jnp.concatenate(halves, axis=0).astype(BF16)
            return state

        state = jnp.zeros((DS, LANES), F32)
        for by, ends in ((3, three_ref), (2, two_ref), (1, one_ref)):
            state = chained(state, ends[:, cols], rate, place >= by)
        state = chained(state, enter_ref[:, cols], rate, True)
        lax.fori_loop(0, T // 2, one, state, unroll=4)
        y = dot(pick, parts[...], NN) + vectors_ref[2:3, cols] * act_ref[0:T, cols]
        y = y * silu(z_ref[:, lanes_of(k, DI)].astype(F32))
        y_ref[:, cols] = y
        return squares + jnp.sum(y * y, axis=1, keepdims=True)

    squares = lax.fori_loop(0, BLOCKS, block, jnp.zeros((T, 1), F32))
    scale = lax.rsqrt(squares * (1.0 / DI) + EPSILON)

    def norm(k, _):
        cols = lanes_of(k)
        out_ref[:, cols] = (y_ref[:, cols] * scale * vectors_ref[3:4, cols]).astype(BF16)
        return 0

    lax.fori_loop(0, BLOCKS, norm, 0)


def scan(xz, act, step, bc, rate, enter, rows, vectors, later):
    return pl.pallas_call(
        scan_kernel,
        out_shape=jax.ShapeDtypeStruct((T, DI), BF16),
        in_specs=[VMEM] * 10 + [ANY] * len(later),
        out_specs=VMEM,
        scratch_shapes=[
            pltpu.VMEM((T, LANES), F32),
            pltpu.VMEM((T, DS, 128), F32),
            pltpu.VMEM((T, DS, 128), F32),
            pltpu.VMEM((8 * T, LANES), BF16),
            pltpu.VMEM((T, DI), F32),
        ],
        compiler_params=params(40),
        cost_estimate=cost(10**9, 45 * 10**6),
        name="scan",
    )(xz, act, step, bc, rate, enter, *rows, vectors, *later)


def attend_kernel(q_ref, kv_ref, gain_ref, *rest):
    out_ref, scores, mixed = rest[-3:]
    r = lax.axis_index("req")
    wide_rows = GROUP * T
    back = WINDOW // T
    key = lax.broadcasted_iota(jnp.int32, (T, wide_rows), 0)
    query = lax.broadcasted_iota(jnp.int32, (T, wide_rows), 1) % T
    for h in range(KEY_VALUE_HEADS):
        first = h * GROUP * HEAD_SIZE
        q = jnp.concatenate(
            [q_ref[first + g * HEAD_SIZE : first + (g + 1) * HEAD_SIZE, :] for g in range(GROUP)],
            axis=1,
        )
        q = (q.astype(F32) * (1.0 / math.sqrt(HEAD_SIZE))).astype(BF16)
        none = jnp.zeros_like(q)
        q = jnp.concatenate([q, none] if h % 2 == 0 else [none, q], axis=0)
        key_cols = slice(128 * (h // 2), 128 * (h // 2) + 128)
        at = KEYW + h * HEAD_SIZE
        value_cols = slice(at // 128 * 128, at // 128 * 128 + 128)
        value_row = at % 128
        top = jnp.full((1, wide_rows), MASKED, F32)
        for j in range(back + 1):
            rows = pl.ds(pl.multiple_of(jnp.maximum(r - back + j, 0) * T, T), T)
            s = dot(kv_ref[rows, key_cols], q, NN)
            if j == back:
                s = jnp.where(key <= query, s, MASKED)
            elif j == 0:
                s = jnp.where(jnp.logical_and(key > query, r >= back), s, MASKED)
            else:
                s = jnp.where(r - back + j >= 0, s, MASKED)
            scores[j] = s
            top = jnp.maximum(top, jnp.max(s, axis=0, keepdims=True))
        total = jnp.zeros((1, wide_rows), F32)
        sums = jnp.zeros((128, wide_rows), F32)
        for j in range(back + 1):
            rows = pl.ds(pl.multiple_of(jnp.maximum(r - back + j, 0) * T, T), T)
            weight = jnp.exp(scores[j] - top)
            total = total + jnp.sum(weight, axis=0, keepdims=True)
            sums = sums + dot(kv_ref[rows, value_cols], weight.astype(BF16), TN)
        part = sums[value_row : value_row + HEAD_SIZE] / total
        for g in range(GROUP):
            mixed[first + g * HEAD_SIZE : first + (g + 1) * HEAD_SIZE, :] = part[
                :, g * T : (g + 1) * T
            ]
    values = mixed[...]
    scale = lax.rsqrt(jnp.mean(values * values, axis=0, keepdims=True) + EPSILON)
    out_ref[...] = (jnp.transpose(values * scale) * gain_ref[...]).astype(BF16)


def attend(q, kv, gain, later):
    return pl.pallas_call(
        attend_kernel,
        out_shape=jax.ShapeDtypeStruct((T, D), BF16),
        in_specs=[VMEM, VMEM, VMEM] + [ANY] * len(later),
        out_specs=VMEM,
        scratch_shapes=[
            pltpu.VMEM((WINDOW // T + 1, T, GROUP * T), F32),
            pltpu.VMEM((D, T), F32),
        ],
        compiler_params=params(40),
        cost_estimate=cost(10**9, 30 * 10**6),
        name="attend",
    )(q, kv, gain, *later)


def tables_kernel(owner_ref, slot_ref, len_ref, out_ref):
    me = lax.axis_index("req")
    entries, devices = owner_ref.shape
    window_pages = entries // len_ref.shape[0]
    most = 64 // devices
    owner_line = lax.broadcasted_iota(jnp.int32, (devices, devices), 0)
    rank_line = lax.broadcasted_iota(jnp.int32, (8, devices), 0)
    lane = lax.broadcasted_iota(jnp.int32, (1, devices), 1)
    wide_lane = lax.broadcasted_iota(jnp.int32, (1, 128), 1)
    seen = jnp.zeros((devices, devices), F32)
    sent = jnp.zeros((8, devices), jnp.int32)
    got = jnp.zeros((1, 128), jnp.int32)
    for e in range(entries):
        request, page = divmod(e, window_pages)
        length = len_ref[request : request + 1, :]
        first = jnp.maximum(length - (WINDOW - 1), 0) >> 7
        used = (first + page) * PAGE < length
        owner = owner_ref[e : e + 1, :]
        hit = jnp.logical_and(owner_line == owner, used)
        rank = jnp.sum(jnp.where(hit, seen, 0.0), axis=0, keepdims=True).astype(jnp.int32)
        seen = jnp.where(hit, seen + 1.0, seen)
        code = slot_ref[e : e + 1, :] + (page * 64 + request * 1024 + 8192)
        here = jnp.logical_and(owner == me, used)
        sent = jnp.where(jnp.logical_and(rank_line == rank, here), code, sent)
        code = owner * most + rank + (request * 64 + 512)
        code = jnp.where(jnp.logical_and(lane == me, used), code, 0).astype(F32)
        code = jnp.sum(code, axis=1, keepdims=True).astype(jnp.int32)
        got = jnp.where(wide_lane == e, code, got)
    out_ref[...] = jnp.zeros_like(out_ref)
    out_ref[0:8, 0:devices] = sent
    out_ref[8:9, :] = got


def tables(owners, slots, lengths):
    return pl.pallas_call(
        tables_kernel,
        out_shape=jax.ShapeDtypeStruct((16, 128), jnp.int32),
        in_specs=[VMEM] * 3,
        out_specs=VMEM,
        compiler_params=params(8),
        cost_estimate=cost(10**6, 4 * 10**6),
        name="tables",
    )(owners, slots, lengths)


def pages_kernel(table_ref, len_ref, pool_ref, *rest):
    out_ref, pages, queries, chosen, sems = rest[-5:]
    me = lax.axis_index("req")
    most = 64 // len_ref.shape[1]
    requests = len_ref.shape[0]

    def code_of(n):
        return table_ref[n & (most - 1), n // most]

    def fetch(n):
        slot = code_of(n) & 63
        return pltpu.make_async_copy(pool_ref.at[slot], pages.at[n], sems.at[n])

    def choose(n, count):
        valid = code_of(n) >> 13
        chosen[count] = n

        @pl.when(valid == 1)
        def _():
            fetch(n).start()

        return count + valid

    count = lax.fori_loop(0, 64, choose, 0)
    held = rest[0].shape[0]
    for k in range(SIDE):
        queries[k * held : (k + 1) * held, :] = rest[k][...]
    head = lax.broadcasted_iota(jnp.int32, (HEADS, 128), 0)
    lane = lax.broadcasted_iota(jnp.int32, (HEADS, 128), 1)
    block_of = head // (2 * GROUP)
    kv_head = head // GROUP

    def share(n):
        code = code_of(n)
        device = n // most
        page_index = (code >> 6) & 15
        request = (code >> 10) & 7
        away = ((me >> 2) - (device >> 2)) & 3
        across = (me - device) & 3
        at = (away * SIDE + across) * requests + request
        length = len_ref[request, device]
        first = jnp.maximum(length - (WINDOW - 1), 0) // PAGE
        base = (first + page_index) * PAGE
        q = queries[pl.ds(pl.multiple_of(at * HEADS, HEADS), HEADS), :].astype(F32)
        q = jnp.concatenate([jnp.where(block_of == b, q, 0.0) for b in range(3)], axis=1)
        q = (q * (1.0 / math.sqrt(HEAD_SIZE))).astype(BF16)
        s = dot(q, pages[n, :, 0:384], NT)
        position = base + lane
        seen = jnp.logical_and(position > length - WINDOW, position < length)
        s = jnp.where(seen, s, MASKED)
        top = jnp.max(s, axis=1, keepdims=True)
        weight = jnp.where(seen, jnp.exp(s - top), 0.0)
        total = jnp.sum(weight, axis=1, keepdims=True)
        sums = dot(weight.astype(BF16), pages[n, :, 256:640], NN)
        picked = jnp.where(
            kv_head == 0,
            sums[:, 0:128],
            jnp.where(kv_head <= 2, sums[:, 128:256], sums[:, 256:384]),
        )
        picked = jnp.where(kv_head % 2 == 0, pltpu.roll(picked, 64, 1), picked)
        level = top + jnp.log(total)
        high = level.astype(BF16).astype(F32)
        middle = (level - high).astype(BF16).astype(F32)
        low = level - high - middle
        tile = jnp.where(
            lane < HEAD_SIZE,
            picked / total,
            jnp.where(
                lane == HEAD_SIZE,
                high,
                jnp.where(lane == HEAD_SIZE + 1, middle, jnp.where(lane == HEAD_SIZE + 2, low, 0.0)),
            ),
        )
        return pl.ds(pl.multiple_of(n * HEADS, HEADS), HEADS), tile.astype(BF16)

    def pair(half, _):
        one = chosen[2 * half]
        two = chosen[jnp.minimum(2 * half + 1, count - 1)]
        fetch(one).wait()

        @pl.when(2 * half + 1 < count)
        def _():
            fetch(two).wait()

        both = [share(one), share(two)]
        for rows, tile in both:
            out_ref[rows, :] = tile
        return 0

    lax.fori_loop(0, (count + 1) // 2, pair, 0)


def page_shares(table, lengths, pool, queries, rows, later):
    return pl.pallas_call(
        pages_kernel,
        out_shape=jax.ShapeDtypeStruct((rows * HEADS, 128), BF16),
        in_specs=[SMEM, SMEM, ANY] + [VMEM] * len(queries) + [ANY] * len(later),
        out_specs=VMEM,
        scratch_shapes=[
            pltpu.VMEM((rows, PAGE, 2 * KEYW), BF16),
            pltpu.VMEM((SIDE * queries[0].shape[0], 128), BF16),
            pltpu.SMEM((rows,), jnp.int32),
            pltpu.SemaphoreType.DMA((rows,)),
        ],
        compiler_params=params(32),
        cost_estimate=cost(10**8, 40 * 10**6),
        name="page_shares",
    )(table, lengths, pool, *queries, *later)


def gather_kernel(
    table_ref, shares_ref, score_ref, value_ref, gain_a_ref, *rest
):
    attn_ref, tops, totals, sums, levels, chosen = rest[-6:]
    requests = score_ref.shape[0]

    def choose(n, count):
        code = table_ref[8, n]
        chosen[count] = code & 511
        return count + (code >> 9)

    count = lax.fori_loop(0, 64, choose, 0)
    tops[...] = score_ref[...]

    def tile_of(row):
        return pl.ds(pl.multiple_of(row * HEADS, HEADS), HEADS)

    def level(row, _):
        share = shares_ref[tile_of(row), :].astype(F32)
        level = share[:, 64:65] + share[:, 65:66] + share[:, 66:67]
        levels[tile_of(row), :] = jnp.broadcast_to(level, (HEADS, 128))
        return 0

    lax.fori_loop(0, shares_ref.shape[0] // HEADS, level, 0, unroll=4)

    def highest(n, _):
        request = chosen[n] >> 6
        tops[request] = jnp.maximum(tops[request], levels[tile_of(chosen[n] & 63), :])
        return 0

    lax.fori_loop(0, count, highest, 0)
    own = jnp.exp(score_ref[...] - tops[...])
    totals[...] = own
    sums[...] = own * value_ref[...]

    def add(n, _):
        request = chosen[n] >> 6
        tile = tile_of(chosen[n] & 63)
        share = shares_ref[tile, :].astype(F32)
        weight = jnp.exp(levels[tile, :] - tops[request])
        totals[request] = totals[request] + weight
        sums[request] = sums[request] + weight * share
        return 0

    lax.fori_loop(0, count, add, 0)
    head = lax.broadcasted_iota(jnp.int32, (HEADS, 128), 0)
    lane = lax.broadcasted_iota(jnp.int32, (HEADS, 128), 1)
    real = jnp.logical_and(head < QUERY_HEADS, lane < HEAD_SIZE)
    for i in range(requests):
        value = jnp.where(real, sums[i] / totals[i], 0.0)
        square = jnp.sum(jnp.sum(value * value, axis=1, keepdims=True), axis=0, keepdims=True)
        scale = lax.rsqrt(square * (1.0 / D) + EPSILON)
        attn_ref[i] = (value * scale * gain_a_ref[...]).astype(BF16)


def gather(table, operands, later):
    requests = operands[1].shape[0]
    tiles = (requests, HEADS, 128)
    return pl.pallas_call(
        gather_kernel,
        out_shape=jax.ShapeDtypeStruct(tiles, BF16),
        in_specs=[SMEM] + [VMEM] * len(operands) + [ANY] * len(later),
        out_specs=VMEM,
        scratch_shapes=[pltpu.VMEM(tiles, F32)] * 3 + [pltpu.VMEM(operands[0].shape, F32)]
        + [pltpu.SMEM((64,), jnp.int32)],
        compiler_params=params(16),
        cost_estimate=cost(10**7, 10 * 10**6),
        name="gather",
    )(table, *operands, *later)


def decode_kernel(
    act_ref, step_ref, bc_ref, state_ref, rate_ref, vectors_ref, last_ref, *rest
):
    y_out_ref, y_ref, z_ref = rest[-3:]
    requests = state_ref.shape[0]
    bc = bc_ref[...]
    y_ref[...] = jnp.zeros_like(y_ref)
    z_ref[...] = jnp.zeros_like(z_ref)
    z_ref[0:requests, :] = last_ref[:, DI:].astype(F32)

    def block(k, squares):
        cols = lanes_of(k)
        rate = rate_ref[:, cols] * -LOG2E
        for i in range(requests):
            size = step_ref[T + i : T + i + 1, cols]
            act = act_ref[T + i : T + i + 1, cols]
            b = bc[:DS, T + i : T + i + 1]
            c = bc[DS:, T + i : T + i + 1]
            state = jnp.exp2(rate * size) * state_ref[i, :, cols] + b * (size * act)
            y_ref[i : i + 1, cols] = jnp.sum(state * c, axis=0, keepdims=True)
        y = y_ref[:, cols] + vectors_ref[2:3, cols] * act_ref[T:ROWS, cols]
        y = y * silu(z_ref[:, cols])
        y_ref[:, cols] = y
        return squares + jnp.sum(y * y, axis=1, keepdims=True)

    squares = lax.fori_loop(0, BLOCKS, block, jnp.zeros((TAIL, 1), F32))
    scale = lax.rsqrt(squares * (1.0 / DI) + EPSILON)

    def norm(k, _):
        cols = lanes_of(k)
        y_out_ref[:, cols] = (y_ref[:, cols] * scale * vectors_ref[3:4, cols]).astype(BF16)
        return 0

    lax.fori_loop(0, BLOCKS, norm, 0)


def decode(operands, after):
    return pl.pallas_call(
        decode_kernel,
        out_shape=jax.ShapeDtypeStruct((TAIL, DI), BF16),
        in_specs=[VMEM] * len(operands) + [ANY] * len(after),
        out_specs=VMEM,
        scratch_shapes=[pltpu.VMEM((TAIL, DI), F32)] * 2,
        compiler_params=params(24),
        cost_estimate=cost(10**8, 16 * 10**6),
        name="decode",
    )(*operands, *after)


def project_kernel(
    place_ref, attn_ref, attn_tail_ref, y_ref, y_tail_ref, resid_ref, gain_ref, *rest
):
    shards = place_ref.shape[0]
    weights = rest[:shards]
    after_ref, normed_ref, mix = rest[shards:]
    width = mix.shape[2]
    for m in range(shards):
        low, high = m * width, (m + 1) * width
        for rows, attn, y in (
            (slice(0, T), attn_ref, y_ref),
            (slice(T, ROWS), attn_tail_ref, y_tail_ref),
        ):
            pieces = []
            if low < D:
                pieces.append(attn[:, low : min(high, D)].astype(F32))
            if high > D:
                pieces.append(y[:, max(low, D) - D : high - D].astype(F32))
            piece = pieces[0] if len(pieces) == 1 else jnp.concatenate(pieces, axis=1)
            mix[m, rows, :] = piece.astype(BF16)
    after_ref[...] = resid_ref[...].astype(F32)
    for s in range(shards):
        after_ref[...] += dot(mix[place_ref[s]], weights[s][...], NN)
    after = after_ref[...]
    scale = lax.rsqrt(jnp.mean(after * after, axis=1, keepdims=True) + EPSILON)
    normed_ref[...] = (after * scale * gain_ref[...]).astype(BF16)


def project(places, attn, attn_tail, y, y_tail, resid, gain, weights):
    width = weights[0].shape[0]
    return pl.pallas_call(
        project_kernel,
        out_shape=(
            jax.ShapeDtypeStruct((ROWS, D), F32),
            jax.ShapeDtypeStruct((ROWS, D), BF16),
        ),
        in_specs=[SMEM] + [VMEM] * (6 + len(weights)),
        out_specs=(VMEM, VMEM),
        scratch_shapes=[pltpu.VMEM((len(weights), ROWS, width), BF16)],
        compiler_params=params(48),
        cost_estimate=cost(2 * 10**9, 30 * 10**6),
        name="project",
    )(places, attn, attn_tail, y, y_tail, resid, gain, *weights)


def mlp_kernel(count, extra, *refs):
    refs = refs[: count + 6] + refs[count + 6 + extra :]
    rows = refs[:count]
    sources = refs[count : count + 6]
    outs = refs[count + 6 : 2 * count + 6]
    buffers = refs[2 * count + 6 : 2 * count + 12]
    sems = refs[2 * count + 12]
    copies = [
        pltpu.make_async_copy(sources[i], buffers[i], sems.at[i]) for i in range(6)
    ]
    for copy in copies:
        copy.start()
    totals = [None] * count
    for s in range(2):
        for i in range(3):
            copies[3 * s + i].wait()
        gate_w, up_w, down_w = buffers[3 * s : 3 * s + 3]
        for n in range(count):
            value = rows[n][...]
            hidden = silu(dot(value, gate_w[...], NT)) * dot(value, up_w[...], NT)
            part = dot(hidden.astype(BF16), down_w[...], NN)
            if s == 0:
                refs[2 * count + 13 + n][...] = part
            else:
                outs[n][...] = (refs[2 * count + 13 + n][...] + part).astype(outs[n].dtype)


def mlp(rows, weights, kind, after=()):
    count = len(rows)
    return pl.pallas_call(
        functools.partial(mlp_kernel, count, len(after)),
        out_shape=tuple(jax.ShapeDtypeStruct((ROWS, D), kind) for _ in rows),
        in_specs=[VMEM] * count + [ANY] * (6 + len(after)),
        out_specs=(VMEM,) * count,
        scratch_shapes=[pltpu.VMEM(w.shape, BF16) for w in weights]
        + [pltpu.SemaphoreType.DMA((6,))]
        + [pltpu.VMEM((ROWS, D), F32) for _ in rows],
        compiler_params=params(48),
        cost_estimate=cost(2 * 10**9 * count, 15 * 10**6),
        name="mlp",
    )(*rows, *weights, *after)


def after(a, *others):
    return lax.optimization_barrier((a, *others))[0]


def padded_to(a, axis, size):
    pads = [(0, 0)] * a.ndim
    pads[axis] = (0, size - a.shape[axis])
    return jnp.pad(a, pads)


def shards(
    decode_query,
    decode_key_value,
    dec_xz,
    dec_resid,
    dec_conv,
    dec_state,
    dec_len,
    page_owner,
    page_slot,
    kv_pool,
    pre_q,
    pre_kv,
    pre_xz,
    pre_resid,
    w_xproj,
    w_dt,
    dt_bias,
    a_rate,
    conv_w,
    conv_b,
    d_skip,
    g_attn,
    g_ssm,
    w_out,
    g_mlp,
    w_gate,
    w_up,
    w_down,
):
    req_count = lax.axis_size("req")
    mlp_count = lax.axis_size("mlp")
    my_mlp = lax.axis_index("mlp")
    my_z, my_core = my_mlp >> 1, my_mlp & 1
    requests = decode_query.shape[0]
    row = lambda a: a[None, :]

    def along_x(a, by):
        pairs = [(r, r // SIDE * SIDE + (r + by) % SIDE) for r in range(req_count)]
        return lax.ppermute(a, "req", pairs)

    def along_y(a, by):
        pairs = [(r, (r // SIDE + by) % SIDE * SIDE + r % SIDE) for r in range(req_count)]
        return lax.ppermute(a, "req", pairs)

    def along_z(a, by):
        pairs = [
            (m, (m // 2 + (by if m % 2 == 0 else -by)) % SIDE * 2 + m % 2) for m in range(mlp_count)
        ]
        return lax.ppermute(a, "mlp", pairs)

    def across(a):
        return lax.ppermute(a, "mlp", [(m, m ^ 1) for m in range(mlp_count)])

    xz = pre_xz[0]
    rim = lax.ppermute(
        xz[T - 16 :, :DI], "req", [(r, r + 1) for r in range(req_count - 1)]
    )

    by_entry = lambda a: jnp.transpose(a[:, 0], (1, 2, 0)).reshape(-1, req_count)
    lengths = jnp.transpose(dec_len[:, 0])
    table = tables(by_entry(page_owner), by_entry(page_slot), lengths)

    heads = decode_query.reshape(requests, QUERY_HEADS, HEAD_SIZE)
    upper = (jnp.arange(QUERY_HEADS) // GROUP % 2 == 1)[None, :, None]
    none = jnp.zeros_like(heads)
    halves = jnp.concatenate([jnp.where(upper, none, heads), jnp.where(upper, heads, none)], axis=2)
    halves = padded_to(halves, 1, HEADS).reshape(requests * HEADS, 128)
    in_row = jnp.concatenate([halves] + [along_x(halves, by) for by in range(1, SIDE)], axis=0)
    queries = [in_row] + [along_y(in_row, by) for by in range(1, SIDE)]
    span_kv = lax.all_gather(pre_kv[0], "req", axis=0, tiled=True)

    up_one = along_z(w_out, 1)
    down_one = along_z(w_out, -1)

    rate = jnp.swapaxes(a_rate, 0, 1)
    w_x = jnp.swapaxes(w_xproj, 0, 1)
    vectors = jnp.concatenate([conv_b, dt_bias, d_skip, g_ssm]).reshape(4, DI)
    act, step, bc, ends = front(
        [xz, rim, dec_xz, dec_conv, conv_w, vectors, w_x, w_dt, rate], []
    )

    shares = page_shares(table, lengths, kv_pool, queries, 64, [bc])

    row_enter, row_ends = join(
        ends, [along_x(ends, by) for by in range(1, SIDE)], rate, [shares]
    )
    other_rows = [along_y(row_ends, by) for by in range(1, SIDE)]

    shares = lax.all_to_all(after(shares, row_ends), "req", split_axis=0, concat_axis=0, tiled=True)
    by_head = lambda a: jnp.repeat(a.reshape(requests, KEY_VALUE_HEADS, HEAD_SIZE), GROUP, axis=1)
    own_key = by_head(decode_key_value[:, :KEYW]).astype(F32)
    own_value = by_head(decode_key_value[:, KEYW:]).astype(F32)
    own_score = jnp.sum(heads.astype(F32) * own_key, axis=2, keepdims=True) / math.sqrt(HEAD_SIZE)
    tile = lambda a: padded_to(padded_to(a, 1, HEADS), 2, 128)
    own_score = padded_to(jnp.broadcast_to(own_score, (requests, QUERY_HEADS, 128)), 1, HEADS)
    gain_a = tile(g_attn.reshape(1, QUERY_HEADS, HEAD_SIZE))[0]
    dec_y = decode(
        [
            act, step, bc, jnp.swapaxes(dec_state, 1, 2), rate, vectors, dec_xz
        ],
        [row_ends],
    )
    dec_attn = gather(
        table, [shares, own_score, tile(own_value), gain_a], [up_one, down_one, *other_rows]
    )
    pre_y = scan(
        xz, act, step, bc, rate, row_enter, other_rows, vectors, [dec_y, dec_attn]
    )
    dec_attn = padded_to(dec_attn[:, :QUERY_HEADS, :HEAD_SIZE].reshape(requests, D), 0, TAIL)
    pre_attn = attend(jnp.swapaxes(pre_q[0], 0, 1), span_kv, row(g_attn), [pre_y])

    up_two = along_z(after(up_one, dec_attn), 1)
    held = [w_out, up_one, down_one, up_two]
    out_weights = held + [across(after(a, dec_attn)) for a in held[:3]] + [across(after(up_two, pre_attn))]
    sign = 1 - 2 * my_core
    offsets = jnp.array([0, -1, 1, -2], jnp.int32)
    mine = ((my_z + sign * offsets) & (SIDE - 1)) * 2 + my_core
    other = ((my_z - sign * offsets) & (SIDE - 1)) * 2 + 1 - my_core
    places = jnp.concatenate([mine, other]).astype(jnp.int32)
    gate_t, up_t = jnp.swapaxes(w_gate, 0, 1), jnp.swapaxes(w_up, 0, 1)
    mlp_weights = [gate_t, up_t, w_down]
    mlp_weights = mlp_weights + [across(after(a, pre_y)) for a in mlp_weights]

    resid = jnp.concatenate([pre_resid[0], padded_to(dec_resid, 0, TAIL)], axis=0)
    after_mix, normed = project(
        places, pre_attn, dec_attn, pre_y, dec_y, resid, row(g_mlp), out_weights
    )

    one_up = along_z(normed, 1)
    one_down = along_z(normed, -1)
    (sum_own,) = mlp([normed], mlp_weights, F32)
    two_up = along_z(after(one_up, sum_own), 1)
    (sum_down,) = mlp([one_down], mlp_weights, BF16, [sum_own])
    (sum_two,) = mlp([two_up], mlp_weights, BF16, [sum_down])
    (sum_up,) = mlp([one_up], mlp_weights, BF16, [sum_two])
    back_two = along_z(sum_two, -1)
    back_down = along_z(sum_down, 1)
    back_up = along_z((sum_up.astype(F32) + back_two.astype(F32)).astype(BF16), -1)
    final_rows = (
        after_mix + sum_own + back_down.astype(F32) + back_up.astype(F32)
    ).astype(BF16)
    return (final_rows[T : T + requests], final_rows[:T][None])


def solution(mesh):
    both = ("req", "mlp")
    in_specs = (
        P(both, None),
        P(both, None),
        P(both, None),
        P(both, None),
        P(both, None, None),
        P(both, None, None),
        P(None, "mlp", None),
        P(None, "mlp", None, None),
        P(None, "mlp", None, None),
        P(both, None, None),
        P("mlp", "req", None),
        P("mlp", "req", None),
        P("mlp", "req", None),
        P("mlp", "req", None),
        P(),
        P(),
        P(),
        P(),
        P(),
        P(),
        P(),
        P(),
        P(),
        P("mlp", None),
        P(),
        P(None, "mlp"),
        P(None, "mlp"),
        P("mlp", None),
    )
    out_specs = (P(both, None), P("mlp", "req", None))
    return jax.shard_map(shards, mesh=mesh, in_specs=in_specs, out_specs=out_specs, check_vma=False)
```

```python
import functools
import math

import jax
import jax.numpy as jnp
from jax import lax
from jax.experimental import pallas as pl
from jax.experimental.pallas import tpu as pltpu
from jax.sharding import PartitionSpec as P

QUERY_HEADS = 25
KEY_VALUE_HEADS = 5
GROUP = QUERY_HEADS // KEY_VALUE_HEADS
HEAD_SIZE = 64
D = QUERY_HEADS * HEAD_SIZE
KEYW = KEY_VALUE_HEADS * HEAD_SIZE
DI = 3200
DS = 16
DTR = 100
CONV = 4
WINDOW = 1024
PAGE = 128

T = 128
ROWS = 144
TAIL = ROWS - T
LANES = 640
BLOCKS = DI // LANES
HEADS = 32
SIDE = 4

EPSILON = 1e-06
MASKED = -1e30
LOG2E = math.log2(math.e)
F32 = jnp.float32
BF16 = jnp.bfloat16
NT = (((1,), (1,)), ((), ()))
NN = (((1,), (0,)), ((), ()))
TN = (((0,), (0,)), ((), ()))

VMEM = pl.BlockSpec(memory_space=pltpu.VMEM)
SMEM = pl.BlockSpec(memory_space=pltpu.SMEM)
ANY = pl.BlockSpec(memory_space=pl.ANY)


def dot(a, b, dims):
    return lax.dot_general(a, b, dims, preferred_element_type=F32)


def params(mib=58):
    return pltpu.CompilerParams(vmem_limit_bytes=mib * 2**20)


def cost(flops, bytes_accessed):
    return pl.CostEstimate(flops=flops, bytes_accessed=bytes_accessed, transcendentals=0)


def lanes_of(block, start=0):
    return pl.ds(pl.multiple_of(start + block * LANES, 128), LANES)


def silu(v):
    return v * lax.logistic(v)


def softplus(v):
    return jnp.maximum(v, 0.0) + jnp.log1p(jnp.exp(-jnp.abs(v)))


def wide(tile):
    return jnp.concatenate([tile] * (LANES // 128), axis=1)


def spread(columns, out_ref):
    for t in range(T):
        out_ref[t] = jnp.broadcast_to(columns[:, t : t + 1], (DS, 128))


def front_kernel(
    x_ref, rim_ref, last_ref, past_ref, taps_ref, vectors_ref, w_ref, w_dt_ref, rate_ref,
    *rest
):
    act_ref, step_ref, bc_ref, end_ref, padded, drive, b_wide, tail_ref = rest[-8:]
    requests = last_ref.shape[0]
    tail_ref[...] = jnp.zeros_like(tail_ref)
    def fill(k, _):
        cols = lanes_of(k)
        padded[0:8, cols] = rim_ref[:, cols].astype(F32)[8:16]
        padded[8 : 8 + T, cols] = x_ref[:, cols].astype(F32)
        recent = taps_ref[CONV - 1 : CONV, cols] * last_ref[:, cols].astype(F32)
        for i in range(requests):
            past = taps_ref[0 : CONV - 1, cols] * past_ref[i, :, cols].astype(F32)
            tail_ref[i : i + 1, cols] = jnp.sum(past, axis=0, keepdims=True) + recent[i : i + 1]
        return 0

    lax.fori_loop(0, BLOCKS, fill, 0)

    def conv(k, carry):
        proj, bc = carry
        cols = lanes_of(k)
        total = taps_ref[0:1, cols] * padded[5 : 5 + T, cols]
        for tap in range(1, CONV):
            total = total + taps_ref[tap : tap + 1, cols] * padded[5 + tap : 5 + tap + T, cols]
        total = jnp.concatenate([total, tail_ref[:, cols]], axis=0)
        act = silu(total + vectors_ref[0:1, cols])
        act_ref[:, cols] = act
        low = act.astype(BF16)
        return (
            proj + dot(low, w_ref[:, cols], NT),
            bc + dot(w_ref[DTR - DTR % 16 :, cols], low, NT),
        )

    proj, bc = lax.fori_loop(
        0, BLOCKS, conv, (jnp.zeros((ROWS, DTR + 2 * DS), F32), jnp.zeros((DTR % 16 + 2 * DS, ROWS), F32))
    )
    bc = bc[DTR % 16 :]
    bc_ref[...] = bc
    dt_low = proj[:, :DTR].astype(BF16)
    spread(bc[:DS], b_wide)

    def step(k, _):
        cols = lanes_of(k)
        size = softplus(dot(dt_low, w_dt_ref[:, cols], NN) + vectors_ref[1:2, cols])
        step_ref[:, cols] = size
        drive[:, cols] = size[:T] * act_ref[0:T, cols]
        return 0

    lax.fori_loop(0, BLOCKS, step, 0)

    def scan(k, _):
        cols = lanes_of(k)
        rate = rate_ref[:, cols] * -LOG2E

        def one(t, state):
            size = step_ref[pl.ds(t, 1), cols]
            push = drive[pl.ds(t, 1), cols]
            return jnp.exp2(rate * size) * state + wide(b_wide[t]) * push

        state = lax.fori_loop(0, T, one, jnp.zeros((DS, LANES), F32), unroll=8)
        total = jnp.sum(step_ref[0:T, cols], axis=0, keepdims=True)
        high = total.astype(BF16).astype(F32)
        row = lax.broadcasted_iota(jnp.int32, (DS, LANES), 0)
        sums = jnp.where(row == 0, high, jnp.where(row == 1, total - high, 0.0))
        end_ref[:, cols] = jnp.concatenate([state, sums], axis=0).astype(BF16)
        return 0

    lax.fori_loop(0, BLOCKS, scan, 0)


def front(operands, later):
    return pl.pallas_call(
        front_kernel,
        out_shape=(
            jax.ShapeDtypeStruct((ROWS, DI), F32),
            jax.ShapeDtypeStruct((ROWS, DI), F32),
            jax.ShapeDtypeStruct((2 * DS, ROWS), F32),
            jax.ShapeDtypeStruct((2 * DS, DI), BF16),
        ),
        in_specs=[VMEM] * len(operands) + [ANY] * len(later),
        out_specs=(VMEM,) * 4,
        scratch_shapes=[
            pltpu.VMEM((8 + T, DI), F32),
            pltpu.VMEM((T, DI), F32),
            pltpu.VMEM((T, DS, 128), F32),
            pltpu.VMEM((TAIL, DI), F32),
        ],
        compiler_params=params(),
        cost_estimate=cost(10**9, 40 * 10**6),
        name="front",
    )(*operands, *later)


def chained(state, block, rate, valid):
    block = block.astype(F32)
    decay = jnp.exp2(rate * (block[DS : DS + 1] + block[DS + 1 : DS + 2]))
    return jnp.where(valid, decay * state + block[:DS], state)


def join_kernel(own_ref, one_ref, two_ref, three_ref, rate_ref, *rest):
    enter_ref, row_ref = rest[-2:]
    x = lax.axis_index("req") & 3
    line = lax.broadcasted_iota(jnp.int32, (DS, LANES), 0)

    def block(k, _):
        cols = lanes_of(k)
        rate = rate_ref[:, cols] * -LOG2E
        near = ((3, three_ref[:, cols]), (2, two_ref[:, cols]), (1, one_ref[:, cols]))
        state = jnp.zeros((DS, LANES), F32)
        before = jnp.zeros((DS, LANES), F32)
        for by, ends in near:
            state = chained(state, ends, rate, x >= by)
            before = jnp.where(x >= by, before + ends[DS:].astype(F32), before)
        enter_ref[:, cols] = jnp.concatenate([state, before], axis=0)
        own = own_ref[:, cols]
        state = chained(state, own, rate, True)
        sums = own[DS:].astype(F32)
        for by, ends in near:
            state = chained(state, ends, rate, x < by)
            sums = sums + ends[DS:].astype(F32)
        total = sums[0:1] + sums[1:2]
        high = total.astype(BF16).astype(F32)
        sums = jnp.where(line == 0, high, jnp.where(line == 1, total - high, 0.0))
        row_ref[:, cols] = jnp.concatenate([state, sums], axis=0).astype(BF16)
        return 0

    lax.fori_loop(0, BLOCKS, block, 0)


def join(own, others, rate, later):
    return pl.pallas_call(
        join_kernel,
        out_shape=(
            jax.ShapeDtypeStruct((2 * DS, DI), F32),
            jax.ShapeDtypeStruct((2 * DS, DI), BF16),
        ),
        in_specs=[VMEM] * 5 + [ANY] * len(later),
        out_specs=(VMEM, VMEM),
        compiler_params=params(50),
        cost_estimate=cost(10**7, 4 * 10**6),
        name="join",
    )(own, *others, rate, *later)


def scan_kernel(
    z_ref, act_ref, step_ref, bc_ref, rate_ref, enter_ref, one_ref, two_ref, three_ref,
    vectors_ref, *rest
):
    out_ref, drive, b_wide, c_wide, parts, y_ref = rest[-6:]
    place = lax.axis_index("req") >> 2
    bc = bc_ref[...]
    spread(bc[:DS], b_wide)
    spread(bc[DS:], c_wide)
    row = lax.broadcasted_iota(jnp.int32, (T, 8 * T), 0)
    col = lax.broadcasted_iota(jnp.int32, (T, 8 * T), 1)
    pick = jnp.where(col // 8 == row, 1.0, 0.0).astype(BF16)

    def block(k, squares):
        cols = lanes_of(k)
        rate = rate_ref[:, cols] * -LOG2E
        drive[...] = step_ref[0:T, cols] * act_ref[0:T, cols]

        def one(pair, state):
            halves = []
            for t in (2 * pair, 2 * pair + 1):
                size = step_ref[pl.ds(t, 1), cols]
                push = drive[pl.ds(t, 1), :]
                state = jnp.exp2(rate * size) * state + wide(b_wide[t]) * push
                seen = state * wide(c_wide[t])
                halves.append(seen[0:8] + seen[8:16])
            at = pl.multiple_of(16 * pair, 16)
            parts[pl.ds(at, 16), :] = jnp.concatenate(halves, axis=0).astype(BF16)
            return state

        state = jnp.zeros((DS, LANES), F32)
        for by, ends in ((3, three_ref), (2, two_ref), (1, one_ref)):
            state = chained(state, ends[:, cols], rate, place >= by)
        state = chained(state, enter_ref[:, cols], rate, True)
        lax.fori_loop(0, T // 2, one, state, unroll=4)
        y = dot(pick, parts[...], NN) + vectors_ref[2:3, cols] * act_ref[0:T, cols]
        y = y * silu(z_ref[:, lanes_of(k, DI)].astype(F32))
        y_ref[:, cols] = y
        return squares + jnp.sum(y * y, axis=1, keepdims=True)

    squares = lax.fori_loop(0, BLOCKS, block, jnp.zeros((T, 1), F32))
    scale = lax.rsqrt(squares * (1.0 / DI) + EPSILON)

    def norm(k, _):
        cols = lanes_of(k)
        out_ref[:, cols] = (y_ref[:, cols] * scale * vectors_ref[3:4, cols]).astype(BF16)
        return 0

    lax.fori_loop(0, BLOCKS, norm, 0)


def scan(xz, act, step, bc, rate, enter, rows, vectors, later):
    return pl.pallas_call(
        scan_kernel,
        out_shape=jax.ShapeDtypeStruct((T, DI), BF16),
        in_specs=[VMEM] * 10 + [ANY] * len(later),
        out_specs=VMEM,
        scratch_shapes=[
            pltpu.VMEM((T, LANES), F32),
            pltpu.VMEM((T, DS, 128), F32),
            pltpu.VMEM((T, DS, 128), F32),
            pltpu.VMEM((8 * T, LANES), BF16),
            pltpu.VMEM((T, DI), F32),
        ],
        compiler_params=params(),
        cost_estimate=cost(10**9, 80 * 10**6),
        name="scan",
    )(xz, act, step, bc, rate, enter, *rows, vectors, *later)


def attend_kernel(q_ref, near_ref, far_ref, last_ref, gain_ref, *rest):
    out_ref, scores, mixed = rest[-3:]
    r = lax.axis_index("req")
    wide_rows = GROUP * T
    back = WINDOW // T

    def keys(distance, cols):
        if distance < 4:
            return near_ref[distance * T : (distance + 1) * T, cols]
        if distance < 8:
            return far_ref[(distance - 4) * T : (distance - 3) * T, cols]
        return last_ref[:, cols]

    key = lax.broadcasted_iota(jnp.int32, (T, wide_rows), 0)
    query = lax.broadcasted_iota(jnp.int32, (T, wide_rows), 1) % T
    for h in range(KEY_VALUE_HEADS):
        first = h * GROUP * HEAD_SIZE
        q = jnp.concatenate(
            [q_ref[first + g * HEAD_SIZE : first + (g + 1) * HEAD_SIZE, :] for g in range(GROUP)],
            axis=1,
        )
        q = (q.astype(F32) * (1.0 / math.sqrt(HEAD_SIZE))).astype(BF16)
        none = jnp.zeros_like(q)
        q = jnp.concatenate([q, none] if h % 2 == 0 else [none, q], axis=0)
        key_cols = slice(128 * (h // 2), 128 * (h // 2) + 128)
        at = KEYW + h * HEAD_SIZE
        value_cols = slice(at // 128 * 128, at // 128 * 128 + 128)
        value_row = at % 128
        top = jnp.full((1, wide_rows), MASKED, F32)
        for j in range(back + 1):
            s = dot(keys(back - j, key_cols), q, NN)
            if j == back:
                s = jnp.where(key <= query, s, MASKED)
            elif j == 0:
                s = jnp.where(jnp.logical_and(key > query, r >= back), s, MASKED)
            else:
                s = jnp.where(r - back + j >= 0, s, MASKED)
            scores[j] = s
            top = jnp.maximum(top, jnp.max(s, axis=0, keepdims=True))
        total = jnp.zeros((1, wide_rows), F32)
        sums = jnp.zeros((128, wide_rows), F32)
        for j in range(back + 1):
            weight = jnp.exp(scores[j] - top)
            total = total + jnp.sum(weight, axis=0, keepdims=True)
            sums = sums + dot(keys(back - j, value_cols), weight.astype(BF16), TN)
        part = sums[value_row : value_row + HEAD_SIZE] / total
        for g in range(GROUP):
            mixed[first + g * HEAD_SIZE : first + (g + 1) * HEAD_SIZE, :] = part[
                :, g * T : (g + 1) * T
            ]
    values = mixed[...]
    scale = lax.rsqrt(jnp.mean(values * values, axis=0, keepdims=True) + EPSILON)
    out_ref[...] = (jnp.transpose(values * scale) * gain_ref[...]).astype(BF16)


def attend(q, near, far, last, gain, later):
    return pl.pallas_call(
        attend_kernel,
        out_shape=jax.ShapeDtypeStruct((T, D), BF16),
        in_specs=[VMEM] * 5 + [ANY] * len(later),
        out_specs=VMEM,
        scratch_shapes=[
            pltpu.VMEM((WINDOW // T + 1, T, GROUP * T), F32),
            pltpu.VMEM((D, T), F32),
        ],
        compiler_params=params(),
        cost_estimate=cost(10**5, 10**4),
        name="attend",
    )(q, near, far, last, gain, *later)


def tables_kernel(owner_ref, slot_ref, len_ref, out_ref):
    me = lax.axis_index("req")
    entries, devices = owner_ref.shape
    window_pages = entries // len_ref.shape[0]
    most = 64 // devices
    owner_line = lax.broadcasted_iota(jnp.int32, (devices, devices), 0)
    rank_line = lax.broadcasted_iota(jnp.int32, (8, devices), 0)
    lane = lax.broadcasted_iota(jnp.int32, (1, devices), 1)
    wide_lane = lax.broadcasted_iota(jnp.int32, (1, 128), 1)
    seen = jnp.zeros((devices, devices), F32)
    sent = jnp.zeros((8, devices), jnp.int32)
    got = jnp.zeros((1, 128), jnp.int32)
    for e in range(entries):
        request, page = divmod(e, window_pages)
        length = len_ref[request : request + 1, :]
        first = jnp.maximum(length - (WINDOW - 1), 0) >> 7
        used = (first + page) * PAGE < length
        owner = owner_ref[e : e + 1, :]
        hit = jnp.logical_and(owner_line == owner, used)
        rank = jnp.sum(jnp.where(hit, seen, 0.0), axis=0, keepdims=True).astype(jnp.int32)
        seen = jnp.where(hit, seen + 1.0, seen)
        code = slot_ref[e : e + 1, :] + (page * 64 + request * 1024 + 8192)
        here = jnp.logical_and(owner == me, used)
        sent = jnp.where(jnp.logical_and(rank_line == rank, here), code, sent)
        code = owner * most + rank + (request * 64 + 512)
        code = jnp.where(jnp.logical_and(lane == me, used), code, 0).astype(F32)
        code = jnp.sum(code, axis=1, keepdims=True).astype(jnp.int32)
        got = jnp.where(wide_lane == e, code, got)
    out_ref[...] = jnp.zeros_like(out_ref)
    out_ref[0:8, 0:devices] = sent
    out_ref[8:9, :] = got


def tables(owners, slots, lengths):
    return pl.pallas_call(
        tables_kernel,
        out_shape=jax.ShapeDtypeStruct((16, 128), jnp.int32),
        in_specs=[VMEM] * 3,
        out_specs=VMEM,
        compiler_params=params(50),
        cost_estimate=cost(10**6, 4 * 10**6),
        name="tables",
    )(owners, slots, lengths)


def pages_kernel(table_ref, len_ref, pool_ref, *rest):
    out_ref, pages, queries, chosen, sems = rest[-5:]
    me = lax.axis_index("req")
    most = 64 // len_ref.shape[1]
    requests = len_ref.shape[0]

    def code_of(n):
        return table_ref[n & (most - 1), n // most]

    def fetch(n):
        slot = code_of(n) & 63
        return pltpu.make_async_copy(pool_ref.at[slot], pages.at[n], sems.at[n])

    def choose(n, count):
        valid = code_of(n) >> 13
        chosen[count] = n

        @pl.when(valid == 1)
        def _():
            fetch(n).start()

        return count + valid

    count = lax.fori_loop(0, 64, choose, 0)
    held = rest[0].shape[0]
    for k in range(SIDE):
        queries[k * held : (k + 1) * held, :] = rest[k][...]
    head = lax.broadcasted_iota(jnp.int32, (HEADS, 128), 0)
    lane = lax.broadcasted_iota(jnp.int32, (HEADS, 128), 1)
    block_of = head // (2 * GROUP)
    kv_head = head // GROUP

    def share(n):
        code = code_of(n)
        device = n // most
        page_index = (code >> 6) & 15
        request = (code >> 10) & 7
        away = ((me >> 2) - (device >> 2)) & 3
        across = (me - device) & 3
        at = (away * SIDE + across) * requests + request
        length = len_ref[request, device]
        first = jnp.maximum(length - (WINDOW - 1), 0) // PAGE
        base = (first + page_index) * PAGE
        q = queries[pl.ds(pl.multiple_of(at * HEADS, HEADS), HEADS), :].astype(F32)
        q = jnp.concatenate([jnp.where(block_of == b, q, 0.0) for b in range(3)], axis=1)
        q = (q * (1.0 / math.sqrt(HEAD_SIZE))).astype(BF16)
        s = dot(q, pages[n, :, 0:384], NT)
        position = base + lane
        seen = jnp.logical_and(position > length - WINDOW, position < length)
        s = jnp.where(seen, s, MASKED)
        top = jnp.max(s, axis=1, keepdims=True)
        weight = jnp.where(seen, jnp.exp(s - top), 0.0)
        total = jnp.sum(weight, axis=1, keepdims=True)
        sums = dot(weight.astype(BF16), pages[n, :, 256:640], NN)
        picked = jnp.where(
            kv_head == 0,
            sums[:, 0:128],
            jnp.where(kv_head <= 2, sums[:, 128:256], sums[:, 256:384]),
        )
        picked = jnp.where(kv_head % 2 == 0, pltpu.roll(picked, 64, 1), picked)
        level = top + jnp.log(total)
        high = level.astype(BF16).astype(F32)
        middle = (level - high).astype(BF16).astype(F32)
        low = level - high - middle
        tile = jnp.where(
            lane < HEAD_SIZE,
            picked / total,
            jnp.where(
                lane == HEAD_SIZE,
                high,
                jnp.where(lane == HEAD_SIZE + 1, middle, jnp.where(lane == HEAD_SIZE + 2, low, 0.0)),
            ),
        )
        return pl.ds(pl.multiple_of(n * HEADS, HEADS), HEADS), tile.astype(BF16)

    def pair(half, _):
        one = chosen[2 * half]
        two = chosen[jnp.minimum(2 * half + 1, count - 1)]
        fetch(one).wait()

        @pl.when(2 * half + 1 < count)
        def _():
            fetch(two).wait()

        both = [share(one), share(two)]
        for rows, tile in both:
            out_ref[rows, :] = tile
        return 0

    lax.fori_loop(0, (count + 1) // 2, pair, 0)


def page_shares(table, lengths, pool, queries, rows, later):
    return pl.pallas_call(
        pages_kernel,
        out_shape=jax.ShapeDtypeStruct((rows * HEADS, 128), BF16),
        in_specs=[SMEM, SMEM, ANY] + [VMEM] * len(queries) + [ANY] * len(later),
        out_specs=VMEM,
        scratch_shapes=[
            pltpu.VMEM((rows, PAGE, 2 * KEYW), BF16),
            pltpu.VMEM((SIDE * queries[0].shape[0], 128), BF16),
            pltpu.SMEM((rows,), jnp.int32),
            pltpu.SemaphoreType.DMA((rows,)),
        ],
        compiler_params=params(52),
        cost_estimate=cost(10**8, 40 * 10**6),
        name="page_shares",
    )(table, lengths, pool, *queries, *later)


def gather_kernel(
    table_ref, shares_ref, score_ref, value_ref, gain_a_ref, *rest
):
    attn_ref, tops, totals, sums, levels, chosen = rest[-6:]
    requests = score_ref.shape[0]

    def choose(n, count):
        code = table_ref[8, n]
        chosen[count] = code & 511
        return count + (code >> 9)

    count = lax.fori_loop(0, 64, choose, 0)
    tops[...] = score_ref[...]

    def tile_of(row):
        return pl.ds(pl.multiple_of(row * HEADS, HEADS), HEADS)

    def level(row, _):
        share = shares_ref[tile_of(row), :].astype(F32)
        level = share[:, 64:65] + share[:, 65:66] + share[:, 66:67]
        levels[tile_of(row), :] = jnp.broadcast_to(level, (HEADS, 128))
        return 0

    lax.fori_loop(0, shares_ref.shape[0] // HEADS, level, 0, unroll=4)

    def highest(n, _):
        request = chosen[n] >> 6
        tops[request] = jnp.maximum(tops[request], levels[tile_of(chosen[n] & 63), :])
        return 0

    lax.fori_loop(0, count, highest, 0)
    own = jnp.exp(score_ref[...] - tops[...])
    totals[...] = own
    sums[...] = own * value_ref[...]

    def add(n, _):
        request = chosen[n] >> 6
        tile = tile_of(chosen[n] & 63)
        share = shares_ref[tile, :].astype(F32)
        weight = jnp.exp(levels[tile, :] - tops[request])
        totals[request] = totals[request] + weight
        sums[request] = sums[request] + weight * share
        return 0

    lax.fori_loop(0, count, add, 0)
    head = lax.broadcasted_iota(jnp.int32, (HEADS, 128), 0)
    lane = lax.broadcasted_iota(jnp.int32, (HEADS, 128), 1)
    real = jnp.logical_and(head < QUERY_HEADS, lane < HEAD_SIZE)
    for i in range(requests):
        value = jnp.where(real, sums[i] / totals[i], 0.0)
        square = jnp.sum(jnp.sum(value * value, axis=1, keepdims=True), axis=0, keepdims=True)
        scale = lax.rsqrt(square * (1.0 / D) + EPSILON)
        attn_ref[i] = (value * scale * gain_a_ref[...]).astype(BF16)


def gather(table, operands, later):
    requests = operands[1].shape[0]
    tiles = (requests, HEADS, 128)
    return pl.pallas_call(
        gather_kernel,
        out_shape=jax.ShapeDtypeStruct(tiles, BF16),
        in_specs=[SMEM] + [VMEM] * len(operands) + [ANY] * len(later),
        out_specs=VMEM,
        scratch_shapes=[pltpu.VMEM(tiles, F32)] * 3 + [pltpu.VMEM(operands[0].shape, F32)]
        + [pltpu.SMEM((64,), jnp.int32)],
        compiler_params=params(50),
        cost_estimate=cost(10**5, 10**4),
        name="gather",
    )(table, *operands, *later)


def decode_kernel(
    act_ref, step_ref, bc_ref, state_ref, rate_ref, vectors_ref, last_ref, *rest
):
    y_out_ref, y_ref, z_ref = rest[-3:]
    requests = state_ref.shape[0]
    bc = bc_ref[...]
    y_ref[...] = jnp.zeros_like(y_ref)
    z_ref[...] = jnp.zeros_like(z_ref)
    z_ref[0:requests, :] = last_ref[:, DI:].astype(F32)

    def block(k, squares):
        cols = lanes_of(k)
        rate = rate_ref[:, cols] * -LOG2E
        for i in range(requests):
            size = step_ref[T + i : T + i + 1, cols]
            act = act_ref[T + i : T + i + 1, cols]
            b = bc[:DS, T + i : T + i + 1]
            c = bc[DS:, T + i : T + i + 1]
            state = jnp.exp2(rate * size) * state_ref[i, :, cols] + b * (size * act)
            y_ref[i : i + 1, cols] = jnp.sum(state * c, axis=0, keepdims=True)
        y = y_ref[:, cols] + vectors_ref[2:3, cols] * act_ref[T:ROWS, cols]
        y = y * silu(z_ref[:, cols])
        y_ref[:, cols] = y
        return squares + jnp.sum(y * y, axis=1, keepdims=True)

    squares = lax.fori_loop(0, BLOCKS, block, jnp.zeros((TAIL, 1), F32))
    scale = lax.rsqrt(squares * (1.0 / DI) + EPSILON)

    def norm(k, _):
        cols = lanes_of(k)
        y_out_ref[:, cols] = (y_ref[:, cols] * scale * vectors_ref[3:4, cols]).astype(BF16)
        return 0

    lax.fori_loop(0, BLOCKS, norm, 0)


def decode(operands, after):
    return pl.pallas_call(
        decode_kernel,
        out_shape=jax.ShapeDtypeStruct((TAIL, DI), BF16),
        in_specs=[VMEM] * len(operands) + [ANY] * len(after),
        out_specs=VMEM,
        scratch_shapes=[pltpu.VMEM((TAIL, DI), F32)] * 2,
        compiler_params=params(50),
        cost_estimate=cost(10**5, 10**4),
        name="decode",
    )(*operands, *after)


def project_kernel(
    place_ref, attn_ref, attn_tail_ref, y_ref, y_tail_ref, resid_ref, gain_ref, *rest
):
    shards = place_ref.shape[0]
    weights = rest[:shards]
    after_ref, normed_ref, mix = rest[shards:]
    width = mix.shape[2]
    for m in range(shards):
        low, high = m * width, (m + 1) * width
        for rows, attn, y in (
            (slice(0, T), attn_ref, y_ref),
            (slice(T, ROWS), attn_tail_ref, y_tail_ref),
        ):
            pieces = []
            if low < D:
                pieces.append(attn[:, low : min(high, D)].astype(F32))
            if high > D:
                pieces.append(y[:, max(low, D) - D : high - D].astype(F32))
            piece = pieces[0] if len(pieces) == 1 else jnp.concatenate(pieces, axis=1)
            mix[m, rows, :] = piece.astype(BF16)
    after_ref[...] = resid_ref[...].astype(F32)
    for s in range(shards):
        after_ref[...] += dot(mix[place_ref[s]], weights[s][...], NN)
    after = after_ref[...]
    scale = lax.rsqrt(jnp.mean(after * after, axis=1, keepdims=True) + EPSILON)
    normed_ref[...] = (after * scale * gain_ref[...]).astype(BF16)


def project(places, attn, attn_tail, y, y_tail, resid, gain, weights):
    count, width = len(weights), weights[0].shape[0]
    return pl.pallas_call(
        project_kernel,
        out_shape=(
            jax.ShapeDtypeStruct((ROWS, D), F32),
            jax.ShapeDtypeStruct((ROWS, D), BF16),
        ),
        in_specs=[SMEM] + [VMEM] * (6 + count),
        out_specs=(VMEM, VMEM),
        scratch_shapes=[pltpu.VMEM((count, ROWS, width), BF16)],
        compiler_params=params(),
        cost_estimate=cost(2 * 10**9, 30 * 10**6),
        name="project",
    )(places, attn, attn_tail, y, y_tail, resid, gain, *weights)


def mlp_kernel(count, extra, *refs):
    refs = refs[: count + 6] + refs[count + 6 + extra :]
    rows = refs[:count]
    sources = refs[count : count + 6]
    outs = refs[count + 6 : 2 * count + 6]
    buffers = refs[2 * count + 6 : 2 * count + 12]
    sems = refs[2 * count + 12]
    copies = [
        pltpu.make_async_copy(sources[i], buffers[i], sems.at[i]) for i in range(6)
    ]
    for copy in copies:
        copy.start()
    totals = [None] * count
    for s in range(2):
        for i in range(3):
            copies[3 * s + i].wait()
        gate_w, up_w, down_w = buffers[3 * s : 3 * s + 3]
        for n in range(count):
            value = rows[n][...]
            hidden = silu(dot(value, gate_w[...], NT)) * dot(value, up_w[...], NT)
            part = dot(hidden.astype(BF16), down_w[...], NN)
            if s == 0:
                refs[2 * count + 13 + n][...] = part
            else:
                outs[n][...] = (refs[2 * count + 13 + n][...] + part).astype(outs[n].dtype)


def mlp(rows, weights, kind, after=()):
    count = len(rows)
    return pl.pallas_call(
        functools.partial(mlp_kernel, count, len(after)),
        out_shape=tuple(jax.ShapeDtypeStruct((ROWS, D), kind) for _ in rows),
        in_specs=[VMEM] * count + [ANY] * (6 + len(after)),
        out_specs=(VMEM,) * count,
        scratch_shapes=[pltpu.VMEM(w.shape, BF16) for w in weights]
        + [pltpu.SemaphoreType.DMA((6,))]
        + [pltpu.VMEM((ROWS, D), F32) for _ in rows],
        compiler_params=params(52),
        cost_estimate=cost(2 * 10**9 * count, 15 * 10**6),
        name="mlp",
    )(*rows, *weights, *after)


def after(a, *others):
    return lax.optimization_barrier((a, *others))[0]


def padded_to(a, axis, size):
    pads = [(0, 0)] * a.ndim
    pads[axis] = (0, size - a.shape[axis])
    return jnp.pad(a, pads)


def shards(
    decode_query,
    decode_key_value,
    dec_xz,
    dec_resid,
    dec_conv,
    dec_state,
    dec_len,
    page_owner,
    page_slot,
    kv_pool,
    pre_q,
    pre_kv,
    pre_xz,
    pre_resid,
    w_xproj,
    w_dt,
    dt_bias,
    a_rate,
    conv_w,
    conv_b,
    d_skip,
    g_attn,
    g_ssm,
    w_out,
    g_mlp,
    w_gate,
    w_up,
    w_down,
):
    req_count = lax.axis_size("req")
    mlp_count = lax.axis_size("mlp")
    my_mlp = lax.axis_index("mlp")
    my_z, my_core = my_mlp >> 1, my_mlp & 1
    requests = decode_query.shape[0]
    row = lambda a: a[None, :]

    def along_x(a, by):
        pairs = [(r, r // SIDE * SIDE + (r + by) % SIDE) for r in range(req_count)]
        return lax.ppermute(a, "req", pairs)

    def along_y(a, by):
        pairs = [(r, (r // SIDE + by) % SIDE * SIDE + r % SIDE) for r in range(req_count)]
        return lax.ppermute(a, "req", pairs)

    def along_z(a, by):
        pairs = [
            (m, (m // 2 + (by if m % 2 == 0 else -by)) % SIDE * 2 + m % 2) for m in range(mlp_count)
        ]
        return lax.ppermute(a, "mlp", pairs)

    def across(a):
        return lax.ppermute(a, "mlp", [(m, m ^ 1) for m in range(mlp_count)])

    xz = pre_xz[0]
    rim = lax.ppermute(
        xz[T - 16 :, :DI], "req", [(r, r + 1) for r in range(req_count - 1)]
    )

    by_entry = lambda a: jnp.transpose(a[:, 0], (1, 2, 0)).reshape(-1, req_count)
    lengths = jnp.transpose(dec_len[:, 0])
    table = tables(by_entry(page_owner), by_entry(page_slot), lengths)

    heads = decode_query.reshape(requests, QUERY_HEADS, HEAD_SIZE)
    upper = (jnp.arange(QUERY_HEADS) // GROUP % 2 == 1)[None, :, None]
    none = jnp.zeros_like(heads)
    halves = jnp.concatenate([jnp.where(upper, none, heads), jnp.where(upper, heads, none)], axis=2)
    halves = padded_to(halves, 1, HEADS).reshape(requests * HEADS, 128)
    in_row = jnp.concatenate([halves] + [along_x(halves, by) for by in range(1, SIDE)], axis=0)
    queries = [in_row] + [along_y(in_row, by) for by in range(1, SIDE)]

    def onward(a, by):
        return lax.ppermute(a, "req", [(r, r + by) for r in range(req_count - by)])

    two_kv = jnp.concatenate([pre_kv[0], onward(pre_kv[0], 1)], axis=0)

    up_one = along_z(w_out, 1)

    rate = jnp.swapaxes(a_rate, 0, 1)
    w_x = jnp.swapaxes(w_xproj, 0, 1)
    vectors = jnp.concatenate([conv_b, dt_bias, d_skip, g_ssm]).reshape(4, DI)
    act, step, bc, ends = front(
        [xz, rim, dec_xz, dec_conv, conv_w, vectors, w_x, w_dt, rate], [two_kv]
    )

    shares = page_shares(table, lengths, kv_pool, queries, 64, [bc])

    near_kv = jnp.concatenate([two_kv, onward(two_kv, 2)], axis=0)

    row_enter, row_ends = join(
        ends, [along_x(ends, by) for by in range(1, SIDE)], rate, [shares, near_kv, up_one]
    )
    other_rows = [along_y(row_ends, by) for by in range(1, SIDE)]
    down_one = along_z(after(w_out, row_ends), -1)
    own_across = across(after(w_out, row_ends))
    far_kv = onward(after(near_kv, *other_rows), 4)
    last_kv = onward(after(pre_kv[0], *other_rows), 8)

    dec_y = decode(
        [
            act, step, bc, jnp.swapaxes(dec_state, 1, 2), rate, vectors, dec_xz
        ],
        [row_ends],
    )
    shares = lax.all_to_all(after(shares, *other_rows), "req", split_axis=0, concat_axis=0, tiled=True)
    by_head = lambda a: jnp.repeat(a.reshape(requests, KEY_VALUE_HEADS, HEAD_SIZE), GROUP, axis=1)
    own_key = by_head(decode_key_value[:, :KEYW]).astype(F32)
    own_value = by_head(decode_key_value[:, KEYW:]).astype(F32)
    own_score = jnp.sum(heads.astype(F32) * own_key, axis=2, keepdims=True) / math.sqrt(HEAD_SIZE)
    tile = lambda a: padded_to(padded_to(a, 1, HEADS), 2, 128)
    own_score = padded_to(jnp.broadcast_to(own_score, (requests, QUERY_HEADS, 128)), 1, HEADS)
    gain_a = tile(g_attn.reshape(1, QUERY_HEADS, HEAD_SIZE))[0]
    pre_y = scan(
        xz, act, step, bc, rate, row_enter, other_rows, vectors, [dec_y, own_across]
    )
    dec_attn = gather(
        table, [shares, own_score, tile(own_value), gain_a], [pre_y]
    )
    shares_home = dec_attn
    dec_attn = padded_to(dec_attn[:, :QUERY_HEADS, :HEAD_SIZE].reshape(requests, D), 0, TAIL)
    pre_attn = attend(jnp.swapaxes(pre_q[0], 0, 1), near_kv, far_kv, last_kv, row(g_attn), [pre_y, shares_home])

    up_two = along_z(after(up_one, *other_rows), 1)
    held = [w_out, up_one, down_one, up_two]
    out_weights = held + [own_across] + [
        across(after(a, first)) for a, first in zip(held[1:], (other_rows[0], pre_y, pre_attn))
    ]
    sign = 1 - 2 * my_core
    offsets = jnp.array([0, -1, 1, -2], jnp.int32)
    mine = ((my_z + sign * offsets) & (SIDE - 1)) * 2 + my_core
    other = ((my_z - sign * offsets) & (SIDE - 1)) * 2 + 1 - my_core
    places = jnp.concatenate([mine, other]).astype(jnp.int32)
    gate_t, up_t = jnp.swapaxes(w_gate, 0, 1), jnp.swapaxes(w_up, 0, 1)
    mlp_weights = [gate_t, up_t, w_down]
    mlp_weights = mlp_weights + [across(after(a, pre_y)) for a in mlp_weights]

    resid = jnp.concatenate([pre_resid[0], padded_to(dec_resid, 0, TAIL)], axis=0)
    after_mix, normed = project(
        places, pre_attn, dec_attn, pre_y, dec_y, resid, row(g_mlp), out_weights
    )

    one_up = along_z(normed, 1)
    one_down = along_z(normed, -1)
    (sum_own,) = mlp([normed], mlp_weights, F32)
    two_up = along_z(after(one_up, sum_own), 1)
    (sum_down,) = mlp([one_down], mlp_weights, BF16, [sum_own])
    back_down = along_z(sum_down, 1)
    (sum_two,) = mlp([two_up], mlp_weights, BF16, [sum_down])
    (sum_up,) = mlp([one_up], mlp_weights, BF16, [sum_two, back_down])
    back_two = along_z(sum_two, -1)
    back_up = along_z((sum_up.astype(F32) + back_two.astype(F32)).astype(BF16), -1)
    final_rows = (
        after_mix + sum_own + back_down.astype(F32) + back_up.astype(F32)
    ).astype(BF16)
    return (final_rows[T : T + requests], final_rows[:T][None])


def solution(mesh):
    both = ("req", "mlp")
    in_specs = (
        P(both, None),
        P(both, None),
        P(both, None),
        P(both, None),
        P(both, None, None),
        P(both, None, None),
        P(None, "mlp", None),
        P(None, "mlp", None, None),
        P(None, "mlp", None, None),
        P(both, None, None),
        P("mlp", "req", None),
        P("mlp", "req", None),
        P("mlp", "req", None),
        P("mlp", "req", None),
        P(),
        P(),
        P(),
        P(),
        P(),
        P(),
        P(),
        P(),
        P(),
        P("mlp", None),
        P(),
        P(None, "mlp"),
        P(None, "mlp"),
        P("mlp", None),
    )
    out_specs = (P(both, None), P("mlp", "req", None))
    return jax.shard_map(shards, mesh=mesh, in_specs=in_specs, out_specs=out_specs, check_vma=False)
```

```python
import functools
import math

import jax
import jax.numpy as jnp
from jax import lax
from jax.experimental import pallas as pl
from jax.experimental.pallas import tpu as pltpu
from jax.sharding import PartitionSpec as P

QUERY_HEADS = 25
KEY_VALUE_HEADS = 5
GROUP = QUERY_HEADS // KEY_VALUE_HEADS
HEAD_SIZE = 64
D = QUERY_HEADS * HEAD_SIZE
KEYW = KEY_VALUE_HEADS * HEAD_SIZE
DI = 3200
DS = 16
DTR = 100
CONV = 4
WINDOW = 1024
PAGE = 128

T = 128
ROWS = 144
TAIL = ROWS - T
LANES = 640
BLOCKS = DI // LANES
HEADS = 32
SIDE = 4

EPSILON = 1e-06
MASKED = -1e30
LOG2E = math.log2(math.e)
F32 = jnp.float32
BF16 = jnp.bfloat16
NT = (((1,), (1,)), ((), ()))
NN = (((1,), (0,)), ((), ()))
TN = (((0,), (0,)), ((), ()))

VMEM = pl.BlockSpec(memory_space=pltpu.VMEM)
SMEM = pl.BlockSpec(memory_space=pltpu.SMEM)
ANY = pl.BlockSpec(memory_space=pl.ANY)


def dot(a, b, dims):
    return lax.dot_general(a, b, dims, preferred_element_type=F32)


def params(mib=58):
    return pltpu.CompilerParams(vmem_limit_bytes=mib * 2**20)


def cost(flops, bytes_accessed):
    return pl.CostEstimate(flops=flops, bytes_accessed=bytes_accessed, transcendentals=0)


def lanes_of(block, start=0):
    return pl.ds(pl.multiple_of(start + block * LANES, 128), LANES)


def silu(v):
    return v * lax.logistic(v)


def softplus(v):
    return jnp.maximum(v, 0.0) + jnp.log1p(jnp.exp(-jnp.abs(v)))


def wide(tile):
    return jnp.concatenate([tile] * (LANES // 128), axis=1)


def spread(columns, out_ref):
    for t in range(T):
        out_ref[t] = jnp.broadcast_to(columns[:, t : t + 1], (DS, 128))


def front_kernel(
    x_hbm, rim_ref, last_ref, past_ref, taps_ref, vectors_ref, w_ref, w_dt_ref, rate_ref,
    *rest
):
    act_out, step_out, bc_ref, end_ref = rest[-13:-9]
    padded, drive, b_wide, tail_ref, x_ref, act_ref, step_ref, sems, out_sems = rest[-9:]

    def fetch(k):
        cols = lanes_of(k)
        return pltpu.make_async_copy(x_hbm.at[:, cols], x_ref.at[:, cols], sems.at[k])

    def store(k):
        cols = lanes_of(k)
        return (
            pltpu.make_async_copy(act_ref.at[:, cols], act_out.at[:, cols], out_sems.at[0, k]),
            pltpu.make_async_copy(step_ref.at[:, cols], step_out.at[:, cols], out_sems.at[1, k]),
        )

    for k in range(BLOCKS):
        fetch(k).start()
    requests = last_ref.shape[0]
    tail_ref[...] = jnp.zeros_like(tail_ref)
    def fill(k, _):
        cols = lanes_of(k)
        fetch(k).wait()
        padded[0:8, cols] = rim_ref[:, cols].astype(F32)[8:16]
        padded[8 : 8 + T, cols] = x_ref[:, cols].astype(F32)
        recent = taps_ref[CONV - 1 : CONV, cols] * last_ref[:, cols].astype(F32)
        for i in range(requests):
            past = taps_ref[0 : CONV - 1, cols] * past_ref[i, :, cols].astype(F32)
            tail_ref[i : i + 1, cols] = jnp.sum(past, axis=0, keepdims=True) + recent[i : i + 1]
        return 0

    lax.fori_loop(0, BLOCKS, fill, 0)

    def conv(k, carry):
        proj, bc = carry
        cols = lanes_of(k)
        total = taps_ref[0:1, cols] * padded[5 : 5 + T, cols]
        for tap in range(1, CONV):
            total = total + taps_ref[tap : tap + 1, cols] * padded[5 + tap : 5 + tap + T, cols]
        total = jnp.concatenate([total, tail_ref[:, cols]], axis=0)
        act = silu(total + vectors_ref[0:1, cols])
        act_ref[:, cols] = act
        low = act.astype(BF16)
        return (
            proj + dot(low, w_ref[:, cols], NT),
            bc + dot(w_ref[DTR - DTR % 16 :, cols], low, NT),
        )

    proj, bc = lax.fori_loop(
        0, BLOCKS, conv, (jnp.zeros((ROWS, DTR + 2 * DS), F32), jnp.zeros((DTR % 16 + 2 * DS, ROWS), F32))
    )
    bc = bc[DTR % 16 :]
    bc_ref[...] = bc
    dt_low = proj[:, :DTR].astype(BF16)
    spread(bc[:DS], b_wide)

    def step(k, _):
        cols = lanes_of(k)
        size = softplus(dot(dt_low, w_dt_ref[:, cols], NN) + vectors_ref[1:2, cols])
        step_ref[:, cols] = size
        drive[:, cols] = size[:T] * act_ref[0:T, cols]
        for copy in store(k):
            copy.start()
        return 0

    lax.fori_loop(0, BLOCKS, step, 0)

    def scan(k, _):
        cols = lanes_of(k)
        rate = rate_ref[:, cols] * -LOG2E

        def one(t, state):
            size = step_ref[pl.ds(t, 1), cols]
            push = drive[pl.ds(t, 1), cols]
            return jnp.exp2(rate * size) * state + wide(b_wide[t]) * push

        state = lax.fori_loop(0, T, one, jnp.zeros((DS, LANES), F32), unroll=8)
        total = jnp.sum(step_ref[0:T, cols], axis=0, keepdims=True)
        high = total.astype(BF16).astype(F32)
        row = lax.broadcasted_iota(jnp.int32, (DS, LANES), 0)
        sums = jnp.where(row == 0, high, jnp.where(row == 1, total - high, 0.0))
        end_ref[:, cols] = jnp.concatenate([state, sums], axis=0).astype(BF16)
        return 0

    lax.fori_loop(0, BLOCKS, scan, 0)
    for k in range(BLOCKS):
        for copy in store(k):
            copy.wait()


def front(operands, later):
    return pl.pallas_call(
        front_kernel,
        out_shape=(
            jax.ShapeDtypeStruct((ROWS, DI), F32),
            jax.ShapeDtypeStruct((ROWS, DI), F32),
            jax.ShapeDtypeStruct((2 * DS, ROWS), F32),
            jax.ShapeDtypeStruct((2 * DS, DI), BF16),
        ),
        in_specs=[ANY] + [VMEM] * (len(operands) - 1) + [ANY] * len(later),
        out_specs=(ANY, ANY, VMEM, VMEM),
        scratch_shapes=[
            pltpu.VMEM((8 + T, DI), F32),
            pltpu.VMEM((T, DI), F32),
            pltpu.VMEM((T, DS, 128), F32),
            pltpu.VMEM((TAIL, DI), F32),
            pltpu.VMEM((T, DI), BF16),
            pltpu.VMEM((ROWS, DI), F32),
            pltpu.VMEM((ROWS, DI), F32),
            pltpu.SemaphoreType.DMA((BLOCKS,)),
            pltpu.SemaphoreType.DMA((2, BLOCKS)),
        ],
        compiler_params=params(),
        cost_estimate=cost(10**9, 40 * 10**6),
        name="front",
    )(*operands, *later)


def chained(state, block, rate, valid):
    block = block.astype(F32)
    decay = jnp.exp2(rate * (block[DS : DS + 1] + block[DS + 1 : DS + 2]))
    return jnp.where(valid, decay * state + block[:DS], state)


def join_kernel(own_ref, one_ref, two_ref, three_ref, rate_ref, *rest):
    enter_ref, row_ref = rest[-2:]
    x = lax.axis_index("req") & 3
    line = lax.broadcasted_iota(jnp.int32, (DS, LANES), 0)

    def block(k, _):
        cols = lanes_of(k)
        rate = rate_ref[:, cols] * -LOG2E
        near = ((3, three_ref[:, cols]), (2, two_ref[:, cols]), (1, one_ref[:, cols]))
        state = jnp.zeros((DS, LANES), F32)
        before = jnp.zeros((DS, LANES), F32)
        for by, ends in near:
            state = chained(state, ends, rate, x >= by)
            before = jnp.where(x >= by, before + ends[DS:].astype(F32), before)
        enter_ref[:, cols] = jnp.concatenate([state, before], axis=0)
        own = own_ref[:, cols]
        state = chained(state, own, rate, True)
        sums = own[DS:].astype(F32)
        for by, ends in near:
            state = chained(state, ends, rate, x < by)
            sums = sums + ends[DS:].astype(F32)
        total = sums[0:1] + sums[1:2]
        high = total.astype(BF16).astype(F32)
        sums = jnp.where(line == 0, high, jnp.where(line == 1, total - high, 0.0))
        row_ref[:, cols] = jnp.concatenate([state, sums], axis=0).astype(BF16)
        return 0

    lax.fori_loop(0, BLOCKS, block, 0)


def join(own, others, rate, later):
    return pl.pallas_call(
        join_kernel,
        out_shape=(
            jax.ShapeDtypeStruct((2 * DS, DI), F32),
            jax.ShapeDtypeStruct((2 * DS, DI), BF16),
        ),
        in_specs=[VMEM] * 5 + [ANY] * len(later),
        out_specs=(VMEM, VMEM),
        compiler_params=params(50),
        cost_estimate=cost(10**7, 4 * 10**6),
        name="join",
    )(own, *others, rate, *later)


def scan_kernel(
    z_hbm, act_hbm, step_hbm, bc_ref, rate_ref, enter_ref, one_ref, two_ref, three_ref,
    vectors_ref, *rest
):
    out_ref, drive, b_wide, c_wide, parts, y_ref, z_ref, act_ref, step_ref, sems = rest[-10:]

    def fetch(k):
        cols = lanes_of(k)
        rows = pl.ds(0, T)
        return (
            pltpu.make_async_copy(
                step_hbm.at[rows, cols], step_ref.at[:, cols], sems.at[0, k]
            ),
            pltpu.make_async_copy(act_hbm.at[rows, cols], act_ref.at[:, cols], sems.at[1, k]),
            pltpu.make_async_copy(
                z_hbm.at[:, lanes_of(k, DI)], z_ref.at[:, cols], sems.at[2, k]
            ),
        )

    for k in range(BLOCKS):
        for copy in fetch(k):
            copy.start()
    place = lax.axis_index("req") >> 2
    bc = bc_ref[...]
    spread(bc[:DS], b_wide)
    spread(bc[DS:], c_wide)
    row = lax.broadcasted_iota(jnp.int32, (T, 8 * T), 0)
    col = lax.broadcasted_iota(jnp.int32, (T, 8 * T), 1)
    pick = jnp.where(col // 8 == row, 1.0, 0.0).astype(BF16)

    def block(k, squares):
        cols = lanes_of(k)
        rate = rate_ref[:, cols] * -LOG2E
        for copy in fetch(k):
            copy.wait()
        drive[...] = step_ref[:, cols] * act_ref[:, cols]

        def one(pair, state):
            halves = []
            for t in (2 * pair, 2 * pair + 1):
                size = step_ref[pl.ds(t, 1), cols]
                push = drive[pl.ds(t, 1), :]
                state = jnp.exp2(rate * size) * state + wide(b_wide[t]) * push
                seen = state * wide(c_wide[t])
                halves.append(seen[0:8] + seen[8:16])
            at = pl.multiple_of(16 * pair, 16)
            parts[pl.ds(at, 16), :] = jnp.concatenate(halves, axis=0).astype(BF16)
            return state

        state = jnp.zeros((DS, LANES), F32)
        for by, ends in ((3, three_ref), (2, two_ref), (1, one_ref)):
            state = chained(state, ends[:, cols], rate, place >= by)
        state = chained(state, enter_ref[:, cols], rate, True)
        lax.fori_loop(0, T // 2, one, state, unroll=4)
        y = dot(pick, parts[...], NN) + vectors_ref[2:3, cols] * act_ref[0:T, cols]
        y = y * silu(z_ref[:, cols].astype(F32))
        y_ref[:, cols] = y
        return squares + jnp.sum(y * y, axis=1, keepdims=True)

    squares = lax.fori_loop(0, BLOCKS, block, jnp.zeros((T, 1), F32))
    scale = lax.rsqrt(squares * (1.0 / DI) + EPSILON)

    def norm(k, _):
        cols = lanes_of(k)
        out_ref[:, cols] = (y_ref[:, cols] * scale * vectors_ref[3:4, cols]).astype(BF16)
        return 0

    lax.fori_loop(0, BLOCKS, norm, 0)


def scan(xz, act, step, bc, rate, enter, rows, vectors, later):
    return pl.pallas_call(
        scan_kernel,
        out_shape=jax.ShapeDtypeStruct((T, DI), BF16),
        in_specs=[ANY] * 3 + [VMEM] * 7 + [ANY] * len(later),
        out_specs=VMEM,
        scratch_shapes=[
            pltpu.VMEM((T, LANES), F32),
            pltpu.VMEM((T, DS, 128), F32),
            pltpu.VMEM((T, DS, 128), F32),
            pltpu.VMEM((8 * T, LANES), BF16),
            pltpu.VMEM((T, DI), F32),
            pltpu.VMEM((T, DI), BF16),
            pltpu.VMEM((T, DI), F32),
            pltpu.VMEM((T, DI), F32),
            pltpu.SemaphoreType.DMA((3, BLOCKS)),
        ],
        compiler_params=params(),
        cost_estimate=cost(10**9, 80 * 10**6),
        name="scan",
    )(xz, act, step, bc, rate, enter, *rows, vectors, *later)


def attend_kernel(q_ref, near_ref, far_ref, last_ref, gain_ref, *rest):
    out_ref, scores, mixed = rest[-3:]
    r = lax.axis_index("req")
    wide_rows = GROUP * T
    back = WINDOW // T

    def keys(distance, cols):
        if distance < 4:
            return near_ref[distance * T : (distance + 1) * T, cols]
        if distance < 8:
            return far_ref[(distance - 4) * T : (distance - 3) * T, cols]
        return last_ref[:, cols]

    key = lax.broadcasted_iota(jnp.int32, (T, wide_rows), 0)
    query = lax.broadcasted_iota(jnp.int32, (T, wide_rows), 1) % T
    for h in range(KEY_VALUE_HEADS):
        first = h * GROUP * HEAD_SIZE
        q = jnp.concatenate(
            [q_ref[first + g * HEAD_SIZE : first + (g + 1) * HEAD_SIZE, :] for g in range(GROUP)],
            axis=1,
        )
        q = (q.astype(F32) * (1.0 / math.sqrt(HEAD_SIZE))).astype(BF16)
        none = jnp.zeros_like(q)
        q = jnp.concatenate([q, none] if h % 2 == 0 else [none, q], axis=0)
        key_cols = slice(128 * (h // 2), 128 * (h // 2) + 128)
        at = KEYW + h * HEAD_SIZE
        value_cols = slice(at // 128 * 128, at // 128 * 128 + 128)
        value_row = at % 128
        top = jnp.full((1, wide_rows), MASKED, F32)
        for j in range(back + 1):
            s = dot(keys(back - j, key_cols), q, NN)
            if j == back:
                s = jnp.where(key <= query, s, MASKED)
            elif j == 0:
                s = jnp.where(jnp.logical_and(key > query, r >= back), s, MASKED)
            else:
                s = jnp.where(r - back + j >= 0, s, MASKED)
            scores[j] = s
            top = jnp.maximum(top, jnp.max(s, axis=0, keepdims=True))
        total = jnp.zeros((1, wide_rows), F32)
        sums = jnp.zeros((128, wide_rows), F32)
        for j in range(back + 1):
            weight = jnp.exp(scores[j] - top)
            total = total + jnp.sum(weight, axis=0, keepdims=True)
            sums = sums + dot(keys(back - j, value_cols), weight.astype(BF16), TN)
        part = sums[value_row : value_row + HEAD_SIZE] / total
        for g in range(GROUP):
            mixed[first + g * HEAD_SIZE : first + (g + 1) * HEAD_SIZE, :] = part[
                :, g * T : (g + 1) * T
            ]
    values = mixed[...]
    scale = lax.rsqrt(jnp.mean(values * values, axis=0, keepdims=True) + EPSILON)
    out_ref[...] = (jnp.transpose(values * scale) * gain_ref[...]).astype(BF16)


def attend(q, near, far, last, gain, later):
    return pl.pallas_call(
        attend_kernel,
        out_shape=jax.ShapeDtypeStruct((T, D), BF16),
        in_specs=[VMEM] * 5 + [ANY] * len(later),
        out_specs=VMEM,
        scratch_shapes=[
            pltpu.VMEM((WINDOW // T + 1, T, GROUP * T), F32),
            pltpu.VMEM((D, T), F32),
        ],
        compiler_params=params(),
        cost_estimate=cost(10**5, 10**4),
        name="attend",
    )(q, near, far, last, gain, *later)


def tables_kernel(owner_ref, slot_ref, len_ref, out_ref):
    me = lax.axis_index("req")
    entries, devices = owner_ref.shape
    window_pages = entries // len_ref.shape[0]
    most = 64 // devices
    owner_line = lax.broadcasted_iota(jnp.int32, (devices, devices), 0)
    rank_line = lax.broadcasted_iota(jnp.int32, (8, devices), 0)
    lane = lax.broadcasted_iota(jnp.int32, (1, devices), 1)
    wide_lane = lax.broadcasted_iota(jnp.int32, (1, 128), 1)
    seen = jnp.zeros((devices, devices), F32)
    sent = jnp.zeros((8, devices), jnp.int32)
    got = jnp.zeros((1, 128), jnp.int32)
    for e in range(entries):
        request, page = divmod(e, window_pages)
        length = len_ref[request : request + 1, :]
        first = jnp.maximum(length - (WINDOW - 1), 0) >> 7
        used = (first + page) * PAGE < length
        owner = owner_ref[e : e + 1, :]
        hit = jnp.logical_and(owner_line == owner, used)
        rank = jnp.sum(jnp.where(hit, seen, 0.0), axis=0, keepdims=True).astype(jnp.int32)
        seen = jnp.where(hit, seen + 1.0, seen)
        code = slot_ref[e : e + 1, :] + (page * 64 + request * 1024 + 8192)
        here = jnp.logical_and(owner == me, used)
        sent = jnp.where(jnp.logical_and(rank_line == rank, here), code, sent)
        code = owner * most + rank + (request * 64 + 512)
        code = jnp.where(jnp.logical_and(lane == me, used), code, 0).astype(F32)
        code = jnp.sum(code, axis=1, keepdims=True).astype(jnp.int32)
        got = jnp.where(wide_lane == e, code, got)
    out_ref[...] = jnp.zeros_like(out_ref)
    out_ref[0:8, 0:devices] = sent
    out_ref[8:9, :] = got


def tables(owners, slots, lengths):
    return pl.pallas_call(
        tables_kernel,
        out_shape=jax.ShapeDtypeStruct((16, 128), jnp.int32),
        in_specs=[VMEM] * 3,
        out_specs=VMEM,
        compiler_params=params(50),
        cost_estimate=cost(10**6, 4 * 10**6),
        name="tables",
    )(owners, slots, lengths)


def pages_kernel(table_ref, len_ref, pool_ref, *rest):
    out_ref, pages, queries, chosen, sems = rest[-5:]
    me = lax.axis_index("req")
    most = 64 // len_ref.shape[1]
    requests = len_ref.shape[0]

    def code_of(n):
        return table_ref[n & (most - 1), n // most]

    def fetch(n):
        slot = code_of(n) & 63
        return pltpu.make_async_copy(pool_ref.at[slot], pages.at[n], sems.at[n])

    def choose(n, count):
        valid = code_of(n) >> 13
        chosen[count] = n

        @pl.when(valid == 1)
        def _():
            fetch(n).start()

        return count + valid

    count = lax.fori_loop(0, 64, choose, 0)
    held = rest[0].shape[0]
    for k in range(SIDE):
        queries[k * held : (k + 1) * held, :] = rest[k][...]
    head = lax.broadcasted_iota(jnp.int32, (HEADS, 128), 0)
    lane = lax.broadcasted_iota(jnp.int32, (HEADS, 128), 1)
    block_of = head // (2 * GROUP)
    kv_head = head // GROUP

    def share(n):
        code = code_of(n)
        device = n // most
        page_index = (code >> 6) & 15
        request = (code >> 10) & 7
        away = ((me >> 2) - (device >> 2)) & 3
        across = (me - device) & 3
        at = (away * SIDE + across) * requests + request
        length = len_ref[request, device]
        first = jnp.maximum(length - (WINDOW - 1), 0) // PAGE
        base = (first + page_index) * PAGE
        q = queries[pl.ds(pl.multiple_of(at * HEADS, HEADS), HEADS), :].astype(F32)
        q = jnp.concatenate([jnp.where(block_of == b, q, 0.0) for b in range(3)], axis=1)
        q = (q * (1.0 / math.sqrt(HEAD_SIZE))).astype(BF16)
        s = dot(q, pages[n, :, 0:384], NT)
        position = base + lane
        seen = jnp.logical_and(position > length - WINDOW, position < length)
        s = jnp.where(seen, s, MASKED)
        top = jnp.max(s, axis=1, keepdims=True)
        weight = jnp.where(seen, jnp.exp(s - top), 0.0)
        total = jnp.sum(weight, axis=1, keepdims=True)
        sums = dot(weight.astype(BF16), pages[n, :, 256:640], NN)
        picked = jnp.where(
            kv_head == 0,
            sums[:, 0:128],
            jnp.where(kv_head <= 2, sums[:, 128:256], sums[:, 256:384]),
        )
        picked = jnp.where(kv_head % 2 == 0, pltpu.roll(picked, 64, 1), picked)
        level = top + jnp.log(total)
        high = level.astype(BF16).astype(F32)
        middle = (level - high).astype(BF16).astype(F32)
        low = level - high - middle
        tile = jnp.where(
            lane < HEAD_SIZE,
            picked / total,
            jnp.where(
                lane == HEAD_SIZE,
                high,
                jnp.where(lane == HEAD_SIZE + 1, middle, jnp.where(lane == HEAD_SIZE + 2, low, 0.0)),
            ),
        )
        return pl.ds(pl.multiple_of(n * HEADS, HEADS), HEADS), tile.astype(BF16)

    def pair(half, _):
        one = chosen[2 * half]
        two = chosen[jnp.minimum(2 * half + 1, count - 1)]
        fetch(one).wait()

        @pl.when(2 * half + 1 < count)
        def _():
            fetch(two).wait()

        both = [share(one), share(two)]
        for rows, tile in both:
            out_ref[rows, :] = tile
        return 0

    lax.fori_loop(0, (count + 1) // 2, pair, 0)


def page_shares(table, lengths, pool, queries, rows, later):
    return pl.pallas_call(
        pages_kernel,
        out_shape=jax.ShapeDtypeStruct((rows * HEADS, 128), BF16),
        in_specs=[SMEM, SMEM, ANY] + [VMEM] * len(queries) + [ANY] * len(later),
        out_specs=VMEM,
        scratch_shapes=[
            pltpu.VMEM((rows, PAGE, 2 * KEYW), BF16),
            pltpu.VMEM((SIDE * queries[0].shape[0], 128), BF16),
            pltpu.SMEM((rows,), jnp.int32),
            pltpu.SemaphoreType.DMA((rows,)),
        ],
        compiler_params=params(52),
        cost_estimate=cost(10**8, 40 * 10**6),
        name="page_shares",
    )(table, lengths, pool, *queries, *later)


def gather_kernel(
    table_ref, shares_ref, score_ref, value_ref, gain_a_ref, *rest
):
    attn_ref, tops, totals, sums, levels, chosen = rest[-6:]
    requests = score_ref.shape[0]

    def choose(n, count):
        code = table_ref[8, n]
        chosen[count] = code & 511
        return count + (code >> 9)

    count = lax.fori_loop(0, 64, choose, 0)
    tops[...] = score_ref[...]

    def tile_of(row):
        return pl.ds(pl.multiple_of(row * HEADS, HEADS), HEADS)

    def level(row, _):
        share = shares_ref[tile_of(row), :].astype(F32)
        level = share[:, 64:65] + share[:, 65:66] + share[:, 66:67]
        levels[tile_of(row), :] = jnp.broadcast_to(level, (HEADS, 128))
        return 0

    lax.fori_loop(0, shares_ref.shape[0] // HEADS, level, 0, unroll=4)

    def highest(n, _):
        request = chosen[n] >> 6
        tops[request] = jnp.maximum(tops[request], levels[tile_of(chosen[n] & 63), :])
        return 0

    lax.fori_loop(0, count, highest, 0)
    own = jnp.exp(score_ref[...] - tops[...])
    totals[...] = own
    sums[...] = own * value_ref[...]

    def add(n, _):
        request = chosen[n] >> 6
        tile = tile_of(chosen[n] & 63)
        share = shares_ref[tile, :].astype(F32)
        weight = jnp.exp(levels[tile, :] - tops[request])
        totals[request] = totals[request] + weight
        sums[request] = sums[request] + weight * share
        return 0

    lax.fori_loop(0, count, add, 0)
    head = lax.broadcasted_iota(jnp.int32, (HEADS, 128), 0)
    lane = lax.broadcasted_iota(jnp.int32, (HEADS, 128), 1)
    real = jnp.logical_and(head < QUERY_HEADS, lane < HEAD_SIZE)
    for i in range(requests):
        value = jnp.where(real, sums[i] / totals[i], 0.0)
        square = jnp.sum(jnp.sum(value * value, axis=1, keepdims=True), axis=0, keepdims=True)
        scale = lax.rsqrt(square * (1.0 / D) + EPSILON)
        attn_ref[i] = (value * scale * gain_a_ref[...]).astype(BF16)


def gather(table, operands, later):
    requests = operands[1].shape[0]
    tiles = (requests, HEADS, 128)
    return pl.pallas_call(
        gather_kernel,
        out_shape=jax.ShapeDtypeStruct(tiles, BF16),
        in_specs=[SMEM] + [VMEM] * len(operands) + [ANY] * len(later),
        out_specs=VMEM,
        scratch_shapes=[pltpu.VMEM(tiles, F32)] * 3 + [pltpu.VMEM(operands[0].shape, F32)]
        + [pltpu.SMEM((64,), jnp.int32)],
        compiler_params=params(50),
        cost_estimate=cost(10**5, 10**4),
        name="gather",
    )(table, *operands, *later)


def decode_kernel(
    act_ref, step_ref, bc_ref, state_ref, rate_ref, vectors_ref, last_ref, *rest
):
    y_out_ref, y_ref, z_ref = rest[-3:]
    requests = state_ref.shape[0]
    bc = bc_ref[...]
    y_ref[...] = jnp.zeros_like(y_ref)
    z_ref[...] = jnp.zeros_like(z_ref)
    z_ref[0:requests, :] = last_ref[:, DI:].astype(F32)

    def block(k, squares):
        cols = lanes_of(k)
        rate = rate_ref[:, cols] * -LOG2E
        for i in range(requests):
            size = step_ref[T + i : T + i + 1, cols]
            act = act_ref[T + i : T + i + 1, cols]
            b = bc[:DS, T + i : T + i + 1]
            c = bc[DS:, T + i : T + i + 1]
            state = jnp.exp2(rate * size) * state_ref[i, :, cols] + b * (size * act)
            y_ref[i : i + 1, cols] = jnp.sum(state * c, axis=0, keepdims=True)
        y = y_ref[:, cols] + vectors_ref[2:3, cols] * act_ref[T:ROWS, cols]
        y = y * silu(z_ref[:, cols])
        y_ref[:, cols] = y
        return squares + jnp.sum(y * y, axis=1, keepdims=True)

    squares = lax.fori_loop(0, BLOCKS, block, jnp.zeros((TAIL, 1), F32))
    scale = lax.rsqrt(squares * (1.0 / DI) + EPSILON)

    def norm(k, _):
        cols = lanes_of(k)
        y_out_ref[:, cols] = (y_ref[:, cols] * scale * vectors_ref[3:4, cols]).astype(BF16)
        return 0

    lax.fori_loop(0, BLOCKS, norm, 0)


def decode(operands, after):
    return pl.pallas_call(
        decode_kernel,
        out_shape=jax.ShapeDtypeStruct((TAIL, DI), BF16),
        in_specs=[VMEM] * len(operands) + [ANY] * len(after),
        out_specs=VMEM,
        scratch_shapes=[pltpu.VMEM((TAIL, DI), F32)] * 2,
        compiler_params=params(50),
        cost_estimate=cost(10**5, 10**4),
        name="decode",
    )(*operands, *after)


def project_kernel(
    place_ref, attn_ref, attn_tail_ref, y_ref, y_tail_ref, resid_ref, resid_tail_ref, gain_ref, *rest
):
    shards = place_ref.shape[0]
    weights = rest[:shards]
    after_ref, normed_ref, mix = rest[shards:]
    width = mix.shape[2]
    for m in range(shards):
        low, high = m * width, (m + 1) * width
        for rows, attn, y in (
            (slice(0, T), attn_ref, y_ref),
            (slice(T, ROWS), attn_tail_ref, y_tail_ref),
        ):
            pieces = []
            if low < D:
                pieces.append(attn[:, low : min(high, D)].astype(F32))
            if high > D:
                pieces.append(y[:, max(low, D) - D : high - D].astype(F32))
            piece = pieces[0] if len(pieces) == 1 else jnp.concatenate(pieces, axis=1)
            mix[m, rows, :] = piece.astype(BF16)
    after_ref[0:T, :] = jnp.transpose(resid_ref[...].astype(F32))
    after_ref[T:ROWS, :] = jnp.zeros((TAIL, D), F32)
    after_ref[T : T + resid_tail_ref.shape[0], :] = resid_tail_ref[...].astype(F32)
    for s in range(shards):
        after_ref[...] += dot(mix[place_ref[s]], weights[s][...], NN)
    after = after_ref[...]
    scale = lax.rsqrt(jnp.mean(after * after, axis=1, keepdims=True) + EPSILON)
    normed_ref[...] = (after * scale * gain_ref[...]).astype(BF16)


def project(places, attn, attn_tail, y, y_tail, resid, resid_tail, gain, weights):
    count, width = len(weights), weights[0].shape[0]
    return pl.pallas_call(
        project_kernel,
        out_shape=(
            jax.ShapeDtypeStruct((ROWS, D), F32),
            jax.ShapeDtypeStruct((ROWS, D), BF16),
        ),
        in_specs=[SMEM] + [VMEM] * (7 + count),
        out_specs=(VMEM, VMEM),
        scratch_shapes=[pltpu.VMEM((count, ROWS, width), BF16)],
        compiler_params=params(),
        cost_estimate=cost(2 * 10**9, 30 * 10**6),
        name="project",
    )(places, attn, attn_tail, y, y_tail, resid, resid_tail, gain, *weights)


def mlp_kernel(count, extra, *refs):
    refs = refs[: count + 6] + refs[count + 6 + extra :]
    rows = refs[:count]
    sources = refs[count : count + 6]
    outs = refs[count + 6 : 2 * count + 6]
    buffers = refs[2 * count + 6 : 2 * count + 12]
    sems = refs[2 * count + 12]
    copies = [
        pltpu.make_async_copy(sources[i], buffers[i], sems.at[i]) for i in range(6)
    ]
    for copy in copies:
        copy.start()
    totals = [None] * count
    for s in range(2):
        for i in range(3):
            copies[3 * s + i].wait()
        gate_w, up_w, down_w = buffers[3 * s : 3 * s + 3]
        for n in range(count):
            value = rows[n][...]
            hidden = silu(dot(value, gate_w[...], NT)) * dot(value, up_w[...], NT)
            part = dot(hidden.astype(BF16), down_w[...], NN)
            if s == 0:
                refs[2 * count + 13 + n][...] = part
            else:
                outs[n][...] = (refs[2 * count + 13 + n][...] + part).astype(outs[n].dtype)


def mlp(rows, weights, kind, after=()):
    count = len(rows)
    return pl.pallas_call(
        functools.partial(mlp_kernel, count, len(after)),
        out_shape=tuple(jax.ShapeDtypeStruct((ROWS, D), kind) for _ in rows),
        in_specs=[VMEM] * count + [ANY] * (6 + len(after)),
        out_specs=(VMEM,) * count,
        scratch_shapes=[pltpu.VMEM(w.shape, BF16) for w in weights]
        + [pltpu.SemaphoreType.DMA((6,))]
        + [pltpu.VMEM((ROWS, D), F32) for _ in rows],
        compiler_params=params(48),
        cost_estimate=cost(2 * 10**9 * count, 15 * 10**6),
        name="mlp",
    )(*rows, *weights, *after)


def after(a, *others):
    return lax.optimization_barrier((a, *others))[0]


def padded_to(a, axis, size):
    pads = [(0, 0)] * a.ndim
    pads[axis] = (0, size - a.shape[axis])
    return jnp.pad(a, pads)


def shards(
    decode_query,
    decode_key_value,
    dec_xz,
    dec_resid,
    dec_conv,
    dec_state,
    dec_len,
    page_owner,
    page_slot,
    kv_pool,
    pre_q,
    pre_kv,
    pre_xz,
    pre_resid,
    w_xproj,
    w_dt,
    dt_bias,
    a_rate,
    conv_w,
    conv_b,
    d_skip,
    g_attn,
    g_ssm,
    w_out,
    g_mlp,
    w_gate,
    w_up,
    w_down,
):
    req_count = lax.axis_size("req")
    mlp_count = lax.axis_size("mlp")
    my_mlp = lax.axis_index("mlp")
    my_z, my_core = my_mlp >> 1, my_mlp & 1
    requests = decode_query.shape[0]
    row = lambda a: a[None, :]

    def along_x(a, by):
        pairs = [(r, r // SIDE * SIDE + (r + by) % SIDE) for r in range(req_count)]
        return lax.ppermute(a, "req", pairs)

    def along_y(a, by):
        pairs = [(r, (r // SIDE + by) % SIDE * SIDE + r % SIDE) for r in range(req_count)]
        return lax.ppermute(a, "req", pairs)

    def along_z(a, by):
        pairs = [
            (m, (m // 2 + (by if m % 2 == 0 else -by)) % SIDE * 2 + m % 2) for m in range(mlp_count)
        ]
        return lax.ppermute(a, "mlp", pairs)

    def across(a):
        return lax.ppermute(a, "mlp", [(m, m ^ 1) for m in range(mlp_count)])

    xz = pre_xz[0]
    rim = lax.ppermute(
        xz[T - 16 :, :DI], "req", [(r, r + 1) for r in range(req_count - 1)]
    )

    by_entry = lambda a: jnp.transpose(a[:, 0], (1, 2, 0)).reshape(-1, req_count)
    lengths = jnp.transpose(dec_len[:, 0])
    table = tables(by_entry(page_owner), by_entry(page_slot), lengths)

    heads = decode_query.reshape(requests, QUERY_HEADS, HEAD_SIZE)
    upper = (jnp.arange(QUERY_HEADS) // GROUP % 2 == 1)[None, :, None]
    none = jnp.zeros_like(heads)
    halves = jnp.concatenate([jnp.where(upper, none, heads), jnp.where(upper, heads, none)], axis=2)
    halves = padded_to(halves, 1, HEADS).reshape(requests * HEADS, 128)
    in_row = jnp.concatenate([halves] + [along_x(halves, by) for by in range(1, SIDE)], axis=0)
    queries = [in_row] + [along_y(in_row, by) for by in range(1, SIDE)]

    def onward(a, by):
        return lax.ppermute(a, "req", [(r, r + by) for r in range(req_count - by)])

    two_kv = jnp.concatenate([pre_kv[0], onward(pre_kv[0], 1)], axis=0)

    up_one = along_z(w_out, 1)

    rate = jnp.swapaxes(a_rate, 0, 1)
    w_x = jnp.swapaxes(w_xproj, 0, 1)
    vectors = jnp.concatenate([conv_b, dt_bias, d_skip, g_ssm]).reshape(4, DI)
    act, step, bc, ends = front(
        [xz, rim, dec_xz, dec_conv, conv_w, vectors, w_x, w_dt, rate], [two_kv]
    )

    shares = page_shares(table, lengths, kv_pool, queries, 64, [bc])

    near_kv = jnp.concatenate([two_kv, onward(two_kv, 2)], axis=0)

    row_enter, row_ends = join(
        ends, [along_x(ends, by) for by in range(1, SIDE)], rate, [shares, near_kv, up_one]
    )
    other_rows = [along_y(row_ends, by) for by in range(1, SIDE)]
    down_one = along_z(after(w_out, row_ends), -1)
    dec_y = decode(
        [
            act, step, bc, jnp.swapaxes(dec_state, 1, 2), rate, vectors, dec_xz
        ],
        [row_ends],
    )
    own_across = across(after(w_out, row_ends))
    far_kv = onward(after(near_kv, dec_y, *other_rows), 4)
    last_kv = onward(after(pre_kv[0], dec_y, *other_rows), 8)

    shares = lax.all_to_all(after(shares, dec_y, *other_rows), "req", split_axis=0, concat_axis=0, tiled=True)
    by_head = lambda a: jnp.repeat(a.reshape(requests, KEY_VALUE_HEADS, HEAD_SIZE), GROUP, axis=1)
    own_key = by_head(decode_key_value[:, :KEYW]).astype(F32)
    own_value = by_head(decode_key_value[:, KEYW:]).astype(F32)
    own_score = jnp.sum(heads.astype(F32) * own_key, axis=2, keepdims=True) / math.sqrt(HEAD_SIZE)
    tile = lambda a: padded_to(padded_to(a, 1, HEADS), 2, 128)
    own_score = padded_to(jnp.broadcast_to(own_score, (requests, QUERY_HEADS, 128)), 1, HEADS)
    gain_a = tile(g_attn.reshape(1, QUERY_HEADS, HEAD_SIZE))[0]
    pre_y = scan(
        xz, act, step, bc, rate, row_enter, other_rows, vectors, [dec_y, own_across]
    )
    dec_attn = gather(
        table, [shares, own_score, tile(own_value), gain_a], [pre_y]
    )
    shares_home = dec_attn
    dec_attn = padded_to(dec_attn[:, :QUERY_HEADS, :HEAD_SIZE].reshape(requests, D), 0, TAIL)
    pre_attn = attend(jnp.swapaxes(pre_q[0], 0, 1), near_kv, far_kv, last_kv, row(g_attn), [pre_y, shares_home])

    up_two = along_z(after(up_one, dec_y, *other_rows), 1)
    held = [w_out, up_one, down_one, up_two]
    out_weights = held + [own_across] + [
        across(after(a, first)) for a, first in zip(held[1:], (other_rows[0], pre_y, pre_attn))
    ]
    sign = 1 - 2 * my_core
    offsets = jnp.array([0, -1, 1, -2], jnp.int32)
    mine = ((my_z + sign * offsets) & (SIDE - 1)) * 2 + my_core
    other = ((my_z - sign * offsets) & (SIDE - 1)) * 2 + 1 - my_core
    places = jnp.concatenate([mine, other]).astype(jnp.int32)
    gate_t, up_t = jnp.swapaxes(w_gate, 0, 1), jnp.swapaxes(w_up, 0, 1)
    mlp_weights = [gate_t, up_t, w_down]
    mlp_weights = mlp_weights + [across(after(a, pre_y)) for a in mlp_weights]

    resid = jnp.swapaxes(pre_resid[0], 0, 1)
    after_mix, normed = project(
        places, pre_attn, dec_attn, pre_y, dec_y, resid, dec_resid, row(g_mlp), out_weights
    )

    one_up = along_z(normed, 1)
    one_down = along_z(normed, -1)
    (sum_own,) = mlp([normed], mlp_weights, F32)
    two_up = along_z(after(one_up, sum_own), 1)
    (sum_down,) = mlp([one_down], mlp_weights, BF16, [sum_own])
    back_down = along_z(sum_down, 1)
    (sum_two,) = mlp([two_up], mlp_weights, BF16, [sum_down])
    (sum_up,) = mlp([one_up], mlp_weights, BF16, [sum_two, back_down])
    back_two = along_z(sum_two, -1)
    back_up = along_z((sum_up.astype(F32) + back_two.astype(F32)).astype(BF16), -1)
    final_rows = (
        after_mix + sum_own + back_down.astype(F32) + back_up.astype(F32)
    ).astype(BF16)
    return (final_rows[T : T + requests], final_rows[:T][None])


def solution(mesh):
    both = ("req", "mlp")
    in_specs = (
        P(both, None),
        P(both, None),
        P(both, None),
        P(both, None),
        P(both, None, None),
        P(both, None, None),
        P(None, "mlp", None),
        P(None, "mlp", None, None),
        P(None, "mlp", None, None),
        P(both, None, None),
        P("mlp", "req", None),
        P("mlp", "req", None),
        P("mlp", "req", None),
        P("mlp", "req", None),
        P(),
        P(),
        P(),
        P(),
        P(),
        P(),
        P(),
        P(),
        P(),
        P("mlp", None),
        P(),
        P(None, "mlp"),
        P(None, "mlp"),
        P("mlp", None),
    )
    out_specs = (P(both, None), P("mlp", "req", None))
    return jax.shard_map(shards, mesh=mesh, in_specs=in_specs, out_specs=out_specs, check_vma=False)
```

```python
import functools
import math

import jax
import jax.numpy as jnp
from jax import lax
from jax.experimental import pallas as pl
from jax.experimental.pallas import tpu as pltpu
from jax.sharding import PartitionSpec as P

QUERY_HEADS = 25
KEY_VALUE_HEADS = 5
GROUP = QUERY_HEADS // KEY_VALUE_HEADS
HEAD_SIZE = 64
D = QUERY_HEADS * HEAD_SIZE
KEYW = KEY_VALUE_HEADS * HEAD_SIZE
DI = 3200
DS = 16
DTR = 100
CONV = 4
WINDOW = 1024
PAGE = 128

T = 128
ROWS = 144
TAIL = ROWS - T
LANES = 640
BLOCKS = DI // LANES
HEADS = 32
SIDE = 4

EPSILON = 1e-06
MASKED = -1e30
LOG2E = math.log2(math.e)
F32 = jnp.float32
BF16 = jnp.bfloat16
NT = (((1,), (1,)), ((), ()))
NN = (((1,), (0,)), ((), ()))
TN = (((0,), (0,)), ((), ()))

VMEM = pl.BlockSpec(memory_space=pltpu.VMEM)
SMEM = pl.BlockSpec(memory_space=pltpu.SMEM)
ANY = pl.BlockSpec(memory_space=pl.ANY)


def dot(a, b, dims):
    return lax.dot_general(a, b, dims, preferred_element_type=F32)


def params(mib=58):
    return pltpu.CompilerParams(vmem_limit_bytes=mib * 2**20)


def cost(flops, bytes_accessed):
    return pl.CostEstimate(flops=flops, bytes_accessed=bytes_accessed, transcendentals=0)


def lanes_of(block, start=0):
    return pl.ds(pl.multiple_of(start + block * LANES, 128), LANES)


def silu(v):
    return v * lax.logistic(v)


def softplus(v):
    return jnp.maximum(v, 0.0) + jnp.log1p(jnp.exp(-jnp.abs(v)))


def wide(tile):
    return jnp.concatenate([tile] * (LANES // 128), axis=1)


def spread(columns, out_ref):
    for t in range(T):
        out_ref[t] = jnp.broadcast_to(columns[:, t : t + 1], (DS, 128))


def front_kernel(
    x_hbm, rim_ref, last_ref, past_ref, taps_ref, vectors_ref, w_ref, w_dt_ref, rate_ref,
    *rest
):
    act_out, step_out, bc_ref, end_ref = rest[-13:-9]
    padded, drive, b_wide, tail_ref, x_ref, act_ref, step_ref, sems, out_sems = rest[-9:]

    def fetch(k):
        cols = lanes_of(k)
        return pltpu.make_async_copy(x_hbm.at[:, cols], x_ref.at[:, cols], sems.at[k])

    def store(k):
        cols = lanes_of(k)
        return (
            pltpu.make_async_copy(act_ref.at[:, cols], act_out.at[:, cols], out_sems.at[0, k]),
            pltpu.make_async_copy(step_ref.at[:, cols], step_out.at[:, cols], out_sems.at[1, k]),
        )

    for k in range(BLOCKS):
        fetch(k).start()
    requests = last_ref.shape[0]
    tail_ref[...] = jnp.zeros_like(tail_ref)
    def fill(k, _):
        cols = lanes_of(k)
        fetch(k).wait()
        padded[0:8, cols] = rim_ref[:, cols].astype(F32)[8:16]
        padded[8 : 8 + T, cols] = x_ref[:, cols].astype(F32)
        recent = taps_ref[CONV - 1 : CONV, cols] * last_ref[:, cols].astype(F32)
        for i in range(requests):
            past = taps_ref[0 : CONV - 1, cols] * past_ref[i, :, cols].astype(F32)
            tail_ref[i : i + 1, cols] = jnp.sum(past, axis=0, keepdims=True) + recent[i : i + 1]
        return 0

    lax.fori_loop(0, BLOCKS, fill, 0)

    def conv(k, carry):
        proj, bc = carry
        cols = lanes_of(k)
        total = taps_ref[0:1, cols] * padded[5 : 5 + T, cols]
        for tap in range(1, CONV):
            total = total + taps_ref[tap : tap + 1, cols] * padded[5 + tap : 5 + tap + T, cols]
        total = jnp.concatenate([total, tail_ref[:, cols]], axis=0)
        act = silu(total + vectors_ref[0:1, cols])
        act_ref[:, cols] = act
        low = act.astype(BF16)
        return (
            proj + dot(low, w_ref[:, cols], NT),
            bc + dot(w_ref[DTR - DTR % 16 :, cols], low, NT),
        )

    proj, bc = lax.fori_loop(
        0, BLOCKS, conv, (jnp.zeros((ROWS, DTR + 2 * DS), F32), jnp.zeros((DTR % 16 + 2 * DS, ROWS), F32))
    )
    bc = bc[DTR % 16 :]
    bc_ref[...] = bc
    dt_low = proj[:, :DTR].astype(BF16)
    spread(bc[:DS], b_wide)

    def step(k, _):
        cols = lanes_of(k)
        size = softplus(dot(dt_low, w_dt_ref[:, cols], NN) + vectors_ref[1:2, cols])
        step_ref[:, cols] = size
        drive[:, cols] = size[:T] * act_ref[0:T, cols]
        for copy in store(k):
            copy.start()
        return 0

    lax.fori_loop(0, BLOCKS, step, 0)

    def scan(k, _):
        cols = lanes_of(k)
        rate = rate_ref[:, cols] * -LOG2E

        def one(t, state):
            size = step_ref[pl.ds(t, 1), cols]
            push = drive[pl.ds(t, 1), cols]
            return jnp.exp2(rate * size) * state + wide(b_wide[t]) * push

        state = lax.fori_loop(0, T, one, jnp.zeros((DS, LANES), F32), unroll=8)
        total = jnp.sum(step_ref[0:T, cols], axis=0, keepdims=True)
        high = total.astype(BF16).astype(F32)
        row = lax.broadcasted_iota(jnp.int32, (DS, LANES), 0)
        sums = jnp.where(row == 0, high, jnp.where(row == 1, total - high, 0.0))
        end_ref[:, cols] = jnp.concatenate([state, sums], axis=0).astype(BF16)
        return 0

    lax.fori_loop(0, BLOCKS, scan, 0)
    for k in range(BLOCKS):
        for copy in store(k):
            copy.wait()


def front(operands, later):
    return pl.pallas_call(
        front_kernel,
        out_shape=(
            jax.ShapeDtypeStruct((ROWS, DI), F32),
            jax.ShapeDtypeStruct((ROWS, DI), F32),
            jax.ShapeDtypeStruct((2 * DS, ROWS), F32),
            jax.ShapeDtypeStruct((2 * DS, DI), BF16),
        ),
        in_specs=[ANY] + [VMEM] * (len(operands) - 1) + [ANY] * len(later),
        out_specs=(ANY, ANY, VMEM, VMEM),
        scratch_shapes=[
            pltpu.VMEM((8 + T, DI), F32),
            pltpu.VMEM((T, DI), F32),
            pltpu.VMEM((T, DS, 128), F32),
            pltpu.VMEM((TAIL, DI), F32),
            pltpu.VMEM((T, DI), BF16),
            pltpu.VMEM((ROWS, DI), F32),
            pltpu.VMEM((ROWS, DI), F32),
            pltpu.SemaphoreType.DMA((BLOCKS,)),
            pltpu.SemaphoreType.DMA((2, BLOCKS)),
        ],
        compiler_params=params(),
        cost_estimate=cost(10**9, 40 * 10**6),
        name="front",
    )(*operands, *later)


def chained(state, block, rate, valid):
    block = block.astype(F32)
    decay = jnp.exp2(rate * (block[DS : DS + 1] + block[DS + 1 : DS + 2]))
    return jnp.where(valid, decay * state + block[:DS], state)


def join_kernel(own_ref, one_ref, two_ref, three_ref, rate_ref, *rest):
    enter_ref, row_ref = rest[-2:]
    x = lax.axis_index("req") & 3
    line = lax.broadcasted_iota(jnp.int32, (DS, LANES), 0)

    def block(k, _):
        cols = lanes_of(k)
        rate = rate_ref[:, cols] * -LOG2E
        near = ((3, three_ref[:, cols]), (2, two_ref[:, cols]), (1, one_ref[:, cols]))
        state = jnp.zeros((DS, LANES), F32)
        before = jnp.zeros((DS, LANES), F32)
        for by, ends in near:
            state = chained(state, ends, rate, x >= by)
            before = jnp.where(x >= by, before + ends[DS:].astype(F32), before)
        enter_ref[:, cols] = jnp.concatenate([state, before], axis=0)
        own = own_ref[:, cols]
        state = chained(state, own, rate, True)
        sums = own[DS:].astype(F32)
        for by, ends in near:
            state = chained(state, ends, rate, x < by)
            sums = sums + ends[DS:].astype(F32)
        total = sums[0:1] + sums[1:2]
        high = total.astype(BF16).astype(F32)
        sums = jnp.where(line == 0, high, jnp.where(line == 1, total - high, 0.0))
        row_ref[:, cols] = jnp.concatenate([state, sums], axis=0).astype(BF16)
        return 0

    lax.fori_loop(0, BLOCKS, block, 0)


def join(own, others, rate, later):
    return pl.pallas_call(
        join_kernel,
        out_shape=(
            jax.ShapeDtypeStruct((2 * DS, DI), F32),
            jax.ShapeDtypeStruct((2 * DS, DI), BF16),
        ),
        in_specs=[VMEM] * 5 + [ANY] * len(later),
        out_specs=(VMEM, VMEM),
        compiler_params=params(50),
        cost_estimate=cost(10**7, 4 * 10**6),
        name="join",
    )(own, *others, rate, *later)


def scan_kernel(
    z_hbm, act_hbm, step_hbm, bc_ref, rate_ref, enter_ref, one_ref, two_ref, three_ref,
    vectors_ref, *rest
):
    out_ref, drive, b_wide, c_wide, parts, y_ref, z_ref, act_ref, step_ref, sems = rest[-10:]

    def fetch(k):
        cols = lanes_of(k)
        rows = pl.ds(0, T)
        return (
            pltpu.make_async_copy(
                step_hbm.at[rows, cols], step_ref.at[:, cols], sems.at[0, k]
            ),
            pltpu.make_async_copy(act_hbm.at[rows, cols], act_ref.at[:, cols], sems.at[1, k]),
            pltpu.make_async_copy(
                z_hbm.at[:, lanes_of(k, DI)], z_ref.at[:, cols], sems.at[2, k]
            ),
        )

    for k in range(BLOCKS):
        for copy in fetch(k):
            copy.start()
    place = lax.axis_index("req") >> 2
    bc = bc_ref[...]
    spread(bc[:DS], b_wide)
    spread(bc[DS:], c_wide)
    row = lax.broadcasted_iota(jnp.int32, (T, 8 * T), 0)
    col = lax.broadcasted_iota(jnp.int32, (T, 8 * T), 1)
    pick = jnp.where(col // 8 == row, 1.0, 0.0).astype(BF16)

    def block(k, squares):
        cols = lanes_of(k)
        rate = rate_ref[:, cols] * -LOG2E
        for copy in fetch(k):
            copy.wait()
        drive[...] = step_ref[:, cols] * act_ref[:, cols]

        def one(pair, state):
            halves = []
            for t in (2 * pair, 2 * pair + 1):
                size = step_ref[pl.ds(t, 1), cols]
                push = drive[pl.ds(t, 1), :]
                state = jnp.exp2(rate * size) * state + wide(b_wide[t]) * push
                seen = state * wide(c_wide[t])
                halves.append(seen[0:8] + seen[8:16])
            at = pl.multiple_of(16 * pair, 16)
            parts[pl.ds(at, 16), :] = jnp.concatenate(halves, axis=0).astype(BF16)
            return state

        state = jnp.zeros((DS, LANES), F32)
        for by, ends in ((3, three_ref), (2, two_ref), (1, one_ref)):
            state = chained(state, ends[:, cols], rate, place >= by)
        state = chained(state, enter_ref[:, cols], rate, True)
        lax.fori_loop(0, T // 2, one, state, unroll=4)
        y = dot(pick, parts[...], NN) + vectors_ref[2:3, cols] * act_ref[0:T, cols]
        y = y * silu(z_ref[:, cols].astype(F32))
        y_ref[:, cols] = y
        return squares + jnp.sum(y * y, axis=1, keepdims=True)

    squares = lax.fori_loop(0, BLOCKS, block, jnp.zeros((T, 1), F32))
    scale = lax.rsqrt(squares * (1.0 / DI) + EPSILON)

    def norm(k, _):
        cols = lanes_of(k)
        out_ref[:, cols] = (y_ref[:, cols] * scale * vectors_ref[3:4, cols]).astype(BF16)
        return 0

    lax.fori_loop(0, BLOCKS, norm, 0)


def scan(xz, act, step, bc, rate, enter, rows, vectors, later):
    return pl.pallas_call(
        scan_kernel,
        out_shape=jax.ShapeDtypeStruct((T, DI), BF16),
        in_specs=[ANY] * 3 + [VMEM] * 7 + [ANY] * len(later),
        out_specs=VMEM,
        scratch_shapes=[
            pltpu.VMEM((T, LANES), F32),
            pltpu.VMEM((T, DS, 128), F32),
            pltpu.VMEM((T, DS, 128), F32),
            pltpu.VMEM((8 * T, LANES), BF16),
            pltpu.VMEM((T, DI), F32),
            pltpu.VMEM((T, DI), BF16),
            pltpu.VMEM((T, DI), F32),
            pltpu.VMEM((T, DI), F32),
            pltpu.SemaphoreType.DMA((3, BLOCKS)),
        ],
        compiler_params=params(),
        cost_estimate=cost(10**9, 80 * 10**6),
        name="scan",
    )(xz, act, step, bc, rate, enter, *rows, vectors, *later)


def attend_kernel(q_ref, near_ref, far_ref, last_ref, gain_ref, *rest):
    out_ref, scores, mixed = rest[-3:]
    r = lax.axis_index("req")
    wide_rows = GROUP * T
    back = WINDOW // T

    def keys(distance, cols):
        if distance < 4:
            return near_ref[distance * T : (distance + 1) * T, cols]
        if distance < 8:
            return far_ref[(distance - 4) * T : (distance - 3) * T, cols]
        return last_ref[:, cols]

    key = lax.broadcasted_iota(jnp.int32, (T, wide_rows), 0)
    query = lax.broadcasted_iota(jnp.int32, (T, wide_rows), 1) % T
    for h in range(KEY_VALUE_HEADS):
        first = h * GROUP * HEAD_SIZE
        q = jnp.concatenate(
            [q_ref[first + g * HEAD_SIZE : first + (g + 1) * HEAD_SIZE, :] for g in range(GROUP)],
            axis=1,
        )
        q = (q.astype(F32) * (1.0 / math.sqrt(HEAD_SIZE))).astype(BF16)
        none = jnp.zeros_like(q)
        q = jnp.concatenate([q, none] if h % 2 == 0 else [none, q], axis=0)
        key_cols = slice(128 * (h // 2), 128 * (h // 2) + 128)
        at = KEYW + h * HEAD_SIZE
        value_cols = slice(at // 128 * 128, at // 128 * 128 + 128)
        value_row = at % 128
        top = jnp.full((1, wide_rows), MASKED, F32)
        for j in range(back + 1):
            s = dot(keys(back - j, key_cols), q, NN)
            if j == back:
                s = jnp.where(key <= query, s, MASKED)
            elif j == 0:
                s = jnp.where(jnp.logical_and(key > query, r >= back), s, MASKED)
            else:
                s = jnp.where(r - back + j >= 0, s, MASKED)
            scores[j] = s
            top = jnp.maximum(top, jnp.max(s, axis=0, keepdims=True))
        total = jnp.zeros((1, wide_rows), F32)
        sums = jnp.zeros((128, wide_rows), F32)
        for j in range(back + 1):
            weight = jnp.exp(scores[j] - top)
            total = total + jnp.sum(weight, axis=0, keepdims=True)
            sums = sums + dot(keys(back - j, value_cols), weight.astype(BF16), TN)
        part = sums[value_row : value_row + HEAD_SIZE] / total
        for g in range(GROUP):
            mixed[first + g * HEAD_SIZE : first + (g + 1) * HEAD_SIZE, :] = part[
                :, g * T : (g + 1) * T
            ]
    values = mixed[...]
    scale = lax.rsqrt(jnp.mean(values * values, axis=0, keepdims=True) + EPSILON)
    out_ref[...] = (jnp.transpose(values * scale) * gain_ref[...]).astype(BF16)


def attend(q, near, far, last, gain, later):
    return pl.pallas_call(
        attend_kernel,
        out_shape=jax.ShapeDtypeStruct((T, D), BF16),
        in_specs=[VMEM] * 5 + [ANY] * len(later),
        out_specs=VMEM,
        scratch_shapes=[
            pltpu.VMEM((WINDOW // T + 1, T, GROUP * T), F32),
            pltpu.VMEM((D, T), F32),
        ],
        compiler_params=params(),
        cost_estimate=cost(10**5, 10**4),
        name="attend",
    )(q, near, far, last, gain, *later)


def tables_kernel(owner_ref, slot_ref, len_ref, out_ref):
    me = lax.axis_index("req")
    entries, devices = owner_ref.shape
    window_pages = entries // len_ref.shape[0]
    most = 64 // devices
    owner_line = lax.broadcasted_iota(jnp.int32, (devices, devices), 0)
    rank_line = lax.broadcasted_iota(jnp.int32, (8, devices), 0)
    lane = lax.broadcasted_iota(jnp.int32, (1, devices), 1)
    wide_lane = lax.broadcasted_iota(jnp.int32, (1, 128), 1)
    seen = jnp.zeros((devices, devices), F32)
    sent = jnp.zeros((8, devices), jnp.int32)
    got = jnp.zeros((1, 128), jnp.int32)
    for e in range(entries):
        request, page = divmod(e, window_pages)
        length = len_ref[request : request + 1, :]
        first = jnp.maximum(length - (WINDOW - 1), 0) >> 7
        used = (first + page) * PAGE < length
        owner = owner_ref[e : e + 1, :]
        hit = jnp.logical_and(owner_line == owner, used)
        rank = jnp.sum(jnp.where(hit, seen, 0.0), axis=0, keepdims=True).astype(jnp.int32)
        seen = jnp.where(hit, seen + 1.0, seen)
        code = slot_ref[e : e + 1, :] + (page * 64 + request * 1024 + 8192)
        here = jnp.logical_and(owner == me, used)
        sent = jnp.where(jnp.logical_and(rank_line == rank, here), code, sent)
        code = owner * most + rank + (request * 64 + 512)
        code = jnp.where(jnp.logical_and(lane == me, used), code, 0).astype(F32)
        code = jnp.sum(code, axis=1, keepdims=True).astype(jnp.int32)
        got = jnp.where(wide_lane == e, code, got)
    out_ref[...] = jnp.zeros_like(out_ref)
    out_ref[0:8, 0:devices] = sent
    out_ref[8:9, :] = got


def tables(owners, slots, lengths):
    return pl.pallas_call(
        tables_kernel,
        out_shape=jax.ShapeDtypeStruct((16, 128), jnp.int32),
        in_specs=[VMEM] * 3,
        out_specs=VMEM,
        compiler_params=params(50),
        cost_estimate=cost(10**6, 4 * 10**6),
        name="tables",
    )(owners, slots, lengths)


def pages_kernel(table_ref, len_ref, pool_ref, *rest):
    out_ref, pages, queries, chosen, sems = rest[-5:]
    me = lax.axis_index("req")
    most = 64 // len_ref.shape[1]
    requests = len_ref.shape[0]

    def code_of(n):
        return table_ref[n & (most - 1), n // most]

    def fetch(n):
        slot = code_of(n) & 63
        return pltpu.make_async_copy(pool_ref.at[slot], pages.at[n], sems.at[n])

    def choose(n, count):
        valid = code_of(n) >> 13
        chosen[count] = n

        @pl.when(valid == 1)
        def _():
            fetch(n).start()

        return count + valid

    count = lax.fori_loop(0, 64, choose, 0)
    held = rest[0].shape[0]
    for k in range(SIDE):
        queries[k * held : (k + 1) * held, :] = rest[k][...]
    head = lax.broadcasted_iota(jnp.int32, (HEADS, 128), 0)
    lane = lax.broadcasted_iota(jnp.int32, (HEADS, 128), 1)
    block_of = head // (2 * GROUP)
    kv_head = head // GROUP

    def share(n):
        code = code_of(n)
        device = n // most
        page_index = (code >> 6) & 15
        request = (code >> 10) & 7
        away = ((me >> 2) - (device >> 2)) & 3
        across = (me - device) & 3
        at = (away * SIDE + across) * requests + request
        length = len_ref[request, device]
        first = jnp.maximum(length - (WINDOW - 1), 0) // PAGE
        base = (first + page_index) * PAGE
        q = queries[pl.ds(pl.multiple_of(at * HEADS, HEADS), HEADS), :].astype(F32)
        q = jnp.concatenate([jnp.where(block_of == b, q, 0.0) for b in range(3)], axis=1)
        q = (q * (1.0 / math.sqrt(HEAD_SIZE))).astype(BF16)
        s = dot(q, pages[n, :, 0:384], NT)
        position = base + lane
        seen = jnp.logical_and(position > length - WINDOW, position < length)
        s = jnp.where(seen, s, MASKED)
        top = jnp.max(s, axis=1, keepdims=True)
        weight = jnp.where(seen, jnp.exp(s - top), 0.0)
        total = jnp.sum(weight, axis=1, keepdims=True)
        sums = dot(weight.astype(BF16), pages[n, :, 256:640], NN)
        picked = jnp.where(
            kv_head == 0,
            sums[:, 0:128],
            jnp.where(kv_head <= 2, sums[:, 128:256], sums[:, 256:384]),
        )
        picked = jnp.where(kv_head % 2 == 0, pltpu.roll(picked, 64, 1), picked)
        level = top + jnp.log(total)
        high = level.astype(BF16).astype(F32)
        middle = (level - high).astype(BF16).astype(F32)
        low = level - high - middle
        tile = jnp.where(
            lane < HEAD_SIZE,
            picked / total,
            jnp.where(
                lane == HEAD_SIZE,
                high,
                jnp.where(lane == HEAD_SIZE + 1, middle, jnp.where(lane == HEAD_SIZE + 2, low, 0.0)),
            ),
        )
        return pl.ds(pl.multiple_of(n * HEADS, HEADS), HEADS), tile.astype(BF16)

    def pair(half, _):
        one = chosen[2 * half]
        two = chosen[jnp.minimum(2 * half + 1, count - 1)]
        fetch(one).wait()

        @pl.when(2 * half + 1 < count)
        def _():
            fetch(two).wait()

        both = [share(one), share(two)]
        for rows, tile in both:
            out_ref[rows, :] = tile
        return 0

    lax.fori_loop(0, (count + 1) // 2, pair, 0)


def page_shares(table, lengths, pool, queries, rows, later):
    return pl.pallas_call(
        pages_kernel,
        out_shape=jax.ShapeDtypeStruct((rows * HEADS, 128), BF16),
        in_specs=[SMEM, SMEM, ANY] + [VMEM] * len(queries) + [ANY] * len(later),
        out_specs=VMEM,
        scratch_shapes=[
            pltpu.VMEM((rows, PAGE, 2 * KEYW), BF16),
            pltpu.VMEM((SIDE * queries[0].shape[0], 128), BF16),
            pltpu.SMEM((rows,), jnp.int32),
            pltpu.SemaphoreType.DMA((rows,)),
        ],
        compiler_params=params(52),
        cost_estimate=cost(10**8, 40 * 10**6),
        name="page_shares",
    )(table, lengths, pool, *queries, *later)


def gather_kernel(
    table_ref, shares_ref, score_ref, value_ref, gain_a_ref, *rest
):
    attn_ref, tops, totals, sums, levels, chosen = rest[-6:]
    requests = score_ref.shape[0]

    def choose(n, count):
        code = table_ref[8, n]
        chosen[count] = code & 511
        return count + (code >> 9)

    count = lax.fori_loop(0, 64, choose, 0)
    tops[...] = score_ref[...]

    def tile_of(row):
        return pl.ds(pl.multiple_of(row * HEADS, HEADS), HEADS)

    def level(row, _):
        share = shares_ref[tile_of(row), :].astype(F32)
        level = share[:, 64:65] + share[:, 65:66] + share[:, 66:67]
        levels[tile_of(row), :] = jnp.broadcast_to(level, (HEADS, 128))
        return 0

    lax.fori_loop(0, shares_ref.shape[0] // HEADS, level, 0, unroll=4)

    def highest(n, _):
        request = chosen[n] >> 6
        tops[request] = jnp.maximum(tops[request], levels[tile_of(chosen[n] & 63), :])
        return 0

    lax.fori_loop(0, count, highest, 0)
    own = jnp.exp(score_ref[...] - tops[...])
    totals[...] = own
    sums[...] = own * value_ref[...]

    def add(n, _):
        request = chosen[n] >> 6
        tile = tile_of(chosen[n] & 63)
        share = shares_ref[tile, :].astype(F32)
        weight = jnp.exp(levels[tile, :] - tops[request])
        totals[request] = totals[request] + weight
        sums[request] = sums[request] + weight * share
        return 0

    lax.fori_loop(0, count, add, 0)
    head = lax.broadcasted_iota(jnp.int32, (HEADS, 128), 0)
    lane = lax.broadcasted_iota(jnp.int32, (HEADS, 128), 1)
    real = jnp.logical_and(head < QUERY_HEADS, lane < HEAD_SIZE)
    for i in range(requests):
        value = jnp.where(real, sums[i] / totals[i], 0.0)
        square = jnp.sum(jnp.sum(value * value, axis=1, keepdims=True), axis=0, keepdims=True)
        scale = lax.rsqrt(square * (1.0 / D) + EPSILON)
        attn_ref[i] = (value * scale * gain_a_ref[...]).astype(BF16)


def gather(table, operands, later):
    requests = operands[1].shape[0]
    tiles = (requests, HEADS, 128)
    return pl.pallas_call(
        gather_kernel,
        out_shape=jax.ShapeDtypeStruct(tiles, BF16),
        in_specs=[SMEM] + [VMEM] * len(operands) + [ANY] * len(later),
        out_specs=VMEM,
        scratch_shapes=[pltpu.VMEM(tiles, F32)] * 3 + [pltpu.VMEM(operands[0].shape, F32)]
        + [pltpu.SMEM((64,), jnp.int32)],
        compiler_params=params(50),
        cost_estimate=cost(10**5, 10**4),
        name="gather",
    )(table, *operands, *later)


def decode_kernel(
    act_ref, step_ref, bc_ref, state_ref, rate_ref, vectors_ref, last_ref, *rest
):
    y_out_ref, y_ref, z_ref = rest[-3:]
    requests = state_ref.shape[0]
    bc = bc_ref[...]
    y_ref[...] = jnp.zeros_like(y_ref)
    z_ref[...] = jnp.zeros_like(z_ref)
    z_ref[0:requests, :] = last_ref[:, DI:].astype(F32)

    def block(k, squares):
        cols = lanes_of(k)
        rate = rate_ref[:, cols] * -LOG2E
        for i in range(requests):
            size = step_ref[T + i : T + i + 1, cols]
            act = act_ref[T + i : T + i + 1, cols]
            b = bc[:DS, T + i : T + i + 1]
            c = bc[DS:, T + i : T + i + 1]
            state = jnp.exp2(rate * size) * state_ref[i, :, cols] + b * (size * act)
            y_ref[i : i + 1, cols] = jnp.sum(state * c, axis=0, keepdims=True)
        y = y_ref[:, cols] + vectors_ref[2:3, cols] * act_ref[T:ROWS, cols]
        y = y * silu(z_ref[:, cols])
        y_ref[:, cols] = y
        return squares + jnp.sum(y * y, axis=1, keepdims=True)

    squares = lax.fori_loop(0, BLOCKS, block, jnp.zeros((TAIL, 1), F32))
    scale = lax.rsqrt(squares * (1.0 / DI) + EPSILON)

    def norm(k, _):
        cols = lanes_of(k)
        y_out_ref[:, cols] = (y_ref[:, cols] * scale * vectors_ref[3:4, cols]).astype(BF16)
        return 0

    lax.fori_loop(0, BLOCKS, norm, 0)


def decode(operands, after):
    return pl.pallas_call(
        decode_kernel,
        out_shape=jax.ShapeDtypeStruct((TAIL, DI), BF16),
        in_specs=[VMEM] * len(operands) + [ANY] * len(after),
        out_specs=VMEM,
        scratch_shapes=[pltpu.VMEM((TAIL, DI), F32)] * 2,
        compiler_params=params(50),
        cost_estimate=cost(10**5, 10**4),
        name="decode",
    )(*operands, *after)


def project_kernel(
    place_ref, attn_ref, attn_tail_ref, y_ref, y_tail_ref, resid_ref, resid_tail_ref, gain_ref, *rest
):
    shards = place_ref.shape[0]
    weights = rest[:shards]
    after_ref, normed_ref, mix = rest[shards:]
    width = mix.shape[2]
    for m in range(shards):
        low, high = m * width, (m + 1) * width
        for rows, attn, y in (
            (slice(0, T), attn_ref, y_ref),
            (slice(T, ROWS), attn_tail_ref, y_tail_ref),
        ):
            pieces = []
            if low < D:
                pieces.append(attn[:, low : min(high, D)].astype(F32))
            if high > D:
                pieces.append(y[:, max(low, D) - D : high - D].astype(F32))
            piece = pieces[0] if len(pieces) == 1 else jnp.concatenate(pieces, axis=1)
            mix[m, rows, :] = piece.astype(BF16)
    after_ref[0:T, :] = jnp.transpose(resid_ref[...].astype(F32))
    after_ref[T:ROWS, :] = jnp.zeros((TAIL, D), F32)
    after_ref[T : T + resid_tail_ref.shape[0], :] = resid_tail_ref[...].astype(F32)
    for s in range(shards):
        after_ref[...] += dot(mix[place_ref[s]], weights[s][...], NN)
    after = after_ref[...]
    scale = lax.rsqrt(jnp.mean(after * after, axis=1, keepdims=True) + EPSILON)
    normed_ref[...] = (after * scale * gain_ref[...]).astype(BF16)


def project(places, attn, attn_tail, y, y_tail, resid, resid_tail, gain, weights):
    count, width = len(weights), weights[0].shape[0]
    return pl.pallas_call(
        project_kernel,
        out_shape=(
            jax.ShapeDtypeStruct((ROWS, D), F32),
            jax.ShapeDtypeStruct((ROWS, D), BF16),
        ),
        in_specs=[SMEM] + [VMEM] * (7 + count),
        out_specs=(VMEM, VMEM),
        scratch_shapes=[pltpu.VMEM((count, ROWS, width), BF16)],
        compiler_params=params(),
        cost_estimate=cost(2 * 10**9, 30 * 10**6),
        name="project",
    )(places, attn, attn_tail, y, y_tail, resid, resid_tail, gain, *weights)


def mlp_kernel(count, extra, *refs):
    refs = refs[: count + 6] + refs[count + 6 + extra :]
    rows = refs[:count]
    sources = refs[count : count + 6]
    outs = refs[count + 6 : 2 * count + 6]
    buffers = refs[2 * count + 6 : 2 * count + 12]
    sems = refs[2 * count + 12]
    copies = [
        pltpu.make_async_copy(sources[i], buffers[i], sems.at[i]) for i in range(6)
    ]
    for copy in copies:
        copy.start()
    totals = [None] * count
    for s in range(2):
        for i in range(3):
            copies[3 * s + i].wait()
        gate_w, up_w, down_w = buffers[3 * s : 3 * s + 3]
        for n in range(count):
            value = rows[n][...]
            hidden = silu(dot(value, gate_w[...], NT)) * dot(value, up_w[...], NT)
            part = dot(hidden.astype(BF16), down_w[...], NN)
            if s == 0:
                refs[2 * count + 13 + n][...] = part
            else:
                outs[n][...] = (refs[2 * count + 13 + n][...] + part).astype(outs[n].dtype)


def mlp(rows, weights, kind, after=()):
    count = len(rows)
    return pl.pallas_call(
        functools.partial(mlp_kernel, count, len(after)),
        out_shape=tuple(jax.ShapeDtypeStruct((ROWS, D), kind) for _ in rows),
        in_specs=[VMEM] * count + [ANY] * (6 + len(after)),
        out_specs=(VMEM,) * count,
        scratch_shapes=[pltpu.VMEM(w.shape, BF16) for w in weights]
        + [pltpu.SemaphoreType.DMA((6,))]
        + [pltpu.VMEM((ROWS, D), F32) for _ in rows],
        compiler_params=params(48),
        cost_estimate=cost(2 * 10**9 * count, 15 * 10**6),
        name="mlp",
    )(*rows, *weights, *after)


def after(a, *others):
    return lax.optimization_barrier((a, *others))[0]


def padded_to(a, axis, size):
    pads = [(0, 0)] * a.ndim
    pads[axis] = (0, size - a.shape[axis])
    return jnp.pad(a, pads)


def shards(
    decode_query,
    decode_key_value,
    dec_xz,
    dec_resid,
    dec_conv,
    dec_state,
    dec_len,
    page_owner,
    page_slot,
    kv_pool,
    pre_q,
    pre_kv,
    pre_xz,
    pre_resid,
    w_xproj,
    w_dt,
    dt_bias,
    a_rate,
    conv_w,
    conv_b,
    d_skip,
    g_attn,
    g_ssm,
    w_out,
    g_mlp,
    w_gate,
    w_up,
    w_down,
):
    req_count = lax.axis_size("req")
    mlp_count = lax.axis_size("mlp")
    my_mlp = lax.axis_index("mlp")
    my_z, my_core = my_mlp >> 1, my_mlp & 1
    requests = decode_query.shape[0]
    row = lambda a: a[None, :]

    def along_x(a, by):
        pairs = [(r, r // SIDE * SIDE + (r + by) % SIDE) for r in range(req_count)]
        return lax.ppermute(a, "req", pairs)

    def along_y(a, by):
        pairs = [(r, (r // SIDE + by) % SIDE * SIDE + r % SIDE) for r in range(req_count)]
        return lax.ppermute(a, "req", pairs)

    def along_z(a, by):
        pairs = [
            (m, (m // 2 + (by if m % 2 == 0 else -by)) % SIDE * 2 + m % 2) for m in range(mlp_count)
        ]
        return lax.ppermute(a, "mlp", pairs)

    def across(a):
        return lax.ppermute(a, "mlp", [(m, m ^ 1) for m in range(mlp_count)])

    xz = pre_xz[0]
    rim = lax.ppermute(
        xz[T - 16 :, :DI], "req", [(r, r + 1) for r in range(req_count - 1)]
    )

    by_entry = lambda a: jnp.transpose(a[:, 0], (1, 2, 0)).reshape(-1, req_count)
    lengths = jnp.transpose(dec_len[:, 0])
    table = tables(by_entry(page_owner), by_entry(page_slot), lengths)

    heads = decode_query.reshape(requests, QUERY_HEADS, HEAD_SIZE)
    upper = (jnp.arange(QUERY_HEADS) // GROUP % 2 == 1)[None, :, None]
    none = jnp.zeros_like(heads)
    halves = jnp.concatenate([jnp.where(upper, none, heads), jnp.where(upper, heads, none)], axis=2)
    halves = padded_to(halves, 1, HEADS).reshape(requests * HEADS, 128)
    in_row = jnp.concatenate([halves] + [along_x(halves, by) for by in range(1, SIDE)], axis=0)
    queries = [in_row] + [along_y(in_row, by) for by in range(1, SIDE)]

    def onward(a, by):
        return lax.ppermute(a, "req", [(r, r + by) for r in range(req_count - by)])

    two_kv = jnp.concatenate([pre_kv[0], onward(pre_kv[0], 1)], axis=0)

    up_one = along_z(w_out, 1)

    rate = jnp.swapaxes(a_rate, 0, 1)
    w_x = jnp.swapaxes(w_xproj, 0, 1)
    vectors = jnp.concatenate([conv_b, dt_bias, d_skip, g_ssm]).reshape(4, DI)
    act, step, bc, ends = front(
        [xz, rim, dec_xz, dec_conv, conv_w, vectors, w_x, w_dt, rate], [two_kv, *queries]
    )

    shares = page_shares(table, lengths, kv_pool, queries, 64, [bc])

    own_across = across(after(w_out, bc))

    row_enter, row_ends = join(
        ends, [along_x(ends, by) for by in range(1, SIDE)], rate, [shares, own_across, up_one]
    )
    other_rows = [along_y(row_ends, by) for by in range(1, SIDE)]
    down_one = along_z(after(w_out, row_ends), -1)
    near_kv = jnp.concatenate([two_kv, onward(after(two_kv, row_ends), 2)], axis=0)
    dec_y = decode(
        [
            act, step, bc, jnp.swapaxes(dec_state, 1, 2), rate, vectors, dec_xz
        ],
        [row_ends, near_kv],
    )
    far_kv = onward(after(near_kv, dec_y, *other_rows), 4)
    last_kv = onward(after(pre_kv[0], dec_y, *other_rows), 8)

    shares = lax.all_to_all(after(shares, dec_y, *other_rows), "req", split_axis=0, concat_axis=0, tiled=True)
    by_head = lambda a: jnp.repeat(a.reshape(requests, KEY_VALUE_HEADS, HEAD_SIZE), GROUP, axis=1)
    own_key = by_head(decode_key_value[:, :KEYW]).astype(F32)
    own_value = by_head(decode_key_value[:, KEYW:]).astype(F32)
    own_score = jnp.sum(heads.astype(F32) * own_key, axis=2, keepdims=True) / math.sqrt(HEAD_SIZE)
    tile = lambda a: padded_to(padded_to(a, 1, HEADS), 2, 128)
    own_score = padded_to(jnp.broadcast_to(own_score, (requests, QUERY_HEADS, 128)), 1, HEADS)
    gain_a = tile(g_attn.reshape(1, QUERY_HEADS, HEAD_SIZE))[0]
    pre_y = scan(
        xz, act, step, bc, rate, row_enter, other_rows, vectors, [dec_y]
    )
    dec_attn = gather(
        table, [shares, own_score, tile(own_value), gain_a], [pre_y]
    )
    shares_home = dec_attn
    dec_attn = padded_to(dec_attn[:, :QUERY_HEADS, :HEAD_SIZE].reshape(requests, D), 0, TAIL)
    pre_attn = attend(jnp.swapaxes(pre_q[0], 0, 1), near_kv, far_kv, last_kv, row(g_attn), [pre_y, shares_home])

    up_two = along_z(after(up_one, dec_y, *other_rows), 1)
    held = [w_out, up_one, down_one, up_two]
    out_weights = held + [own_across] + [
        across(after(a, first)) for a, first in zip(held[1:], (other_rows[0], pre_y, pre_attn))
    ]
    sign = 1 - 2 * my_core
    offsets = jnp.array([0, -1, 1, -2], jnp.int32)
    mine = ((my_z + sign * offsets) & (SIDE - 1)) * 2 + my_core
    other = ((my_z - sign * offsets) & (SIDE - 1)) * 2 + 1 - my_core
    places = jnp.concatenate([mine, other]).astype(jnp.int32)
    gate_t, up_t = jnp.swapaxes(w_gate, 0, 1), jnp.swapaxes(w_up, 0, 1)
    mlp_weights = [gate_t, up_t, w_down]
    mlp_weights = mlp_weights + [across(after(a, pre_y)) for a in mlp_weights]

    resid = jnp.swapaxes(pre_resid[0], 0, 1)
    after_mix, normed = project(
        places, pre_attn, dec_attn, pre_y, dec_y, resid, dec_resid, row(g_mlp), out_weights
    )

    one_up = along_z(normed, 1)
    one_down = along_z(normed, -1)
    (sum_own,) = mlp([normed], mlp_weights, F32)
    two_up = along_z(after(one_up, sum_own), 1)
    (sum_down,) = mlp([one_down], mlp_weights, BF16, [sum_own])
    back_down = along_z(sum_down, 1)
    (sum_two,) = mlp([two_up], mlp_weights, BF16, [sum_down])
    (sum_up,) = mlp([one_up], mlp_weights, BF16, [sum_two, back_down])
    back_two = along_z(sum_two, -1)
    back_up = along_z((sum_up.astype(F32) + back_two.astype(F32)).astype(BF16), -1)
    final_rows = (
        after_mix + sum_own + back_down.astype(F32) + back_up.astype(F32)
    ).astype(BF16)
    return (final_rows[T : T + requests], final_rows[:T][None])


def solution(mesh):
    both = ("req", "mlp")
    in_specs = (
        P(both, None),
        P(both, None),
        P(both, None),
        P(both, None),
        P(both, None, None),
        P(both, None, None),
        P(None, "mlp", None),
        P(None, "mlp", None, None),
        P(None, "mlp", None, None),
        P(both, None, None),
        P("mlp", "req", None),
        P("mlp", "req", None),
        P("mlp", "req", None),
        P("mlp", "req", None),
        P(),
        P(),
        P(),
        P(),
        P(),
        P(),
        P(),
        P(),
        P(),
        P("mlp", None),
        P(),
        P(None, "mlp"),
        P(None, "mlp"),
        P("mlp", None),
    )
    out_specs = (P(both, None), P("mlp", "req", None))
    return jax.shard_map(shards, mesh=mesh, in_specs=in_specs, out_specs=out_specs, check_vma=False)
```
